32 devices in a mesh: dp: 8 (over y, x, core), mp: 4 (over z).
Axes of the slice: x: 2, y: 2, z: 4, core: 2. Of those that a mesh axis runs over, the one named last changes fastest.
Arguments:
- hidden_in: bfloat16 [16384, 768], P(('dp', 'mp')), may hold values from -6 to 6
- lengths: int32 [8, 3], P('dp'), may hold values from 1 to 1664, as said below
- w_qkv: float32 [3, 768, 768], P(None, 'dp', 'mp'), may hold values from -0.21875 to 0.21875
- b_qv: float32 [2, 768], P(None, ('dp', 'mp')), may hold values from -1.75 to 1.75
- w_out: float32 [768, 768], P('mp', 'dp'), may hold values from -0.875 to 0.875
- b_out: float32 [768], P(('dp', 'mp')), may hold values from -1.75 to 1.75
- ln1_gain: float32 [768], P(('dp', 'mp')), may hold values from 0.1 to 1.9
- ln1_bias: float32 [768], P(('dp', 'mp')), may hold values from -1.75 to 1.75
- w_gu: float32 [2, 768, 3072], P(None, 'dp', 'mp'), may hold values from -0.21875 to 0.21875
- b_gu: float32 [2, 3072], P(None, ('dp', 'mp')), may hold values from -1.75 to 1.75
- w_down: float32 [3072, 768], P('mp', 'dp'), may hold values from -0.21875 to 0.21875
- b_down: float32 [768], P(('dp', 'mp')), may hold values from -1.75 to 1.75
- ln2_gain: float32 [768], P(('dp', 'mp')), may hold values from 0.1 to 1.9
- ln2_bias: float32 [768], P(('dp', 'mp')), may hold values from -1.75 to 1.75
- cotangent: bfloat16 [16384, 768], P(('dp', 'mp')), may hold values from -6 to 6
Outputs:
- result: bfloat16 [16384, 768], P(('dp', 'mp'))
- grad_in: bfloat16 [16384, 768], P(('dp', 'mp'))
- grad_w_qkv: float32 [3, 768, 768], P(None, 'dp', 'mp')
- grad_b_qv: float32 [2, 768], P(None, ('dp', 'mp'))
- grad_w_out: float32 [768, 768], P('mp', 'dp')
- grad_b_out: float32 [768], P(('dp', 'mp'))
- grad_ln1_gain: float32 [768], P(('dp', 'mp'))
- grad_ln1_bias: float32 [768], P(('dp', 'mp'))
- grad_w_gu: float32 [2, 768, 3072], P(None, 'dp', 'mp')
- grad_b_gu: float32 [2, 3072], P(None, ('dp', 'mp'))
- grad_w_down: float32 [3072, 768], P('mp', 'dp')
- grad_b_down: float32 [768], P(('dp', 'mp'))
- grad_ln2_gain: float32 [768], P(('dp', 'mp'))
- grad_ln2_bias: float32 [768], P(('dp', 'mp'))
The draws below stay inside these ranges and needn't reach their ends.
Inputs may be any that keep to these rules, and one draw needn't show every extreme that they name: `lengths`: the first sequence of every group has 1664 tokens; each row sums to 2048.
All inputs are finite; a program needn't handle non-finite values.
Results may differ from the reference program's by a relative error of at most 0.025.
Values may be sent and summed in bfloat16 or wider, within the bound.
A program may use at most 128 MiB of HBM per device.

```python
import jax
import jax.numpy as jnp
from jax import lax

D = 768
HEADS = 12
HEAD = 64
FF = 3072
SEQS = 3
GROUP = 2048
LONGEST = 1664
QBLOCK = 512
TOKENS = 16384
N_DP = 8


def draw_lengths(key, part):
    key = jax.random.fold_in(key, 7)
    spare = GROUP - LONGEST - (SEQS - 1)
    base = jax.random.randint(key, (N_DP, SEQS - 1), 1, 40)
    heavy = base * base * base
    shares = spare * heavy // jnp.sum(heavy, axis=1, keepdims=True)
    leftover = spare - jnp.sum(shares, axis=1, keepdims=True)
    shares = shares.at[:, 0:1].add(leftover)
    longest = jnp.full((N_DP, 1), LONGEST, jnp.int32)
    return jnp.concatenate([longest, 1 + shares], axis=1).astype(jnp.int32)


def block_levels(rng, shape, cuts, smallest, high):
    factor_of, own = 1.0, jax.random.fold_in(rng, 6)
    for position, shards_of in cuts:
        draws = jnp.exp(jax.random.uniform(jax.random.fold_in(own, position), (shards_of,), jnp.float32, smallest / len(cuts), high / len(cuts)))
        factor_of = factor_of * jnp.repeat(draws, shape[position] // shards_of).reshape([-1 if axis == position else 1 for axis in range(len(shape))])
    return factor_of


def scatter_about(rng, extent, scale, reach, shards=(), kind=jnp.bfloat16):
    result = jax.random.normal(rng, extent, jnp.float32) * scale
    if len(shards) > 0:
        result = block_levels(rng, extent, shards, -0.22, 0.18) * result
    return jnp.clip(result, min=-reach, max=reach).astype(kind)


def setup_inputs(seed: int = 0) -> dict:
    seeds = jax.random.split(jax.random.key(seed), 16)
    return {
        "hidden_in": scatter_about(seeds[0], (TOKENS, D), 1.0, 6.0, ((0, 32),)),
        "lengths": draw_lengths(jax.random.fold_in(seeds[15], 71), 0),
        "w_qkv": scatter_about(seeds[2], (3, D, D), D ** -0.5, 0.21875, ((1, 8), (2, 4)), jnp.float32),
        "b_qv": scatter_about(seeds[3], (2, D), 0.3, 1.75, ((1, 32),), jnp.float32),
        "w_out": scatter_about(seeds[4], (D, D), (D // 16) ** -0.5, 0.875, ((0, 4), (1, 8)), jnp.float32),
        "b_out": scatter_about(seeds[5], (D,), 0.3, 1.75, ((0, 32),), jnp.float32),
        "ln1_gain": jnp.clip(1.0 + 0.18 * jax.random.normal(seeds[6], (D,), jnp.float32), 0.1, 1.9),
        "ln1_bias": scatter_about(seeds[7], (D,), 0.3, 1.75, ((0, 32),), jnp.float32),
        "w_gu": scatter_about(seeds[8], (2, D, FF), D ** -0.5, 0.21875, ((1, 8), (2, 4)), jnp.float32),
        "b_gu": scatter_about(seeds[9], (2, FF), 0.3, 1.75, ((1, 32),), jnp.float32),
        "w_down": scatter_about(seeds[10], (FF, D), (FF // 4) ** -0.5, 0.21875, ((0, 4), (1, 8)), jnp.float32),
        "b_down": scatter_about(seeds[11], (D,), 0.3, 1.75, ((0, 32),), jnp.float32),
        "ln2_gain": jnp.clip(1.0 + 0.18 * jax.random.normal(seeds[12], (D,), jnp.float32), 0.1, 1.9),
        "ln2_bias": scatter_about(seeds[13], (D,), 0.3, 1.75, ((0, 32),), jnp.float32),
        "cotangent": scatter_about(seeds[14], (TOKENS, D), 1.0, 6.0, ((0, 32),)),
    }


@jax.custom_vjp
def low(v):
    return lax.optimization_barrier(v.astype(jnp.bfloat16)).astype(jnp.float32)

@jax.custom_vjp
def low_back(v):
    return v

def low_keep(v):
    return (low(v), None)

def low_pass(kept, grad):
    return (grad,)

def back_keep(v):
    return (v, None)

def back_low(kept, grad):
    return (low(grad),)
low.defvjp(low_keep, low_pass)
low_back.defvjp(back_keep, back_low)

def layer_norm(row_part, gain, shift):
    centre = row_part - lax.optimization_barrier(jnp.mean(row_part, axis=-1, keepdims=True))
    spread = lax.optimization_barrier(jnp.mean(centre * centre, axis=-1, keepdims=True))
    return centre * lax.rsqrt(spread + 1e-05) * gain + shift

def gated_unit(gate_pair):
    return jax.nn.gelu(gate_pair[:, 0], approximate=True) * gate_pair[:, 1]

def head_slopes(first_head, head_count):
    number = first_head + jnp.arange(head_count, dtype=jnp.int32)
    exponent = jnp.where(number < 8, number.astype(jnp.float32) + 1.0, number.astype(jnp.float32) - 7.5)
    return jnp.exp2(-exponent)

def segment_ids(seq_lengths, group_rows):
    seq_ends = jnp.cumsum(seq_lengths)
    places = jnp.arange(group_rows, dtype=jnp.int32)
    return lax.optimization_barrier(jnp.sum((places[:, None] >= seq_ends[None, :]).astype(jnp.int32), axis=1))

def mask_bias(raw_scores, first_row, segment, slopes, score_scale):
    block_rows = raw_scores.shape[1]
    group_rows = raw_scores.shape[2]
    row_ids = first_row + jnp.arange(block_rows, dtype=jnp.int32)
    places = jnp.arange(group_rows, dtype=jnp.int32)
    distance = jnp.abs(row_ids[:, None] - places[None, :]).astype(jnp.float32)
    scaled = raw_scores * score_scale - slopes[:, None, None] * distance[None]
    same_seq = lax.dynamic_slice_in_dim(segment, first_row, block_rows, 0)[:, None] == segment[None, :]
    return jnp.where(same_seq[None], scaled, -1e+30)

def group_forward(params, tokens, segment):
    w_qkv, b_qv, w_out, b_out, ln1_gain, ln1_bias, w_gu, b_gu, w_down, b_down, ln2_gain, ln2_bias = params
    best = lax.Precision.HIGHEST
    zero_row = jnp.zeros((1, D), jnp.float32)
    qkv_bias = jnp.concatenate([b_qv[0:1], zero_row, b_qv[1:2]], axis=0)
    proj_qkv = low(low_back(jnp.einsum('td,sdc->stc', tokens, low(w_qkv), precision=best) + qkv_bias[:, None, :]))
    queries = proj_qkv[0].reshape(GROUP, HEADS, HEAD)
    key_rows = proj_qkv[1].reshape(GROUP, HEADS, HEAD)
    value_rows = proj_qkv[2].reshape(GROUP, HEADS, HEAD)
    slopes = head_slopes(0, HEADS)
    score_scale = HEAD ** (-0.5)

    def one_block(first_row):
        q_part = lax.dynamic_slice_in_dim(queries, first_row, QBLOCK, 0)
        raw_scores = low_back(jnp.einsum('bhe,khe->hbk', q_part, key_rows, precision=best))
        scaled = mask_bias(raw_scores, first_row, segment, slopes, score_scale)
        prob_rows = low(jax.nn.softmax(scaled, axis=-1))
        return jnp.einsum('hbk,khe->bhe', prob_rows, value_rows, precision=best)
    starts = jnp.arange(GROUP // QBLOCK, dtype=jnp.int32) * QBLOCK
    attn_rows = low(low_back(lax.map(jax.checkpoint(one_block), starts).reshape(GROUP, D)))
    branch_attn = low_back(jnp.dot(attn_rows, low(w_out), precision=best) + b_out)
    mid_rows = layer_norm(tokens + branch_attn, ln1_gain, ln1_bias)
    mid_low = low(mid_rows)
    gate_up = low_back(jnp.einsum('td,sdf->tsf', mid_low, low(w_gu), precision=best) + b_gu[None])
    act_rows = low(gated_unit(gate_up))
    branch_ffn = low_back(jnp.dot(act_rows, low(w_down), precision=best) + b_down)
    return layer_norm(mid_rows + branch_ffn, ln2_gain, ln2_bias)

def reference(hidden_in, lengths, w_qkv, b_qv, w_out, b_out, ln1_gain, ln1_bias, w_gu, b_gu, w_down, b_down, ln2_gain, ln2_bias, cotangent):
    params = (w_qkv, b_qv, w_out, b_out, ln1_gain, ln1_bias, w_gu, b_gu, w_down, b_down, ln2_gain, ln2_bias)
    params = tuple((p.astype(jnp.float32) for p in params))
    inputs = hidden_in.astype(jnp.float32).reshape(N_DP, GROUP, D)
    cotans = cotangent.astype(jnp.float32).reshape(N_DP, GROUP, D)

    def step(totals, block_item):
        tokens, cot_rows, seq_lengths = block_item
        segment = segment_ids(seq_lengths, GROUP)
        normed, pull = jax.vjp(lambda weights, inputs_in: group_forward(weights, inputs_in, segment), params, tokens)
        grad_params, grad_tokens = pull(cot_rows)
        totals = jax.tree.map(jnp.add, totals, grad_params)
        return (totals, (normed, grad_tokens))
    zeros = jax.tree.map(jnp.zeros_like, params)
    totals, (outputs, grads) = lax.scan(step, zeros, (inputs, cotans, lengths))
    return (outputs.reshape(TOKENS, D).astype(jnp.bfloat16), grads.reshape(TOKENS, D).astype(jnp.bfloat16), totals[0], totals[1], totals[2], totals[3], totals[4], totals[5], totals[6], totals[7], totals[8], totals[9], totals[10], totals[11])
```

```python
import functools

import jax
import jax.numpy as jnp
from jax import lax
from jax.experimental import pallas as pl
from jax.experimental.pallas import tpu as pltpu
from jax.sharding import PartitionSpec as P

HEAD = 64
LONGEST = 1664
QB = 256
BF = jnp.bfloat16
F32 = jnp.float32
VMEM_LIMIT = 56 * 1024 * 1024


def dot(a, b):
    return lax.dot_general(a, b, (((1,), (0,)), ((), ())), preferred_element_type=F32)


def dot_nt(a, b):
    return lax.dot_general(a, b, (((1,), (1,)), ((), ())), preferred_element_type=F32)


def vmem():
    return pl.BlockSpec(memory_space=pltpu.VMEM)


def smem():
    return pl.BlockSpec(memory_space=pltpu.SMEM)


def hbm():
    return pl.BlockSpec(memory_space=pl.ANY)


def query_blocks(longest):
    whole = longest // QB
    rest = longest - whole * QB
    return whole, rest


def attention_forward(
    x, w, bias, slope, length, qkv, o, u, p, p2, kt, vext, dist, pbuf, psem
):
    group = x.shape[0]
    own = o.shape[1]
    cols = w.shape[2]
    heads = cols // HEAD
    tail = group - LONGEST
    for c in range(0, group, own):
        rows = pl.ds(c, own)
        xc = x[rows, :]
        q = (dot(xc, w[0]) + bias[0:1, :]).astype(BF)
        qkv[0, rows, :] = q * jnp.asarray(HEAD**-0.5, BF)
        k = (dot(xc, w[1]) + bias[1:2, :]).astype(BF)
        qkv[1, rows, :] = k
        kt[:, rows] = k.astype(F32).T.astype(BF)
        v = (dot(xc, w[2]) + bias[2:3, :]).astype(BF)
        qkv[2, rows, :] = v
        one = jnp.where(lax.broadcasted_iota(jnp.int32, (own, HEAD), 1) == 0, 1.0, 0.0)
        for h in range(heads):
            vh = v[:, h * HEAD : (h + 1) * HEAD].astype(F32)
            vext[h, rows, :] = jnp.concatenate([vh, one], axis=1).astype(BF)
    width = dist.shape[1]
    base = width - LONGEST
    i = lax.broadcasted_iota(jnp.int32, (QB, width), 0)
    j = lax.broadcasted_iota(jnp.int32, (QB, width), 1)
    dist[...] = jnp.abs(i + base - j).astype(F32)

    def softmax_block(s):
        m = jnp.max(s, axis=1, keepdims=True)
        return jnp.exp(s - m).astype(BF)

    def finish(h, row, rows, uu):
        u[h, pl.ds(row, rows), :] = uu
        return (uu[:, :HEAD] * (1.0 / uu[:, HEAD : HEAD + 1])).astype(BF)

    whole, rest = query_blocks(LONGEST)
    for h in range(heads):
        hs = slice(h * HEAD, (h + 1) * HEAD)
        sl = slope[h]

        def long_block(row, rows, slot):
            qh = qkv[0, pl.ds(row, rows), hs]
            s = dot(qh, kt[hs, :LONGEST])
            off = pl.multiple_of(base - row, 128)
            s = s - sl * dist[:rows, pl.ds(off, LONGEST)]
            pb = softmax_block(s)
            pbuf[slot, :rows, :] = pb
            uu = dot(pb, vext[h, :LONGEST, :])
            return finish(h, row, rows, uu)

        def copy_out(row, rows, slot):
            return pltpu.make_async_copy(
                pbuf.at[slot, pl.ds(0, rows), :],
                p.at[h, pl.ds(row, rows), :],
                psem.at[slot],
            )

        def step(b, _):
            row = pl.multiple_of(b * QB, QB)
            slot = lax.rem(b, 2)

            @pl.when(b >= 2)
            def _():
                copy_out(row - 2 * QB, QB, slot).wait()

            oh = long_block(row, QB, slot)
            copy_out(row, QB, slot).start()
            o[row // own, pl.ds(pl.multiple_of(row % own, QB), QB), hs] = oh
            return 0

        lax.fori_loop(0, whole, step, 0)
        copy_out((whole - 2) * QB, QB, whole % 2).wait()
        row = whole * QB
        oh = long_block(row, rest, whole % 2)
        copy_out(row, rest, whole % 2).start()
        o[row // own, pl.ds(row % own, rest), hs] = oh
        copy_out((whole - 1) * QB, QB, (whole - 1) % 2).wait()
        qh = qkv[0, LONGEST:, hs]
        s = dot(qh, kt[hs, LONGEST:])
        ii = lax.broadcasted_iota(jnp.int32, (tail, tail), 0)
        jj = lax.broadcasted_iota(jnp.int32, (tail, tail), 1)
        s = s - sl * jnp.abs(ii - jj).astype(F32)
        cut = length[0, 1]
        same = (ii < cut) == (jj < cut)
        s = jnp.where(same, s, -1e30)
        pb = softmax_block(s)
        p2[h] = pb
        uu = dot(pb, vext[h, LONGEST:, :])
        oh = finish(h, LONGEST, tail, uu)
        o[LONGEST // own, pl.ds(LONGEST % own, tail), hs] = oh
        copy_out(row, rest, whole % 2).wait()


def attention_backward(qkv, g, u, p, p2, d, vt, pbuf, dkt, dvt, psem):
    group = qkv.shape[1]
    own = d.shape[2]
    cols = qkv.shape[2]
    heads = cols // HEAD
    tail = group - LONGEST
    whole, rest = query_blocks(LONGEST)
    for c in range(0, group, own):
        rows = pl.ds(c, own)
        v = qkv[2, rows, :]
        vtc = v.astype(F32).T
        extra = jnp.where(lax.broadcasted_iota(jnp.int32, (HEAD, own), 0) < 2, -1.0, 0.0)
        for h in range(heads):
            vt[h, :, rows] = jnp.concatenate(
                [vtc[h * HEAD : (h + 1) * HEAD], extra], axis=0
            ).astype(BF)

    for h in range(heads):
        hs = slice(h * HEAD, (h + 1) * HEAD)

        def block(row, rows, chunk, place, pb, keys, first):
            uu = u[h, pl.ds(row, rows), :]
            inv = 1.0 / uu[:, HEAD : HEAD + 1]
            gg = g[chunk, pl.ds(place, rows), hs].astype(F32) * inv
            total = jnp.sum(gg * uu[:, :HEAD], axis=1, keepdims=True) * inv
            high = total.astype(BF).astype(F32)
            low = total - high
            lane = lax.broadcasted_iota(jnp.int32, (rows, HEAD), 1)
            extra = jnp.where(lane == 0, high, jnp.where(lane == 1, low, 0.0))
            gext = jnp.concatenate([gg, extra], axis=1).astype(BF)
            dp = dot(gext, vt[h, :, keys])
            ds = (pb.astype(F32) * dp).astype(BF)
            dq = dot(ds, qkv[1, keys, hs]) * (HEAD**-0.5)
            d[chunk, 0, pl.ds(place, rows), hs] = dq.astype(BF)
            qt = qkv[0, pl.ds(row, rows), hs].astype(F32).T.astype(BF)
            gt = gg.T.astype(BF)
            dk = dot(qt, ds)
            dv = dot(gt, pb)
            if first is None:
                dkt[:, keys] = dk
                dvt[:, keys] = dv
            else:
                dkt[:, keys] = dkt[:, keys] + dk
                dvt[:, keys] = dvt[:, keys] + dv

        def copy_in(row, rows, slot):
            return pltpu.make_async_copy(
                p.at[h, pl.ds(row, rows), :],
                pbuf.at[slot, pl.ds(0, rows), :],
                psem.at[slot],
            )

        copy_in(0, QB, 0).start()
        dkt[:, :LONGEST] = jnp.zeros((HEAD, LONGEST), F32)
        dvt[:, :LONGEST] = jnp.zeros((HEAD, LONGEST), F32)

        def step(b, _):
            row = pl.multiple_of(b * QB, QB)
            slot = lax.rem(b, 2)

            @pl.when(b < whole - 1)
            def _():
                copy_in(row + QB, QB, 1 - slot).start()

            @pl.when(b == whole - 1)
            def _():
                copy_in(whole * QB, rest, whole % 2).start()

            copy_in(row, QB, slot).wait()
            block(
                row,
                QB,
                row // own,
                pl.multiple_of(row % own, QB),
                pbuf[slot],
                slice(0, LONGEST),
                0,
            )
            return 0

        lax.fori_loop(0, whole, step, 0)
        row = whole * QB
        copy_in(row, rest, whole % 2).wait()
        block(row, rest, row // own, row % own, pbuf[whole % 2, :rest], slice(0, LONGEST), 0)
        block(
            LONGEST,
            tail,
            LONGEST // own,
            LONGEST % own,
            p2[h],
            slice(LONGEST, group),
            None,
        )
        for c in range(0, group, own):
            d[c // own, 1, :, hs] = dkt[:, c : c + own].T.astype(BF)
            d[c // own, 2, :, hs] = dvt[:, c : c + own].T.astype(BF)


def norm_parts(r):
    centre = r - jnp.mean(r, axis=-1, keepdims=True)
    spread = jnp.mean(centre * centre, axis=-1, keepdims=True)
    rstd = lax.rsqrt(spread + 1e-05)
    return centre * rstd, rstd


def norm_back(dn, n, rstd):
    return rstd * (
        dn - jnp.mean(dn, axis=-1, keepdims=True) - n * jnp.mean(dn * n, axis=-1, keepdims=True)
    )


def colsum(a):
    return jnp.sum(a, axis=0, keepdims=True)


def flip(a):
    return a.astype(F32).T.astype(BF)


GELU_C = 0.7978845608
GELU_A = 0.044715


def middle(
    attn, x, cot, wout, small, bgu, w,
    result, dsum1, dattn, gw, gwout, gsmall, gbgu,
    mid, midb, midt, gate, up, y, dffn, dffnt, dmid,
):
    i = pl.program_id(0)
    n = pl.num_programs(0) // 2
    parts = attn.shape[0]

    @pl.when(i == 0)
    def _():
        branch = x[...].astype(F32) + small[2:3, :]
        for r in range(parts):
            branch += dot_nt(attn[r], wout[r])
        nn, _ = norm_parts(branch)
        m = nn * small[3:4, :] + small[4:5, :]
        dsum1[...] = branch
        mid[...] = m
        midb[...] = m.astype(BF)
        midt[...] = m.T.astype(BF)
        y[...] = jnp.zeros_like(y)

    @pl.when(i < n)
    def _():
        mb = midb[...]
        ga = dot(mb, w[0, 0]) + bgu[0, 0:1, :]
        u = dot(mb, w[1, 0]) + bgu[0, 1:2, :]
        gate[i] = ga
        up[i] = u
        t = jnp.tanh(GELU_C * (ga + GELU_A * ga * ga * ga))
        act = (0.5 * ga * (1.0 + t) * u).astype(BF)
        y[...] += dot_nt(act, w[2, 0])

    @pl.when(i == n - 1)
    def _():
        r = mid[...] + y[...] + small[5:6, :]
        nn, rstd = norm_parts(r)
        gain = small[6:7, :]
        result[...] = (nn * gain + small[7:8, :]).astype(BF)
        c = cot[...].astype(F32)
        ds = norm_back(c * gain, nn, rstd)
        gsmall[6:7, :] = colsum(c * nn)
        gsmall[7:8, :] = colsum(c)
        dmid[...] = ds
        db = ds.astype(BF)
        dffn[...] = db
        dffnt[...] = ds.T.astype(BF)
        gsmall[5:6, :] = colsum(db.astype(F32))
        gsmall[0:2, :] = jnp.zeros_like(gsmall[0:2, :])

    @pl.when(i >= n)
    def _():
        k = 2 * n - 1 - i
        ga = gate[k]
        u = up[k]
        sq = ga * ga
        t = jnp.tanh(GELU_C * (ga + GELU_A * ga * sq))
        half = 0.5 * (1.0 + t)
        gelu = ga * half
        slope = half + (0.5 * GELU_C) * ga * (1.0 - t * t) * (1.0 + 3.0 * GELU_A * sq)
        act = (gelu * u).astype(BF)
        dact = dot(dffn[...], w[2, 0])
        gw[0, 2] = dot(dffnt[...], act).astype(BF)
        dga = (dact * u * slope).astype(BF)
        du = (dact * gelu).astype(BF)
        gbgu[0, 0:1, :] = colsum(dga.astype(F32))
        gbgu[0, 1:2, :] = colsum(du.astype(F32))
        gw[0, 0] = dot(midt[...], dga).astype(BF)
        gw[0, 1] = dot(midt[...], du).astype(BF)
        dmid[...] += dot_nt(dga, w[0, 0]) + dot_nt(du, w[1, 0])

    @pl.when(i == 2 * n - 1)
    def _():
        nn, rstd = norm_parts(dsum1[...])
        dm = dmid[...]
        gsmall[3:4, :] = colsum(dm * nn)
        gsmall[4:5, :] = colsum(dm)
        ds = norm_back(dm * small[3:4, :], nn, rstd)
        dsum1[...] = ds
        db = ds.astype(BF)
        gsmall[2:3, :] = colsum(db.astype(F32))
        dbt = ds.T.astype(BF)
        for r in range(parts):
            dattn[r] = dot(db, wout[r]).astype(BF)
            gwout[r] = dot(dbt, attn[r]).astype(BF)


def head_slopes(first_head, head_count):
    number = first_head + jnp.arange(head_count, dtype=jnp.int32)
    exponent = jnp.where(number < 8, number.astype(F32) + 1.0, number.astype(F32) - 7.5)
    return jnp.exp2(-exponent)


def params(**kw):
    return pltpu.CompilerParams(vmem_limit_bytes=VMEM_LIMIT, **kw)


def per_device(
    hidden_in, lengths, w_qkv, b_qv, w_out, b_out, ln1_gain, ln1_bias, w_gu, b_gu, w_down,
    b_down, ln2_gain, ln2_bias, cotangent,
):
    both = ("dp", "mp")
    n_dp, n_mp = lax.axis_size("dp"), lax.axis_size("mp")
    n = n_dp * n_mp
    mp_rank = lax.axis_index("mp")
    own, width = hidden_in.shape
    group = own * n_mp
    sds = jax.ShapeDtypeStruct

    small_own = jnp.concatenate(
        [b_qv, jnp.stack([b_out, ln1_gain, ln1_bias, b_down, ln2_gain, ln2_bias])], axis=0
    )
    small_flat = jnp.concatenate([small_own.reshape(1, -1), b_gu.reshape(1, -1)], axis=1)
    small_all = lax.all_gather(small_flat, both, axis=0, tiled=True)
    cut = small_own.size
    small = small_all[:, :cut].reshape(n, 8, -1).transpose(1, 0, 2).reshape(8, width)
    bgu = small_all[:, cut:].reshape(n, 2, -1).transpose(1, 0, 2).reshape(2, n_mp, -1)
    bgu = bgu.transpose(1, 0, 2)
    ff_part = bgu.shape[2]

    wq = w_qkv.astype(BF)
    wq_own = lax.all_gather(wq, "dp", axis=1, tiled=True)
    hid = lax.all_gather(hidden_in, "mp", axis=0, tiled=True)
    cols = wq.shape[2]
    heads = cols // HEAD

    attn_pack = jnp.concatenate([wq[0], wq[1], wq[2], w_out.T.astype(BF)], axis=1)
    pack = jnp.concatenate([w_gu.astype(BF), w_down.T.astype(BF)[None], attn_pack[None]], axis=0)
    weights = lax.all_gather(pack, ("mp", "dp"), axis=1, tiled=True)
    weights = weights.reshape(4, n_mp, width, ff_part)
    wqkv_full = weights[3, :, :, : 3 * cols]
    wout_full = weights[3, :, :, 3 * cols :]

    qv_bias = lax.dynamic_slice_in_dim(small[:2], mp_rank * cols, cols, 1)
    qkv_bias = jnp.stack([qv_bias[0], jnp.zeros_like(qv_bias[0]), qv_bias[1]])
    slopes = head_slopes(mp_rank * heads, heads)
    tail = group - LONGEST

    qkv, o, u, p, p2 = pl.pallas_call(
        attention_forward,
        out_shape=(
            sds((3, group, cols), BF),
            sds((n_mp, own, cols), BF),
            sds((heads, group, 2 * HEAD), F32),
            sds((heads, LONGEST, LONGEST), BF),
            sds((heads, tail, tail), BF),
        ),
        in_specs=[vmem(), vmem(), vmem(), smem(), smem()],
        out_specs=(vmem(), vmem(), vmem(), hbm(), vmem()),
        scratch_shapes=[
            pltpu.VMEM((cols, group), BF),
            pltpu.VMEM((heads, group, 2 * HEAD), BF),
            pltpu.VMEM((QB, LONGEST + LONGEST // QB * QB), F32),
            pltpu.VMEM((2, QB, LONGEST), BF),
            pltpu.SemaphoreType.DMA((2,)),
        ],
        compiler_params=params(),
        name="attention_forward",
    )(hid, wq_own, qkv_bias, slopes, lengths)

    attn = lax.all_to_all(o, "mp", 0, 0, tiled=True)

    fixed = lambda *s: pl.BlockSpec(s, lambda i: (0,) * len(s))
    walk = lambda i: jnp.where(i < n_mp, i, 2 * n_mp - 1 - i)
    back = lambda i: jnp.where(i < n_mp, n_mp - 1, 2 * n_mp - 1 - i)
    result, dsum1, dattn, gw, gwout, gsmall, gbgu = pl.pallas_call(
        middle,
        grid=(2 * n_mp,),
        out_shape=(
            sds((own, width), BF),
            sds((own, width), F32),
            sds((n_mp, own, cols), BF),
            sds((n_mp, 3, width, ff_part), BF),
            sds((n_mp, width, cols), BF),
            sds((8, width), F32),
            sds((n_mp, 2, ff_part), F32),
        ),
        in_specs=[
            fixed(n_mp, own, cols),
            fixed(own, width),
            fixed(own, width),
            fixed(n_mp, width, cols),
            fixed(8, width),
            pl.BlockSpec((1, 2, ff_part), lambda i: (walk(i), 0, 0)),
            pl.BlockSpec((3, 1, width, ff_part), lambda i: (0, walk(i), 0, 0)),
        ],
        out_specs=(
            fixed(own, width),
            fixed(own, width),
            fixed(n_mp, own, cols),
            pl.BlockSpec((1, 3, width, ff_part), lambda i: (back(i), 0, 0, 0)),
            fixed(n_mp, width, cols),
            fixed(8, width),
            pl.BlockSpec((1, 2, ff_part), lambda i: (back(i), 0, 0)),
        ),
        scratch_shapes=[
            pltpu.VMEM((own, width), F32),
            pltpu.VMEM((own, width), BF),
            pltpu.VMEM((width, own), BF),
            pltpu.VMEM((n_mp, own, ff_part), F32),
            pltpu.VMEM((n_mp, own, ff_part), F32),
            pltpu.VMEM((own, width), F32),
            pltpu.VMEM((own, width), BF),
            pltpu.VMEM((width, own), BF),
            pltpu.VMEM((own, width), F32),
        ],
        compiler_params=params(),
        name="middle",
    )(attn, hidden_in, cotangent, wout_full, small, bgu, weights[:3])

    g = lax.all_to_all(dattn, "mp", 0, 0, tiled=True)

    d = pl.pallas_call(
        attention_backward,
        out_shape=sds((n_mp, 3, own, cols), BF),
        in_specs=[vmem(), vmem(), vmem(), hbm(), vmem()],
        out_specs=vmem(),
        scratch_shapes=[
            pltpu.VMEM((heads, 2 * HEAD, group), BF),
            pltpu.VMEM((2, QB, LONGEST), BF),
            pltpu.VMEM((HEAD, group), F32),
            pltpu.VMEM((HEAD, group), F32),
            pltpu.SemaphoreType.DMA((2,)),
        ],
        compiler_params=params(),
        name="attention_backward",
    )(qkv, g, u, p, p2)

    dl = lax.all_to_all(d, "mp", 0, 0, tiled=True)
    grad_in = (
        dsum1
        + jnp.einsum(
            "rstc,rdsc->td",
            dl,
            wqkv_full.reshape(n_mp, width, 3, cols),
            preferred_element_type=F32,
        )
    ).astype(BF)
    gqkv = jnp.einsum(
        "rtd,rstc->sdc", hid.reshape(n_mp, own, width), d, preferred_element_type=F32
    ).astype(BF)
    sums = jnp.sum(d.astype(F32), axis=(0, 2))
    gqv = lax.dynamic_update_slice_in_dim(
        gsmall[:2], jnp.stack([sums[0], sums[2]]), mp_rank * cols, 1
    )
    gsmall = jnp.concatenate([gqv, gsmall[2:]], axis=0)

    gsmall = gsmall.reshape(8, n, -1).transpose(1, 0, 2).reshape(n, -1)
    gbgu = gbgu.transpose(1, 0, 2).reshape(2, n, -1).transpose(1, 0, 2).reshape(n, -1)
    gall = jnp.concatenate([gsmall, gbgu], axis=1)
    gown = lax.psum_scatter(gall, both, scatter_dimension=0, tiled=True)
    gs = gown[0, :cut].reshape(8, -1)
    g_gu = gown[0, cut:].reshape(2, -1)

    gqkv = lax.psum_scatter(gqkv, "dp", scatter_dimension=1, tiled=True).astype(F32)
    gw = lax.psum_scatter(gw, "dp", scatter_dimension=2, tiled=True)
    gw = gw.reshape(-1, ff_part)
    gw = lax.psum_scatter(gw, "mp", scatter_dimension=0, tiled=True).reshape(3, -1, ff_part)
    gwout = lax.psum_scatter(gwout, "dp", scatter_dimension=1, tiled=True)
    gwout = lax.psum_scatter(gwout, "mp", scatter_dimension=0, tiled=True)[0]
    return (
        result,
        grad_in,
        gqkv,
        gs[0:2],
        gwout.T.astype(F32),
        gs[2],
        gs[3],
        gs[4],
        gw[:2].astype(F32),
        g_gu,
        gw[2].T.astype(F32),
        gs[5],
        gs[6],
        gs[7],
    )


def solution(mesh):
    rows = P(("dp", "mp"), None)
    vec = P(("dp", "mp"))
    vecs = P(None, ("dp", "mp"))
    wide = P(None, "dp", "mp")
    tall = P("mp", "dp")
    return jax.shard_map(
        per_device,
        mesh=mesh,
        in_specs=(
            rows, P("dp", None), wide, vecs, tall, vec, vec, vec, wide, vecs, tall, vec, vec, vec,
            rows,
        ),
        out_specs=(
            rows, rows, wide, vecs, tall, vec, vec, vec, wide, vecs, tall, vec, vec, vec,
        ),
        check_vma=False,
    )
```

```python
import functools

import jax
import jax.numpy as jnp
from jax import lax
from jax.experimental import pallas as pl
from jax.experimental.pallas import tpu as pltpu
from jax.sharding import PartitionSpec as P

HEAD = 64
LONGEST = 1664
QB = 256
BF = jnp.bfloat16
F32 = jnp.float32
VMEM_LIMIT = 60 * 1024 * 1024


def dot(a, b):
    return lax.dot_general(a, b, (((1,), (0,)), ((), ())), preferred_element_type=F32)


def dot_nt(a, b):
    return lax.dot_general(a, b, (((1,), (1,)), ((), ())), preferred_element_type=F32)


def vmem():
    return pl.BlockSpec(memory_space=pltpu.VMEM)


def smem():
    return pl.BlockSpec(memory_space=pltpu.SMEM)


def hbm():
    return pl.BlockSpec(memory_space=pl.ANY)


MESH = pl.DeviceIdType.MESH
PIECES = 4


def greet(n_dp, n_mp, me_dp, me_mp):
    barrier = pltpu.get_barrier_semaphore()
    for j in range(1, n_mp):
        pl.semaphore_signal(
            barrier, 1, device_id=(me_dp, lax.rem(me_mp + j, n_mp)), device_id_type=MESH
        )
    for j in range(1, n_dp):
        pl.semaphore_signal(
            barrier, 1, device_id=(lax.rem(me_dp + j, n_dp), me_mp), device_id_type=MESH
        )
    pl.semaphore_wait(barrier, n_mp - 1 + n_dp - 1)


def front(
    n_dp, n_mp,
    x, wq, sin, slope, length,
    small, xt, qt, kp, vte, ut, attnt, p, p2,
    hid, wslot, wf, wb, slot1, ssum, slot2, bias, qs, kt, vext, dist, pbuf, obuf, land,
    hs_sem, hr_sem, ws_sem, wr_sem, s1s, s1r, s2s, s2r, os_sem, or_sem, psem,
):
    me_dp, me = lax.axis_index("dp"), lax.axis_index("mp")
    own = x.shape[0]
    group = own * n_mp
    wrows, cols = wq.shape[1], wq.shape[2]
    heads = cols // HEAD
    tail = group - LONGEST
    full = LONGEST // own
    rest = LONGEST - full * own
    piece = own // PIECES

    def across_mp(j, src, dst, ss, rs):
        to = lax.rem(me + j, n_mp)
        return pltpu.make_async_remote_copy(
            src_ref=src, dst_ref=dst, send_sem=ss, recv_sem=rs,
            device_id=(me_dp, to), device_id_type=MESH,
        )

    def across_dp(j, src, dst, ss, rs):
        to = lax.rem(me_dp + j, n_dp)
        return pltpu.make_async_remote_copy(
            src_ref=src, dst_ref=dst, send_sem=ss, recv_sem=rs,
            device_id=(to, me), device_id_type=MESH,
        )

    greet(n_dp, n_mp, me_dp, me)

    send1 = [across_mp(j, sin, slot1.at[j], s1s.at[j], s1r.at[j]) for j in range(1, n_mp)]
    sendw = [across_dp(j, wq, wslot.at[j], ws_sem.at[j], wr_sem.at[j]) for j in range(1, n_dp)]
    send2 = [across_dp(j, ssum, slot2.at[j], s2s.at[j], s2r.at[j]) for j in range(1, n_dp)]
    for c in send1 + sendw:
        c.start()

    def hidden(way, step, k):
        shard = me - step if way == 0 else me + step
        to = me + 1 if way == 0 else me - 1
        shard, to = jnp.clip(shard, 0, n_mp - 1), jnp.clip(to, 0, n_mp - 1)
        rows = pl.ds(k * piece, piece)
        src = x.at[rows, :] if step == 0 else hid.at[shard, rows, :]
        return pltpu.make_async_remote_copy(
            src_ref=src, dst_ref=hid.at[shard, rows, :],
            send_sem=hs_sem.at[way, step, k], recv_sem=hr_sem.at[way, step, k],
            device_id=(me_dp, to), device_id_type=MESH,
        )

    def sends(way, step):
        if way == 0:
            return (me >= step) & (me < n_mp - 1)
        return (me + step <= n_mp - 1) & (me > 0)

    def receives(way, step):
        return me - 1 - step >= 0 if way == 0 else me + 1 + step <= n_mp - 1

    def send_hidden(step, k):
        for way in range(2):

            @pl.when(sends(way, step))
            def _():
                hidden(way, step, k).start()

    def wait_hidden(step, k):
        for way in range(2):

            @pl.when(receives(way, step))
            def _():
                hidden(way, step, k).wait_recv()

    for k in range(PIECES):
        send_hidden(0, k)

    width = dist.shape[1]
    base = width - LONGEST
    i = lax.broadcasted_iota(jnp.int32, (QB, width), 0)
    j = lax.broadcasted_iota(jnp.int32, (QB, width), 1)
    dist[...] = jnp.abs(i + base - j).astype(F32)

    total = sin[...]
    for c in send1:
        c.wait_recv()
    for j in range(1, n_mp):
        total += slot1[j]
    ssum[...] = total
    for c in send2:
        c.start()

    for k in range(PIECES):
        wait_hidden(0, k)
        if n_mp > 2:
            send_hidden(1, k)

    for c in sendw:
        c.wait_recv()
    for j in range(n_dp):
        place = pl.multiple_of(lax.rem(me_dp - j + n_dp, n_dp) * wrows, wrows)
        for s in range(3):
            part = wq[s] if j == 0 else wslot[j, s]
            wf[s, pl.ds(place, wrows), :] = part.astype(F32)
    for s in range(3):
        wb[s] = wf[s].astype(BF)

    for c in send2:
        c.wait_recv()
    total = ssum[...]
    for j in range(1, n_dp):
        total += slot2[j]
    small[...] = total
    bias[...] = jnp.zeros_like(bias)
    for r in range(n_mp):

        @pl.when(me == r)
        def _():
            bias[0:2, :] = total[0:2, r * cols : (r + 1) * cols]

    one = jnp.where(lax.broadcasted_iota(jnp.int32, (QB, HEAD), 1) == 0, 1.0, 0.0)
    minus = jnp.where(lax.broadcasted_iota(jnp.int32, (HEAD, QB), 0) < 2, -1.0, 0.0)
    none = jnp.zeros((QB, HEAD), F32)

    def project(ref, shard):
        def part(c, _):
            rows = pl.ds(pl.multiple_of(c * QB, QB), QB)
            at = pl.ds(pl.multiple_of(shard * own + c * QB, QB), QB)
            xc = ref[rows, :]
            xt[:, at] = xc.astype(F32).T.astype(BF)
            q = (dot(xc, wb[0]) + bias[0:1, :]).astype(BF).astype(F32) * HEAD**-0.5
            qs[at, :] = q.astype(BF)
            qt[:, at] = q.T.astype(BF)
            k = dot(xc, wb[1])
            kt[:, at] = k.T.astype(BF)
            v = dot(xc, wb[2]) + bias[1:2, :]
            vt = v.T
            for h in range(heads):
                hs = slice(h * HEAD, (h + 1) * HEAD)
                kp[h, at, :] = jnp.concatenate([k[:, hs], none], axis=1).astype(BF)
                vext[h, at, :] = jnp.concatenate([v[:, hs], one], axis=1).astype(BF)
                vte[h, :, at] = jnp.concatenate([vt[hs], minus], axis=0).astype(BF)
            return 0

        lax.fori_loop(0, own // QB, part, 0)

    project(x, me)
    for step in range(1, n_mp):
        if step > 1:
            for k in range(PIECES):
                wait_hidden(step - 1, k)
                if step < n_mp - 1:
                    send_hidden(step, k)
        for way in range(2):

            @pl.when(receives(way, step - 1))
            def _():
                shard = me - step if way == 0 else me + step
                shard = jnp.clip(shard, 0, n_mp - 1)
                project(hid.at[shard], shard)

    def score_block(h, c, place, rows, sl):
        hs = slice(h * HEAD, (h + 1) * HEAD)
        row = c * own + place
        at = pl.ds(pl.multiple_of(row, 128), rows)
        s = dot(qs[at, hs], kt[hs, :LONGEST])
        off = pl.multiple_of(base - row, 128)
        s = s - sl * dist[:rows, pl.ds(off, LONGEST)]
        m = jnp.max(s, axis=1, keepdims=True)
        pb = jnp.exp(s - m).astype(BF)
        pbuf[h, at, :] = pb
        finish(h, c, place, at, rows, dot(pb, vext[h, :LONGEST, :]))

    def finish(h, c, place, at, rows, uu):
        uut = uu.T
        ut[h, :, at] = uut
        oh = uut[:HEAD] * (1.0 / uut[HEAD : HEAD + 1])
        obuf[c, h * HEAD : (h + 1) * HEAD, pl.ds(place, rows)] = oh.astype(BF)

    def short_block(h, c, sl):
        hs = slice(h * HEAD, (h + 1) * HEAD)
        s = dot(qs[LONGEST:, hs], kt[hs, LONGEST:])
        ii = lax.broadcasted_iota(jnp.int32, (tail, tail), 0)
        jj = lax.broadcasted_iota(jnp.int32, (tail, tail), 1)
        s = s - sl * jnp.abs(ii - jj).astype(F32)
        cut = length[0, 1]
        s = jnp.where((ii < cut) == (jj < cut), s, -1e30)
        m = jnp.max(s, axis=1, keepdims=True)
        pb = jnp.exp(s - m).astype(BF)
        p2[h] = pb
        finish(h, c, rest, pl.ds(LONGEST, tail), tail, dot(pb, vext[h, LONGEST:, :]))

    def out_copy(h, j):
        to = lax.rem(me + j, n_mp)
        hs = pl.ds(h * HEAD, HEAD)
        return pltpu.make_async_remote_copy(
            src_ref=obuf.at[to, hs, :], dst_ref=land.at[j, hs, :],
            send_sem=os_sem.at[h, j], recv_sem=or_sem.at[h, j],
            device_id=(me_dp, to), device_id_type=MESH,
        )

    for h in range(heads):
        sl = slope[h]

        def chunk(j, _):
            c = lax.rem(me + 1 + j, n_mp)

            @pl.when(c < full)
            def _():
                for half in range(own // QB):
                    score_block(h, c, half * QB, QB, sl)

            @pl.when(c == full)
            def _():
                score_block(h, c, 0, rest, sl)
                short_block(h, c, sl)

            @pl.when(j < n_mp - 1)
            def _():
                out_copy(h, j + 1).start()

            return 0

        lax.fori_loop(0, n_mp, chunk, 0)
        pltpu.make_async_copy(pbuf.at[h], p.at[h], psem.at[h]).start()

    attnt[me] = obuf[me]
    for h in range(heads):
        hs = slice(h * HEAD, (h + 1) * HEAD)
        for j in range(1, n_mp):
            out_copy(h, j).wait_recv()
            attnt[lax.rem(me - j + n_mp, n_mp), hs, :] = land[j, hs, :]
    for h in range(heads):
        for j in range(1, n_mp):
            out_copy(h, j).wait_send()
        pltpu.make_async_copy(pbuf.at[h], p.at[h], psem.at[h]).wait()
    for c in send1 + sendw + send2:
        c.wait_send()
    for step in range(n_mp - 1):
        for k in range(PIECES):
            for way in range(2):

                @pl.when(sends(way, step))
                def _():
                    hidden(way, step, k).wait_send()


def back(
    n_dp, n_mp,
    gt, xt, qt, kp, vte, ut, p, p2, weights, dsum1, sin, gw, gwo,
    grad_in, gq, small, gff, gout,
    gl, pbuf, dkt, dvt, dbuf, dland, wfull, gbuf, qland, ssum, slot1, slot2,
    pair, cland, xland, zsum, zland, opair, ocland, oxland, ozsum, ozland,
    gs_sem, gr_sem, qs_sem, qr_sem, ds_sem, dr_sem, ws_sem, wr_sem, s1s, s1r, s2s, s2r,
    psem, wsem, ls_sem, cs_sem, cr_sem, xs_sem, xr_sem, zs_sem, zr_sem,
):
    me_dp, me = lax.axis_index("dp"), lax.axis_index("mp")
    own = gt.shape[2]
    cols = gt.shape[1]
    heads = cols // HEAD
    group = own * n_mp
    tail = group - LONGEST
    full = LONGEST // own
    rest = LONGEST - full * own
    wrows = gq.shape[0]

    def across_mp(j, src, dst, ss, rs):
        to = lax.rem(me + j, n_mp)
        return pltpu.make_async_remote_copy(
            src_ref=src, dst_ref=dst, send_sem=ss, recv_sem=rs,
            device_id=(me_dp, to), device_id_type=MESH,
        )

    def across_dp(j, src, dst, ss, rs):
        to = lax.rem(me_dp + j, n_dp)
        return pltpu.make_async_remote_copy(
            src_ref=src, dst_ref=dst, send_sem=ss, recv_sem=rs,
            device_id=(to, me), device_id_type=MESH,
        )

    def fetch_p(h, j, act):
        c = lax.rem(me - j + n_mp, n_mp)
        slot = lax.rem(h * n_mp + j, 2)

        @pl.when(c < full)
        def _():
            rows = pl.ds(pl.multiple_of(c * own, own), own)
            act(pltpu.make_async_copy(p.at[h, rows, :], pbuf.at[slot], psem.at[slot]))

        @pl.when(c == full)
        def _():
            src = p.at[h, pl.ds(full * own, rest), :]
            act(pltpu.make_async_copy(src, pbuf.at[slot, pl.ds(0, rest), :], psem.at[slot]))

    start, wait = lambda copy: copy.start(), lambda copy: copy.wait()
    fetch_p(0, 0, start)
    fetch_w = pltpu.make_async_copy(weights.at[3], wfull, wsem)

    n_q = n_dp // 2
    me_q, me_c = me_dp // 2, lax.rem(me_dp, 2)
    other = me_dp + 1 - 2 * me_c
    kinds = ((gw, pair, cland, xland, zsum, zland), (gwo, opair, ocland, oxland, ozsum, ozland))

    def rank_of(o):
        return lax.rem(me + 1 + o, n_mp)

    def load_copy(o, t):
        src, own_part = kinds[t][:2]
        return pltpu.make_async_copy(
            src.at[rank_of(o), :, :, me_c], own_part.at[o], ls_sem.at[o, t]
        )

    def pair_up(o, t):
        src, land = kinds[t][0], kinds[t][2]
        return pltpu.make_async_remote_copy(
            src_ref=src.at[rank_of(o), :, :, 1 - me_c], dst_ref=land.at[o],
            send_sem=cs_sem.at[o, t], recv_sem=cr_sem.at[o, t],
            device_id=(other, me), device_id_type=MESH,
        )

    def cross(o, j, t):
        src, land = kinds[t][1], kinds[t][3]
        to = lax.rem(me_q + j, n_q)
        return pltpu.make_async_remote_copy(
            src_ref=src.at[o, :, to], dst_ref=land.at[o, j - 1],
            send_sem=xs_sem.at[o, j, t], recv_sem=xr_sem.at[o, j, t],
            device_id=(to * 2 + me_c, me), device_id_type=MESH,
        )

    def along(o, t):
        src, land = kinds[t][4:]
        return pltpu.make_async_remote_copy(
            src_ref=src.at[o], dst_ref=land.at[o],
            send_sem=zs_sem.at[o, t], recv_sem=zr_sem.at[o, t],
            device_id=(me_dp, rank_of(o)), device_id_type=MESH,
        )

    def add_pair(o):
        for t in range(2):
            own_part, land = kinds[t][1], kinds[t][2]
            load_copy(o, t).wait()
            pair_up(o, t).wait_recv()
            mats = own_part.shape[1]

            def add(i, _):
                a = own_part[o, i // n_q, lax.rem(i, n_q)].astype(F32)
                b = land[o, i // n_q, lax.rem(i, n_q)].astype(F32)
                own_part[o, i // n_q, lax.rem(i, n_q)] = (a + b).astype(BF)
                return 0

            lax.fori_loop(0, mats * n_q, add, 0)
            for j in range(1, n_q):
                cross(o, j, t).start()

    def add_cross(o):
        for t in range(2):
            own_part, land, total = kinds[t][1], kinds[t][3], kinds[t][4]
            for j in range(1, n_q):
                cross(o, j, t).wait_recv()
            for m in range(own_part.shape[1]):
                a = own_part[o, m, me_q].astype(F32)
                for j in range(1, n_q):
                    a += land[o, j - 1, m].astype(F32)
                total[o, m] = a.astype(BF)
            if o < n_mp - 1:
                along(o, t).start()

    for o in range(n_mp):
        for t in range(2):
            load_copy(o, t).start()

    greet(n_dp, n_mp, me_dp, me)

    def grad_copy(h, j):
        hs = pl.ds(h * HEAD, HEAD)
        to = lax.rem(me + j, n_mp)
        return across_mp(
            j, gt.at[to, hs, :], gl.at[j, hs, :], gs_sem.at[h, j], gr_sem.at[h, j]
        )

    for h in range(heads):
        for j in range(1, n_mp):
            grad_copy(h, j).start()
    for o in range(n_mp):
        for t in range(2):
            pair_up(o, t).start()
    fetch_w.start()
    gl[0] = gt[me]

    def query_copy(h, j):
        to = lax.rem(me - j + n_mp, n_mp)
        hs = pl.ds(h * HEAD, HEAD)
        return pltpu.make_async_remote_copy(
            src_ref=dbuf.at[to, 0, hs, :], dst_ref=dland.at[j, 0, hs, :],
            send_sem=qs_sem.at[h, j], recv_sem=qr_sem.at[h, j],
            device_id=(me_dp, to), device_id_type=MESH,
        )

    def pair_copy(h, j):
        to = lax.rem(me - j + n_mp, n_mp)
        hs = pl.ds(h * HEAD, HEAD)
        return pltpu.make_async_remote_copy(
            src_ref=dbuf.at[to, pl.ds(1, 2), hs, :], dst_ref=dland.at[j, pl.ds(1, 2), hs, :],
            send_sem=ds_sem.at[h, j], recv_sem=dr_sem.at[h, j],
            device_id=(me_dp, to), device_id_type=MESH,
        )

    def block(h, j, c, place, rows, pb, keys, add):
        row = c * own + place
        at = pl.ds(pl.multiple_of(row, 128), rows)
        hs = slice(h * HEAD, (h + 1) * HEAD)
        uu = ut[h, :, at]
        inv = 1.0 / uu[HEAD : HEAD + 1]
        gg = gl[j, hs, pl.ds(place, rows)].astype(F32) * inv
        total = jnp.sum(gg * uu[:HEAD], axis=0, keepdims=True) * inv
        high = total.astype(BF).astype(F32)
        low = total - high
        index = lax.broadcasted_iota(jnp.int32, (HEAD, rows), 0)
        extra = jnp.where(index == 0, high, jnp.where(index == 1, low, 0.0))
        gext = jnp.concatenate([gg, extra], axis=0).T.astype(BF)
        dp = dot(gext, vte[h, :, keys])
        ds = (pb.astype(F32) * dp).astype(BF)
        dq = dot(ds, kp[h, keys, :]).T[:HEAD] * (HEAD**-0.5)
        dbuf[c, 0, hs, pl.ds(place, rows)] = dq.astype(BF)
        dk = dot(qt[hs, at], ds)
        dv = dot(gg.astype(BF), pb)
        if add:
            dkt[:, keys] = dkt[:, keys] + dk
            dvt[:, keys] = dvt[:, keys] + dv
        else:
            dkt[:, keys] = dk
            dvt[:, keys] = dv

    pump = [1 + o for o in range(n_mp)]
    for h in range(heads):
        hs = slice(h * HEAD, (h + 1) * HEAD)
        dkt[:, :LONGEST] = jnp.zeros((HEAD, LONGEST), F32)
        dvt[:, :LONGEST] = jnp.zeros((HEAD, LONGEST), F32)

        def chunk(j, _):
            c = lax.rem(me - j + n_mp, n_mp)
            slot = lax.rem(h * n_mp + j, 2)

            @pl.when(j < n_mp - 1)
            def _():
                fetch_p(h, j + 1, start)

            if h < heads - 1:

                @pl.when(j == n_mp - 1)
                def _():
                    fetch_p(h + 1, 0, start)

            @pl.when(j > 0)
            def _():
                grad_copy(h, j).wait_recv()

            fetch_p(h, j, wait)

            keys = slice(0, LONGEST)

            @pl.when(c < full)
            def _():
                for half in range(own // QB):
                    at = pl.ds(half * QB, QB)
                    block(h, j, c, half * QB, QB, pbuf[slot, at, :], keys, True)

            @pl.when(c == full)
            def _():
                block(h, j, c, 0, rest, pbuf[slot, :rest, :], keys, True)
                block(h, j, c, rest, tail, p2[h], slice(LONGEST, group), False)

            @pl.when(j > 0)
            def _():
                query_copy(h, j).start()

            for o in range(n_mp):
                if pump[o] // n_mp == h:

                    @pl.when(j == pump[o] % n_mp)
                    def _():
                        add_pair(o)

            return 0

        lax.fori_loop(0, n_mp, chunk, 0)
        if h == heads - 1:
            add_cross(0)
        for c in range(n_mp):
            dbuf[c, 1, hs, :] = dkt[:, c * own : (c + 1) * own].astype(BF)
            dbuf[c, 2, hs, :] = dvt[:, c * own : (c + 1) * own].astype(BF)
        for j in range(1, n_mp):
            pair_copy(h, j).start()

    ones = jnp.ones((8, own), BF)
    sq = jnp.zeros((8, cols), F32)
    sv = jnp.zeros((8, cols), F32)
    for c in range(n_mp):
        sq += dot_nt(ones, dbuf[c, 0])
        sv += dot_nt(ones, dbuf[c, 2])
    ssum[...] = sin[...]
    for r in range(n_mp):

        @pl.when(me == r)
        def _():
            ssum[0:1, r * cols : (r + 1) * cols] = sq[0:1]
            ssum[1:2, r * cols : (r + 1) * cols] = sv[0:1]

    send1 = [across_mp(j, ssum, slot1.at[j], s1s.at[j], s1r.at[j]) for j in range(1, n_mp)]
    for c in send1:
        c.start()

    total = jnp.zeros((xt.shape[0], 3 * cols), F32)
    for c in range(n_mp):
        total += dot_nt(xt[:, c * own : (c + 1) * own], dbuf[c].reshape(3 * cols, own))
    for d in range(n_dp):
        gbuf[d] = total[d * wrows : (d + 1) * wrows].astype(BF)

    def weight_copy(j):
        to = lax.rem(me_dp + j, n_dp)
        return across_dp(j, gbuf.at[to], qland.at[j], ws_sem.at[j], wr_sem.at[j])

    for j in range(1, n_dp):
        weight_copy(j).start()

    add_cross(1)
    for c in send1:
        c.wait_send()
        c.wait_recv()
    total = ssum[...]
    for j in range(1, n_mp):
        total += slot1[j]
    ssum[...] = total
    send2 = [across_dp(j, ssum, slot2.at[j], s2s.at[j], s2r.at[j]) for j in range(1, n_dp)]
    for c in send2:
        c.start()

    fetch_w.wait()
    into = dot(wfull[me, :, : 3 * cols], dbuf[me].reshape(3 * cols, own))
    for j in range(1, n_mp):
        for h in range(heads):
            query_copy(h, j).wait_recv()
            pair_copy(h, j).wait_recv()
        r = lax.rem(me + j, n_mp)
        into += dot(wfull[r, :, : 3 * cols], dland[j].reshape(3 * cols, own))
    grad_in[...] = (dsum1[...] + into.T).astype(BF)

    for o in range(2, n_mp):
        add_cross(o)
    total = gbuf[me_dp].astype(F32)
    for j in range(1, n_dp):
        weight_copy(j).wait_recv()
        total += qland[j].astype(F32)
    gq[...] = total
    total = ssum[...]
    for c in send2:
        c.wait_recv()
    for j in range(1, n_dp):
        total += slot2[j]
    small[...] = total
    for t, out in ((0, gff), (1, gout)):
        total, land = kinds[t][4:]
        for o in range(n_mp - 1):
            along(o, t).wait_recv()
        for m in range(out.shape[0]):
            a = total[n_mp - 1, m].astype(F32)
            for o in range(n_mp - 1):
                a += land[o, m].astype(F32)
            out[m] = a
    for t in range(2):
        for o in range(n_mp):
            pair_up(o, t).wait_send()
            for j in range(1, n_q):
                cross(o, j, t).wait_send()
            if o < n_mp - 1:
                along(o, t).wait_send()
    for c in send2:
        c.wait_send()
    for j in range(1, n_dp):
        weight_copy(j).wait_send()
    for h in range(heads):
        for j in range(1, n_mp):
            grad_copy(h, j).wait_send()
            query_copy(h, j).wait_send()
            pair_copy(h, j).wait_send()


def norm_parts(r):
    centre = r - jnp.mean(r, axis=-1, keepdims=True)
    spread = jnp.mean(centre * centre, axis=-1, keepdims=True)
    rstd = lax.rsqrt(spread + 1e-05)
    return centre * rstd, rstd


def norm_back(dn, n, rstd):
    return rstd * (
        dn - jnp.mean(dn, axis=-1, keepdims=True) - n * jnp.mean(dn * n, axis=-1, keepdims=True)
    )


def colsum(a):
    return jnp.sum(a, axis=0, keepdims=True)


def flip(a):
    return a.astype(F32).T.astype(BF)


GELU_C = 0.7978845608
GELU_A = 0.044715


def middle(
    attn, x, cot, wlast, small, w,
    result, dsum1, dattn, gw, gwout, gsmall,
    wout, mid, midb, midt, gate, up, y, dffn, dffnt, dmid,
):
    i = pl.program_id(0)
    n = pl.num_programs(0) // 2
    parts, cols = attn.shape[0], attn.shape[1]

    @pl.when(i == 0)
    def _():
        branch = jnp.zeros((x.shape[1], x.shape[0]), F32)
        for r in range(parts):
            wout[r] = wlast[0, r, :, 3 * cols :]
            branch += dot(wout[r], attn[r])
        branch = branch.T + x[...].astype(F32) + small[2:3, :]
        nn, _ = norm_parts(branch)
        m = nn * small[3:4, :] + small[4:5, :]
        dsum1[...] = branch
        mid[...] = m
        midb[...] = m.astype(BF)
        midt[...] = m.T.astype(BF)
        y[...] = jnp.zeros_like(y)

    @pl.when(i < n)
    def _():
        mb = midb[...]
        ga = dot(mb, w[0, 0]) + small[pl.ds(8 + i, 1), :]
        u = dot(mb, w[1, 0]) + small[pl.ds(8 + n + i, 1), :]
        gate[i] = ga
        up[i] = u
        t = jnp.tanh(GELU_C * (ga + GELU_A * ga * ga * ga))
        act = (0.5 * ga * (1.0 + t) * u).astype(BF)
        y[...] += dot_nt(act, w[2, 0])

    @pl.when(i == n - 1)
    def _():
        r = mid[...] + y[...] + small[5:6, :]
        nn, rstd = norm_parts(r)
        gain = small[6:7, :]
        result[...] = (nn * gain + small[7:8, :]).astype(BF)
        c = cot[...].astype(F32)
        ds = norm_back(c * gain, nn, rstd)
        gsmall[6:7, :] = colsum(c * nn)
        gsmall[7:8, :] = colsum(c)
        dmid[...] = ds
        db = ds.astype(BF)
        dffn[...] = db
        dffnt[...] = ds.T.astype(BF)
        gsmall[5:6, :] = colsum(db.astype(F32))
        gsmall[0:2, :] = jnp.zeros_like(gsmall[0:2, :])

    @pl.when(i >= n)
    def _():
        k = 2 * n - 1 - i
        ga = gate[k]
        u = up[k]
        sq = ga * ga
        t = jnp.tanh(GELU_C * (ga + GELU_A * ga * sq))
        half = 0.5 * (1.0 + t)
        gelu = ga * half
        slope = half + (0.5 * GELU_C) * ga * (1.0 - t * t) * (1.0 + 3.0 * GELU_A * sq)
        act = (gelu * u).astype(BF)
        dact = dot(dffn[...], w[2, 0])
        gw[0, 2] = dot(dffnt[...], act).astype(BF)
        dga = (dact * u * slope).astype(BF)
        du = (dact * gelu).astype(BF)
        gsmall[pl.ds(8 + k, 1), :] = colsum(dga.astype(F32))
        gsmall[pl.ds(8 + n + k, 1), :] = colsum(du.astype(F32))
        gw[0, 0] = dot(midt[...], dga).astype(BF)
        gw[0, 1] = dot(midt[...], du).astype(BF)
        dmid[...] += dot_nt(dga, w[0, 0]) + dot_nt(du, w[1, 0])

    @pl.when(i == 2 * n - 1)
    def _():
        nn, rstd = norm_parts(dsum1[...])
        dm = dmid[...]
        gsmall[3:4, :] = colsum(dm * nn)
        gsmall[4:5, :] = colsum(dm)
        ds = norm_back(dm * small[3:4, :], nn, rstd)
        dsum1[...] = ds
        db = ds.astype(BF)
        gsmall[2:3, :] = colsum(db.astype(F32))
        dbt = ds.T.astype(BF)
        for r in range(parts):
            dattn[r] = dot(db, wout[r]).T.astype(BF)
            gwout[r] = dot_nt(dbt, attn[r]).astype(BF)


def head_slopes(first_head, head_count):
    number = first_head + jnp.arange(head_count, dtype=jnp.int32)
    exponent = jnp.where(number < 8, number.astype(F32) + 1.0, number.astype(F32) - 7.5)
    return jnp.exp2(-exponent)


def cost(flops):
    return pl.CostEstimate(flops=flops, bytes_accessed=1 << 24, transcendentals=0)


def params(**kw):
    return pltpu.CompilerParams(vmem_limit_bytes=VMEM_LIMIT, **kw)


def per_device(
    hidden_in, lengths, w_qkv, b_qv, w_out, b_out, ln1_gain, ln1_bias, w_gu, b_gu, w_down,
    b_down, ln2_gain, ln2_bias, cotangent,
):
    both = ("dp", "mp")
    n_dp, n_mp = lax.axis_size("dp"), lax.axis_size("mp")
    n = n_dp * n_mp
    mp_rank = lax.axis_index("mp")
    own, width = hidden_in.shape
    group = own * n_mp
    sds = jax.ShapeDtypeStruct

    dev = lax.axis_index("dp") * n_mp + mp_rank

    def placed(a):
        zero = jnp.zeros((a.shape[0], a.shape[1] * n), F32)
        return lax.dynamic_update_slice_in_dim(zero, a, dev * a.shape[1], 1)

    vectors = jnp.stack([b_out, ln1_gain, ln1_bias, b_down, ln2_gain, ln2_bias])
    vectors = jnp.concatenate([b_qv, vectors], axis=0)
    small_own = jnp.concatenate(
        [placed(vectors), placed(b_gu).reshape(-1, width)], axis=0
    )
    srows = small_own.shape[0]

    wq = w_qkv.astype(BF)
    wrows, cols = wq.shape[1], wq.shape[2]
    ff_part = w_gu.shape[2]
    heads = cols // HEAD
    tail = group - LONGEST

    attn_pack = jnp.concatenate([wq[0], wq[1], wq[2], w_out.T.astype(BF)], axis=1)
    pack = jnp.concatenate([w_gu.astype(BF), w_down.T.astype(BF)[None], attn_pack[None]], axis=0)
    weights = lax.all_gather(pack, ("mp", "dp"), axis=1, tiled=True)
    weights = weights.reshape(4, n_mp, width, ff_part)

    slopes = head_slopes(mp_rank * heads, heads)
    dma = pltpu.SemaphoreType.DMA

    small, xt, qt, kp, vte, ut, attn, p, p2 = pl.pallas_call(
        functools.partial(front, n_dp, n_mp),
        out_shape=(
            sds((srows, width), F32),
            sds((width, group), BF),
            sds((cols, group), BF),
            sds((heads, group, 2 * HEAD), BF),
            sds((heads, 2 * HEAD, group), BF),
            sds((heads, 2 * HEAD, group), F32),
            sds((n_mp, cols, own), BF),
            sds((heads, LONGEST, LONGEST), BF),
            sds((heads, tail, tail), BF),
        ),
        in_specs=[vmem(), vmem(), vmem(), smem(), smem()],
        out_specs=(vmem(), vmem(), vmem(), vmem(), vmem(), vmem(), vmem(), hbm(), vmem()),
        scratch_shapes=[
            pltpu.VMEM((n_mp, own, width), BF),
            pltpu.VMEM((n_dp, 3, wrows, cols), BF),
            pltpu.VMEM((3, width, cols), F32),
            pltpu.VMEM((3, width, cols), BF),
            pltpu.VMEM((n_mp, srows, width), F32),
            pltpu.VMEM((srows, width), F32),
            pltpu.VMEM((n_dp, srows, width), F32),
            pltpu.VMEM((8, cols), F32),
            pltpu.VMEM((group, cols), BF),
            pltpu.VMEM((cols, group), BF),
            pltpu.VMEM((heads, group, 2 * HEAD), BF),
            pltpu.VMEM((QB, LONGEST + LONGEST // QB * QB), F32),
            pltpu.VMEM((heads, LONGEST, LONGEST), BF),
            pltpu.VMEM((n_mp, cols, own), BF),
            pltpu.VMEM((n_mp, cols, own), BF),
            dma((2, n_mp - 1, PIECES)),
            dma((2, n_mp - 1, PIECES)),
            dma((n_dp,)),
            dma((n_dp,)),
            dma((n_mp,)),
            dma((n_mp,)),
            dma((n_dp,)),
            dma((n_dp,)),
            dma((heads, n_mp)),
            dma((heads, n_mp)),
            dma((heads,)),
        ],
        compiler_params=params(collective_id=0, has_side_effects=True),
        cost_estimate=cost(11 * LONGEST * LONGEST * HEAD * heads * 12),
        name="front",
    )(hidden_in, wq, small_own, slopes, lengths)

    fixed = lambda *s: pl.BlockSpec(s, lambda i: (0,) * len(s))
    walk = lambda i: jnp.where(i < n_mp, i, 2 * n_mp - 1 - i)
    late = lambda i: jnp.where(i < n_mp, n_mp - 1, 2 * n_mp - 1 - i)
    result, dsum1, dattn, gw, gwout, gsmall = pl.pallas_call(
        middle,
        grid=(2 * n_mp,),
        out_shape=(
            sds((own, width), BF),
            sds((own, width), F32),
            sds((n_mp, cols, own), BF),
            sds((n_mp, 3, width, ff_part), BF),
            sds((n_mp, width, cols), BF),
            sds((srows, width), F32),
        ),
        in_specs=[
            fixed(n_mp, cols, own),
            fixed(own, width),
            fixed(own, width),
            pl.BlockSpec(
                (1, n_mp, width, ff_part),
                lambda i: (3, 0, 0, 0),
                pipeline_mode=pl.Buffered(1),
            ),
            fixed(srows, width),
            pl.BlockSpec((3, 1, width, ff_part), lambda i: (0, walk(i), 0, 0)),
        ],
        out_specs=(
            fixed(own, width),
            fixed(own, width),
            fixed(n_mp, cols, own),
            pl.BlockSpec((1, 3, width, ff_part), lambda i: (late(i), 0, 0, 0)),
            fixed(n_mp, width, cols),
            fixed(srows, width),
        ),
        scratch_shapes=[
            pltpu.VMEM((n_mp, width, cols), BF),
            pltpu.VMEM((own, width), F32),
            pltpu.VMEM((own, width), BF),
            pltpu.VMEM((width, own), BF),
            pltpu.VMEM((n_mp, own, ff_part), F32),
            pltpu.VMEM((n_mp, own, ff_part), F32),
            pltpu.VMEM((own, width), F32),
            pltpu.VMEM((own, width), BF),
            pltpu.VMEM((width, own), BF),
            pltpu.VMEM((own, width), F32),
        ],
        compiler_params=params(),
        name="middle",
    )(attn, hidden_in, cotangent, weights, small, weights)

    n_q = n_dp // 2
    gw = gw.reshape(n_mp, 3, n_q, 2, wrows, ff_part)
    gwout = gwout.reshape(n_mp, 1, n_q, 2, wrows, cols)
    grad_in, gqkv, gsmall, gff, gout = pl.pallas_call(
        functools.partial(back, n_dp, n_mp),
        out_shape=(
            sds((own, width), BF),
            sds((wrows, 3 * cols), F32),
            sds((srows, width), F32),
            sds((3, wrows, ff_part), F32),
            sds((1, wrows, cols), F32),
        ),
        in_specs=[
            vmem(), vmem(), vmem(), vmem(), vmem(), vmem(), hbm(), vmem(), hbm(), vmem(), vmem(),
            hbm(), hbm(),
        ],
        out_specs=(vmem(), vmem(), vmem(), vmem(), vmem()),
        scratch_shapes=[
            pltpu.VMEM((n_mp, cols, own), BF),
            pltpu.VMEM((2, own, LONGEST), BF),
            pltpu.VMEM((HEAD, group), F32),
            pltpu.VMEM((HEAD, group), F32),
            pltpu.VMEM((n_mp, 3, cols, own), BF),
            pltpu.VMEM((n_mp, 3, cols, own), BF),
            pltpu.VMEM((n_mp, width, ff_part), BF),
            pltpu.VMEM((n_dp, wrows, 3 * cols), BF),
            pltpu.VMEM((n_dp, wrows, 3 * cols), BF),
            pltpu.VMEM((srows, width), F32),
            pltpu.VMEM((n_mp, srows, width), F32),
            pltpu.VMEM((n_dp, srows, width), F32),
            pltpu.VMEM((n_mp, 3, n_q, wrows, ff_part), BF),
            pltpu.VMEM((n_mp, 3, n_q, wrows, ff_part), BF),
            pltpu.VMEM((n_mp, n_q - 1, 3, wrows, ff_part), BF),
            pltpu.VMEM((n_mp, 3, wrows, ff_part), BF),
            pltpu.VMEM((n_mp - 1, 3, wrows, ff_part), BF),
            pltpu.VMEM((n_mp, 1, n_q, wrows, cols), BF),
            pltpu.VMEM((n_mp, 1, n_q, wrows, cols), BF),
            pltpu.VMEM((n_mp, n_q - 1, 1, wrows, cols), BF),
            pltpu.VMEM((n_mp, 1, wrows, cols), BF),
            pltpu.VMEM((n_mp - 1, 1, wrows, cols), BF),
            dma((heads, n_mp)),
            dma((heads, n_mp)),
            dma((heads, n_mp)),
            dma((heads, n_mp)),
            dma((heads, n_mp)),
            dma((heads, n_mp)),
            dma((n_dp,)),
            dma((n_dp,)),
            dma((n_mp,)),
            dma((n_mp,)),
            dma((n_dp,)),
            dma((n_dp,)),
            dma((2,)),
            dma,
            dma((n_mp, 2)),
            dma((n_mp, 2)),
            dma((n_mp, 2)),
            dma((n_mp, n_q, 2)),
            dma((n_mp, n_q, 2)),
            dma((n_mp - 1, 2)),
            dma((n_mp - 1, 2)),
        ],
        compiler_params=params(collective_id=1, has_side_effects=True),
        cost_estimate=cost(11 * LONGEST * LONGEST * HEAD * heads * 12),
        name="back",
    )(dattn, xt, qt, kp, vte, ut, p, p2, weights, dsum1, gsmall, gw, gwout)

    def own_columns(a):
        part = a.shape[1] // n
        return lax.dynamic_slice_in_dim(a, dev * part, part, 1)

    gs = own_columns(gsmall[:8])
    g_gu = own_columns(gsmall[8:].reshape(2, -1))
    gqkv = gqkv.reshape(wrows, 3, cols).transpose(1, 0, 2)

    return (
        result,
        grad_in,
        gqkv,
        gs[0:2],
        gout[0].T,
        gs[2],
        gs[3],
        gs[4],
        gff[:2],
        g_gu,
        gff[2].T,
        gs[5],
        gs[6],
        gs[7],
    )


def solution(mesh):
    rows = P(("dp", "mp"), None)
    vec = P(("dp", "mp"))
    vecs = P(None, ("dp", "mp"))
    wide = P(None, "dp", "mp")
    tall = P("mp", "dp")
    return jax.shard_map(
        per_device,
        mesh=mesh,
        in_specs=(
            rows, P("dp", None), wide, vecs, tall, vec, vec, vec, wide, vecs, tall, vec, vec, vec,
            rows,
        ),
        out_specs=(
            rows, rows, wide, vecs, tall, vec, vec, vec, wide, vecs, tall, vec, vec, vec,
        ),
        check_vma=False,
    )
```

```python
import functools

import jax
import jax.numpy as jnp
from jax import lax
from jax.experimental import pallas as pl
from jax.experimental.pallas import tpu as pltpu
from jax.sharding import PartitionSpec as P

HEAD = 64
LONGEST = 1664
QB = 256
BF = jnp.bfloat16
F32 = jnp.float32
VMEM_LIMIT = 60 * 1024 * 1024


def dot(a, b):
    return lax.dot_general(a, b, (((1,), (0,)), ((), ())), preferred_element_type=F32)


def dot_nt(a, b):
    return lax.dot_general(a, b, (((1,), (1,)), ((), ())), preferred_element_type=F32)


def vmem():
    return pl.BlockSpec(memory_space=pltpu.VMEM)


def smem():
    return pl.BlockSpec(memory_space=pltpu.SMEM)


def hbm():
    return pl.BlockSpec(memory_space=pl.ANY)


MESH = pl.DeviceIdType.MESH
PIECES = 4


def greet(n_dp, n_mp, me_dp, me_mp):
    barrier = pltpu.get_barrier_semaphore()
    for j in range(1, n_mp):
        pl.semaphore_signal(
            barrier, 1, device_id=(me_dp, lax.rem(me_mp + j, n_mp)), device_id_type=MESH
        )
    for j in range(1, n_dp):
        pl.semaphore_signal(
            barrier, 1, device_id=(lax.rem(me_dp + j, n_dp), me_mp), device_id_type=MESH
        )
    pl.semaphore_wait(barrier, n_mp - 1 + n_dp - 1)


def front(
    n_dp, n_mp,
    x, pack, sin, slope, length,
    small, xt_out, qt_out, kp_out, vte_out, ut_out, attnt, p, p2_out, wall,
    xt, qt, kp, vte, ut, p2, hid, wslot, wf, wb, slot1, ssum, slot2, bias, qs, kt, vext, dist, pbuf, obuf, land,
    hs_sem, hr_sem, s1s, s1r, s2s, s2r, os_sem, or_sem, psem,
    local_sem, early_sem, late_sem, wzs, wzr, wqs, wqr, wps, wpr,
):
    me_dp, me = lax.axis_index("dp"), lax.axis_index("mp")
    own = x.shape[0]
    group = own * n_mp
    wrows, cols = pack.shape[1], wb.shape[2]
    heads = cols // HEAD
    tail = group - LONGEST
    full = LONGEST // own
    rest = LONGEST - full * own
    piece = own // PIECES

    def across_mp(j, src, dst, ss, rs):
        to = lax.rem(me + j, n_mp)
        return pltpu.make_async_remote_copy(
            src_ref=src, dst_ref=dst, send_sem=ss, recv_sem=rs,
            device_id=(me_dp, to), device_id_type=MESH,
        )

    def across_dp(j, src, dst, ss, rs):
        to = lax.rem(me_dp + j, n_dp)
        return pltpu.make_async_remote_copy(
            src_ref=src, dst_ref=dst, send_sem=ss, recv_sem=rs,
            device_id=(to, me), device_id_type=MESH,
        )

    greet(n_dp, n_mp, me_dp, me)

    send1 = [across_mp(j, sin, slot1.at[j], s1s.at[j], s1r.at[j]) for j in range(1, n_mp)]
    send2 = [across_dp(j, ssum, slot2.at[j], s2s.at[j], s2r.at[j]) for j in range(1, n_dp)]
    for c in send1:
        c.start()

    def hidden(way, step, k):
        shard = me - step if way == 0 else me + step
        to = me + 1 if way == 0 else me - 1
        shard, to = jnp.clip(shard, 0, n_mp - 1), jnp.clip(to, 0, n_mp - 1)
        rows = pl.ds(k * piece, piece)
        src = x.at[rows, :] if step == 0 else hid.at[shard, rows, :]
        return pltpu.make_async_remote_copy(
            src_ref=src, dst_ref=hid.at[shard, rows, :],
            send_sem=hs_sem.at[way, step, k], recv_sem=hr_sem.at[way, step, k],
            device_id=(me_dp, to), device_id_type=MESH,
        )

    def sends(way, step):
        if way == 0:
            return (me >= step) & (me < n_mp - 1)
        return (me + step <= n_mp - 1) & (me > 0)

    def receives(way, step):
        return me - 1 - step >= 0 if way == 0 else me + 1 + step <= n_mp - 1

    def send_hidden(step, k):
        for way in range(2):

            @pl.when(sends(way, step))
            def _():
                hidden(way, step, k).start()

    def wait_hidden(step, k):
        for way in range(2):

            @pl.when(receives(way, step))
            def _():
                hidden(way, step, k).wait_recv()

    n_q = n_dp // 2
    me_q, me_c = me_dp // 2, lax.rem(me_dp, 2)
    square = n_q == 4
    halves = ((3, 2), (0, 1))

    def unit_rank(level):
        if level == 0:
            return me
        step, way = (level - 1) // 2, (level - 1) % 2
        return jnp.clip(me - 1 - step if way == 0 else me + 1 + step, 0, n_mp - 1)

    def here(level):
        return True if level == 0 else receives((level - 1) % 2, (level - 1) // 2)

    def mate(j):
        if not square:
            return lax.rem(me_q + j, n_q)
        x1, y1 = lax.rem(me_q, 2), me_q // 2
        x2 = 1 - x1 if j % 2 else x1
        y2 = 1 - y1 if j // 2 else y1
        return 2 * y2 + x2

    def weight_z(way, step, m):
        level = 0 if step == 0 else 1 + 2 * (step - 1) + way
        r = unit_rank(level)
        to = jnp.clip(me + 1 if way == 0 else me - 1, 0, n_mp - 1)
        dst = wall.at[m, r, me_q, me_c]
        src = pack.at[m] if step == 0 else dst
        return pltpu.make_async_remote_copy(
            src_ref=src, dst_ref=dst,
            send_sem=wzs.at[way, step, m], recv_sem=wzr.at[way, step, m],
            device_id=(me_dp, to), device_id_type=MESH,
        )

    def weight_q(level, m, slot):
        r = unit_rank(level)
        j, what = (slot, 0) if slot else ((1, 2) if m % 2 else (2, 1))
        dst = wall.at[m, r, mate(what), me_c]
        src = pack.at[m] if level == 0 and slot else dst
        return pltpu.make_async_remote_copy(
            src_ref=src, dst_ref=dst,
            send_sem=wqs.at[level, m, slot], recv_sem=wqr.at[level, m, slot],
            device_id=(mate(j) * 2 + me_c, me), device_id_type=MESH,
        )

    def weight_p(level, half, j):
        part = pl.ds(min(halves[half]), 2)
        dst = wall.at[part, unit_rank(level), mate(j), me_c]
        src = pack.at[part] if level == 0 and j == 0 else dst
        return pltpu.make_async_remote_copy(
            src_ref=src, dst_ref=dst,
            send_sem=wps.at[level, half, j], recv_sem=wpr.at[level, half, j],
            device_id=(me_q * 2 + 1 - me_c, me), device_id_type=MESH,
        )

    near = (1, 2) if square else tuple(range(1, n_q))
    slots = ((0,) if square else ()) + near

    def weight_on(way, step, m):
        @pl.when(sends(way, step))
        def _():
            weight_z(way, step, m).start()

    def weight_stage(level, stage, half):
        step, way = (level - 1) // 2, (level - 1) % 2

        def run():
            for m in halves[half]:
                if stage == 0:
                    if level > 0:
                        weight_z(way, step, m).wait_recv()
                        if 0 < step < n_mp - 2:
                            weight_on(way, step + 1, m)
                    for j in near:
                        weight_q(level, m, j).start()
                elif stage == 1:
                    if square:
                        weight_q(level, m, 2 if m % 2 else 1).wait_recv()
                        weight_q(level, m, 0).start()
                        weight_q(level, m, 1 if m % 2 else 2).wait_recv()
                    else:
                        for j in near:
                            weight_q(level, m, j).wait_recv()
                elif stage == 2 and square:
                    weight_q(level, m, 0).wait_recv()
                elif stage == 4:
                    for j in slots:
                        weight_q(level, m, j).wait_send()
            if stage == 0:
                weight_p(level, half, 0).start()
            elif stage == 1:
                for j in near:
                    weight_p(level, half, j).start()
            elif stage == 2 and square:
                weight_p(level, half, 3).start()
            elif stage == 3:
                for j in range(n_q):
                    weight_p(level, half, j).wait_recv()
            elif stage == 4:
                for j in range(n_q):
                    weight_p(level, half, j).wait_send()

        if level == 0:
            run()
        else:
            pl.when(here(level))(run)

    def both_ways(step, stage, half):
        for way in range(2):
            weight_stage(1 + 2 * step + way, stage, half)

    for k in range(PIECES):
        send_hidden(0, k)
    for half in range(2):
        for m in halves[half]:
            for way in range(2):
                weight_on(way, 0, m)
        weight_stage(0, 0, half)
    keep = pltpu.make_async_copy(pack, wall.at[:, me, me_q, me_c], local_sem.at[0])
    keep.start()

    width = dist.shape[1]
    base = width - LONGEST
    i = lax.broadcasted_iota(jnp.int32, (QB, width), 0)
    j = lax.broadcasted_iota(jnp.int32, (QB, width), 1)
    dist[...] = jnp.abs(i + base - j).astype(F32)

    total = sin[...]
    for c in send1:
        c.wait_recv()
    for j in range(1, n_mp):
        total += slot1[j]
    ssum[...] = total
    for c in send2:
        c.start()

    for k in range(PIECES):
        wait_hidden(0, k)
        send_hidden(1, k)

    for stage in range(1, 4):
        weight_stage(0, stage, 0)
        if stage == 1:
            weight_stage(0, 1, 1)
    keep.wait()
    fetch = pltpu.make_async_copy(wall.at[3, me], wslot, local_sem.at[1])
    fetch.start()

    for c in send2:
        c.wait_recv()
    total = ssum[...]
    for j in range(1, n_dp):
        total += slot2[j]
    small[...] = total
    bias[...] = jnp.zeros_like(bias)
    for r in range(n_mp):

        @pl.when(me == r)
        def _():
            bias[0:2, :] = total[0:2, r * cols : (r + 1) * cols]

    fetch.wait()
    for j in range(n_dp):
        for s in range(3):
            part = wslot[j // 2, j % 2, :, s * cols : (s + 1) * cols]
            wf[s, j * wrows : (j + 1) * wrows, :] = part.astype(F32)
    for s in range(3):
        wb[s] = wf[s].astype(BF)

    one = jnp.where(lax.broadcasted_iota(jnp.int32, (QB, HEAD), 1) == 0, 1.0, 0.0)
    minus = jnp.where(lax.broadcasted_iota(jnp.int32, (HEAD, QB), 0) < 2, -1.0, 0.0)
    none = jnp.zeros((QB, HEAD), F32)

    def project(ref, shard):
        def part(c, _):
            rows = pl.ds(pl.multiple_of(c * QB, QB), QB)
            at = pl.ds(pl.multiple_of(shard * own + c * QB, QB), QB)
            xc = ref[rows, :]
            xt[:, at] = xc.astype(F32).T.astype(BF)
            q = (dot(xc, wb[0]) + bias[0:1, :]).astype(BF).astype(F32) * HEAD**-0.5
            qs[at, :] = q.astype(BF)
            qt[:, at] = q.T.astype(BF)
            k = dot(xc, wb[1])
            kt[:, at] = k.T.astype(BF)
            v = dot(xc, wb[2]) + bias[1:2, :]
            vt = v.T
            for h in range(heads):
                hs = slice(h * HEAD, (h + 1) * HEAD)
                kp[h, at, :] = jnp.concatenate([k[:, hs], none], axis=1).astype(BF)
                vext[h, at, :] = jnp.concatenate([v[:, hs], one], axis=1).astype(BF)
                vte[h, :, at] = jnp.concatenate([vt[hs], minus], axis=0).astype(BF)
            return 0

        lax.fori_loop(0, own // QB, part, 0)

    project(x, me)
    for half in range(2):
        both_ways(0, 0, half)
    for step in range(n_mp - 1):
        if step > 0:
            for k in range(PIECES):
                wait_hidden(step, k)
                if step < n_mp - 2:
                    send_hidden(step + 1, k)
        if step == n_mp - 2:
            for way in range(2):

                @pl.when(sends(way, step))
                def _():
                    for k in range(PIECES):
                        hidden(way, step, k).wait_send()

                for half in range(2):
                    for m in halves[half]:
                        weight_on(way, 1, m)

        for way in range(2):

            @pl.when(receives(way, step))
            def _():
                shard = me - 1 - step if way == 0 else me + 1 + step
                shard = jnp.clip(shard, 0, n_mp - 1)
                project(hid.at[shard], shard)

        if step == 1:
            weight_stage(0, 2, 1)
            for half in range(2):
                both_ways(0, 1, half)

    early = [
        pltpu.make_async_copy(a, b, early_sem.at[i])
        for i, (a, b) in enumerate(((xt, xt_out), (qt, qt_out), (kp, kp_out), (vte, vte_out)))
    ]
    for c in early:
        c.start()

    def score_block(h, c, place, rows, sl):
        hs = slice(h * HEAD, (h + 1) * HEAD)
        row = c * own + place
        at = pl.ds(pl.multiple_of(row, 128), rows)
        s = dot(qs[at, hs], kt[hs, :LONGEST])
        off = pl.multiple_of(base - row, 128)
        s = s - sl * dist[:rows, pl.ds(off, LONGEST)]
        m = jnp.max(s, axis=1, keepdims=True)
        pb = jnp.exp(s - m).astype(BF)
        pbuf[h, at, :] = pb
        finish(h, c, place, at, rows, dot(pb, vext[h, :LONGEST, :]))

    def finish(h, c, place, at, rows, uu):
        uut = uu.T
        ut[h, :, at] = uut
        oh = uut[:HEAD] * (1.0 / uut[HEAD : HEAD + 1])
        obuf[c, h * HEAD : (h + 1) * HEAD, pl.ds(place, rows)] = oh.astype(BF)

    def short_block(h, c, sl):
        hs = slice(h * HEAD, (h + 1) * HEAD)
        s = dot(qs[LONGEST:, hs], kt[hs, LONGEST:])
        ii = lax.broadcasted_iota(jnp.int32, (tail, tail), 0)
        jj = lax.broadcasted_iota(jnp.int32, (tail, tail), 1)
        s = s - sl * jnp.abs(ii - jj).astype(F32)
        cut = length[0, 1]
        s = jnp.where((ii < cut) == (jj < cut), s, -1e30)
        m = jnp.max(s, axis=1, keepdims=True)
        pb = jnp.exp(s - m).astype(BF)
        p2[h] = pb
        finish(h, c, rest, pl.ds(LONGEST, tail), tail, dot(pb, vext[h, LONGEST:, :]))

    def out_copy(h, j):
        to = lax.rem(me + j, n_mp)
        hs = pl.ds(h * HEAD, HEAD)
        return pltpu.make_async_remote_copy(
            src_ref=obuf.at[to, hs, :], dst_ref=land.at[j, hs, :],
            send_sem=os_sem.at[h, j], recv_sem=or_sem.at[h, j],
            device_id=(me_dp, to), device_id_type=MESH,
        )

    def late(what, h):
        a, b = ((ut, ut_out), (p2, p2_out))[what]
        return pltpu.make_async_copy(a.at[h], b.at[h], late_sem.at[what, h])

    def keep_p(h, c, act):
        @pl.when(c < full)
        def _():
            rows = pl.ds(pl.multiple_of(c * own, own), own)
            act(pltpu.make_async_copy(pbuf.at[h, rows], p.at[h, rows], psem.at[h, c]))

        @pl.when(c == full)
        def _():
            rows = pl.ds(full * own, rest)
            act(pltpu.make_async_copy(pbuf.at[h, rows], p.at[h, rows], psem.at[h, c]))

    pump = [
        (1, 0, 2, 0), (1, 0, 2, 1), (3, 1, 0, 0), (5, 1, 0, 1), (8, 1, 1, 0), (9, 2, 0, 0),
        (10, 1, 1, 1), (11, 1, 2, 0),
    ]
    for h in range(heads):
        sl = slope[h]

        def chunk(j, _):
            c = lax.rem(me + 1 + j, n_mp)

            @pl.when(c < full)
            def _():
                for half in range(own // QB):
                    score_block(h, c, half * QB, QB, sl)

            @pl.when(c == full)
            def _():
                score_block(h, c, 0, rest, sl)
                short_block(h, c, sl)

            keep_p(h, c, lambda copy: copy.start())

            @pl.when(j < n_mp - 1)
            def _():
                out_copy(h, j + 1).start()

            for when, step, stage, half in pump:
                if when // n_mp == h:

                    @pl.when(j == when % n_mp)
                    def _():
                        both_ways(step, stage, half)

            return 0

        lax.fori_loop(0, n_mp, chunk, 0)
        late(0, h).start()
        late(1, h).start()

    for step, stage, half in ((1, 2, 1), (2, 0, 1), (2, 1, 0), (2, 2, 0), (2, 1, 1), (2, 2, 1)):
        both_ways(step, stage, half)
    attnt[me] = obuf[me]
    for h in range(heads):
        hs = slice(h * HEAD, (h + 1) * HEAD)
        for j in range(1, n_mp):
            out_copy(h, j).wait_recv()
            attnt[lax.rem(me - j + n_mp, n_mp), hs, :] = land[j, hs, :]
    for h in range(heads):
        for j in range(1, n_mp):
            out_copy(h, j).wait_send()
        for c in range(n_mp):
            keep_p(h, c, lambda copy: copy.wait())
        late(0, h).wait()
        late(1, h).wait()
    for c in early:
        c.wait()
    for c in send1 + send2:
        c.wait_send()
    for step in range(n_mp - 1):
        for way in range(2):

            @pl.when(sends(way, step))
            def _():
                if step < n_mp - 2:
                    for k in range(PIECES):
                        hidden(way, step, k).wait_send()
                for m in range(4):
                    weight_z(way, step, m).wait_send()

    weight_stage(0, 3, 1)
    for half in range(2):
        weight_stage(0, 4, half)
        for step in range(n_mp - 1):
            both_ways(step, 3, half)
            both_ways(step, 4, half)


def back(
    n_dp, n_mp,
    gt, xt, qt, kp, vte, ut, p, p2, weights, dsum1, sin, gw, gwo,
    grad_in, gq, small, gff, gout,
    gl, pbuf, dkt, dvt, dbuf, dland, wfull, gbuf, qland, ssum, slot1, slot2,
    pair, cland, xland, zsum, zland, opair, ocland, oxland, ozsum, ozland,
    gs_sem, gr_sem, qs_sem, qr_sem, ds_sem, dr_sem, ws_sem, wr_sem, s1s, s1r, s2s, s2r,
    psem, wsem, ls_sem, cs_sem, cr_sem, xs_sem, xr_sem, zs_sem, zr_sem,
):
    me_dp, me = lax.axis_index("dp"), lax.axis_index("mp")
    own = gt.shape[2]
    cols = gt.shape[1]
    heads = cols // HEAD
    group = own * n_mp
    tail = group - LONGEST
    full = LONGEST // own
    rest = LONGEST - full * own
    wrows = gq.shape[0]

    def across_mp(j, src, dst, ss, rs):
        to = lax.rem(me + j, n_mp)
        return pltpu.make_async_remote_copy(
            src_ref=src, dst_ref=dst, send_sem=ss, recv_sem=rs,
            device_id=(me_dp, to), device_id_type=MESH,
        )

    def across_dp(j, src, dst, ss, rs):
        to = lax.rem(me_dp + j, n_dp)
        return pltpu.make_async_remote_copy(
            src_ref=src, dst_ref=dst, send_sem=ss, recv_sem=rs,
            device_id=(to, me), device_id_type=MESH,
        )

    def fetch_p(h, j, act):
        c = lax.rem(me - j + n_mp, n_mp)
        slot = lax.rem(h * n_mp + j, 2)

        @pl.when(c < full)
        def _():
            rows = pl.ds(pl.multiple_of(c * own, own), own)
            act(pltpu.make_async_copy(p.at[h, rows, :], pbuf.at[slot], psem.at[slot]))

        @pl.when(c == full)
        def _():
            src = p.at[h, pl.ds(full * own, rest), :]
            act(pltpu.make_async_copy(src, pbuf.at[slot, pl.ds(0, rest), :], psem.at[slot]))

    start, wait = lambda copy: copy.start(), lambda copy: copy.wait()
    fetch_p(0, 0, start)
    fetch_w = pltpu.make_async_copy(weights.at[3], wfull, wsem)

    n_q = n_dp // 2
    me_q, me_c = me_dp // 2, lax.rem(me_dp, 2)
    other = me_dp + 1 - 2 * me_c
    kinds = ((gw, pair, cland, xland, zsum, zland), (gwo, opair, ocland, oxland, ozsum, ozland))

    def rank_of(o):
        return lax.rem(me + 1 + o, n_mp)

    def load_copy(o, t):
        src, own_part = kinds[t][:2]
        return pltpu.make_async_copy(
            src.at[rank_of(o), :, :, me_c], own_part.at[o], ls_sem.at[o, t]
        )

    def pair_up(o, t):
        src, land = kinds[t][0], kinds[t][2]
        return pltpu.make_async_remote_copy(
            src_ref=src.at[rank_of(o), :, :, 1 - me_c], dst_ref=land.at[o],
            send_sem=cs_sem.at[o, t], recv_sem=cr_sem.at[o, t],
            device_id=(other, me), device_id_type=MESH,
        )

    def cross(o, j, t):
        src, land = kinds[t][1], kinds[t][3]
        to = lax.rem(me_q + j, n_q)
        return pltpu.make_async_remote_copy(
            src_ref=src.at[o, :, to], dst_ref=land.at[o, j - 1],
            send_sem=xs_sem.at[o, j, t], recv_sem=xr_sem.at[o, j, t],
            device_id=(to * 2 + me_c, me), device_id_type=MESH,
        )

    def along(o, t):
        src, land = kinds[t][4:]
        return pltpu.make_async_remote_copy(
            src_ref=src.at[o], dst_ref=land.at[o],
            send_sem=zs_sem.at[o, t], recv_sem=zr_sem.at[o, t],
            device_id=(me_dp, rank_of(o)), device_id_type=MESH,
        )

    def add_pair(o):
        for t in range(2):
            own_part, land = kinds[t][1], kinds[t][2]
            load_copy(o, t).wait()
            pair_up(o, t).wait_recv()
            mats = own_part.shape[1]

            def add(i, _):
                a = own_part[o, i // n_q, lax.rem(i, n_q)].astype(F32)
                b = land[o, i // n_q, lax.rem(i, n_q)].astype(F32)
                own_part[o, i // n_q, lax.rem(i, n_q)] = (a + b).astype(BF)
                return 0

            lax.fori_loop(0, mats * n_q, add, 0)
            for j in range(1, n_q):
                cross(o, j, t).start()

    def add_cross(o):
        for t in range(2):
            own_part, land, total = kinds[t][1], kinds[t][3], kinds[t][4]
            for j in range(1, n_q):
                cross(o, j, t).wait_recv()
            for m in range(own_part.shape[1]):
                a = own_part[o, m, me_q].astype(F32)
                for j in range(1, n_q):
                    a += land[o, j - 1, m].astype(F32)
                total[o, m] = a.astype(BF)
            if o < n_mp - 1:
                along(o, t).start()

    for o in range(n_mp):
        for t in range(2):
            load_copy(o, t).start()

    greet(n_dp, n_mp, me_dp, me)

    def grad_copy(h, j):
        hs = pl.ds(h * HEAD, HEAD)
        to = lax.rem(me + j, n_mp)
        return across_mp(
            j, gt.at[to, hs, :], gl.at[j, hs, :], gs_sem.at[h, j], gr_sem.at[h, j]
        )

    for h in range(heads):
        for j in range(1, n_mp):
            grad_copy(h, j).start()
    for o in range(n_mp):
        for t in range(2):
            pair_up(o, t).start()
    fetch_w.start()
    gl[0] = gt[me]

    def query_copy(h, j):
        to = lax.rem(me - j + n_mp, n_mp)
        hs = pl.ds(h * HEAD, HEAD)
        return pltpu.make_async_remote_copy(
            src_ref=dbuf.at[to, 0, hs, :], dst_ref=dland.at[j, 0, hs, :],
            send_sem=qs_sem.at[h, j], recv_sem=qr_sem.at[h, j],
            device_id=(me_dp, to), device_id_type=MESH,
        )

    def pair_copy(h, j):
        to = lax.rem(me - j + n_mp, n_mp)
        hs = pl.ds(h * HEAD, HEAD)
        return pltpu.make_async_remote_copy(
            src_ref=dbuf.at[to, pl.ds(1, 2), hs, :], dst_ref=dland.at[j, pl.ds(1, 2), hs, :],
            send_sem=ds_sem.at[h, j], recv_sem=dr_sem.at[h, j],
            device_id=(me_dp, to), device_id_type=MESH,
        )

    def block(h, j, c, place, rows, pb, keys, add):
        row = c * own + place
        at = pl.ds(pl.multiple_of(row, 128), rows)
        hs = slice(h * HEAD, (h + 1) * HEAD)
        uu = ut[h, :, at]
        inv = 1.0 / uu[HEAD : HEAD + 1]
        gg = gl[j, hs, pl.ds(place, rows)].astype(F32) * inv
        total = jnp.sum(gg * uu[:HEAD], axis=0, keepdims=True) * inv
        high = total.astype(BF).astype(F32)
        low = total - high
        index = lax.broadcasted_iota(jnp.int32, (HEAD, rows), 0)
        extra = jnp.where(index == 0, high, jnp.where(index == 1, low, 0.0))
        gext = jnp.concatenate([gg, extra], axis=0).T.astype(BF)
        dp = dot(gext, vte[h, :, keys])
        ds = (pb.astype(F32) * dp).astype(BF)
        dq = dot(ds, kp[h, keys, :]).T[:HEAD] * (HEAD**-0.5)
        dbuf[c, 0, hs, pl.ds(place, rows)] = dq.astype(BF)
        dk = dot(qt[hs, at], ds)
        dv = dot(gg.astype(BF), pb)
        if add:
            dkt[:, keys] = dkt[:, keys] + dk
            dvt[:, keys] = dvt[:, keys] + dv
        else:
            dkt[:, keys] = dk
            dvt[:, keys] = dv

    pump = [1 + o for o in range(n_mp)]
    for h in range(heads):
        hs = slice(h * HEAD, (h + 1) * HEAD)
        dkt[:, :LONGEST] = jnp.zeros((HEAD, LONGEST), F32)
        dvt[:, :LONGEST] = jnp.zeros((HEAD, LONGEST), F32)

        def chunk(j, _):
            c = lax.rem(me - j + n_mp, n_mp)
            slot = lax.rem(h * n_mp + j, 2)

            @pl.when(j < n_mp - 1)
            def _():
                fetch_p(h, j + 1, start)

            if h < heads - 1:

                @pl.when(j == n_mp - 1)
                def _():
                    fetch_p(h + 1, 0, start)

            @pl.when(j > 0)
            def _():
                grad_copy(h, j).wait_recv()

            fetch_p(h, j, wait)

            keys = slice(0, LONGEST)

            @pl.when(c < full)
            def _():
                for half in range(own // QB):
                    at = pl.ds(half * QB, QB)
                    block(h, j, c, half * QB, QB, pbuf[slot, at, :], keys, True)

            @pl.when(c == full)
            def _():
                block(h, j, c, 0, rest, pbuf[slot, :rest, :], keys, True)
                block(h, j, c, rest, tail, p2[h], slice(LONGEST, group), False)

            @pl.when(j > 0)
            def _():
                query_copy(h, j).start()

            for o in range(n_mp):
                if pump[o] // n_mp == h:

                    @pl.when(j == pump[o] % n_mp)
                    def _():
                        add_pair(o)

            return 0

        lax.fori_loop(0, n_mp, chunk, 0)
        if h == heads - 1:
            add_cross(0)
        for c in range(n_mp):
            dbuf[c, 1, hs, :] = dkt[:, c * own : (c + 1) * own].astype(BF)
            dbuf[c, 2, hs, :] = dvt[:, c * own : (c + 1) * own].astype(BF)
        for j in range(1, n_mp):
            pair_copy(h, j).start()

    ones = jnp.ones((8, own), BF)
    sq = jnp.zeros((8, cols), F32)
    sv = jnp.zeros((8, cols), F32)
    for c in range(n_mp):
        sq += dot_nt(ones, dbuf[c, 0])
        sv += dot_nt(ones, dbuf[c, 2])
    ssum[...] = sin[...]
    for r in range(n_mp):

        @pl.when(me == r)
        def _():
            ssum[0:1, r * cols : (r + 1) * cols] = sq[0:1]
            ssum[1:2, r * cols : (r + 1) * cols] = sv[0:1]

    send1 = [across_mp(j, ssum, slot1.at[j], s1s.at[j], s1r.at[j]) for j in range(1, n_mp)]
    for c in send1:
        c.start()

    total = jnp.zeros((xt.shape[0], 3 * cols), F32)
    for c in range(n_mp):
        total += dot_nt(xt[:, c * own : (c + 1) * own], dbuf[c].reshape(3 * cols, own))
    for d in range(n_dp):
        gbuf[d] = total[d * wrows : (d + 1) * wrows].astype(BF)

    def weight_copy(j):
        to = lax.rem(me_dp + j, n_dp)
        return across_dp(j, gbuf.at[to], qland.at[j], ws_sem.at[j], wr_sem.at[j])

    for j in range(1, n_dp):
        weight_copy(j).start()

    add_cross(1)
    for c in send1:
        c.wait_send()
        c.wait_recv()
    total = ssum[...]
    for j in range(1, n_mp):
        total += slot1[j]
    ssum[...] = total
    send2 = [across_dp(j, ssum, slot2.at[j], s2s.at[j], s2r.at[j]) for j in range(1, n_dp)]
    for c in send2:
        c.start()

    fetch_w.wait()
    into = dot(wfull[me, :, : 3 * cols], dbuf[me].reshape(3 * cols, own))
    for j in range(1, n_mp):
        for h in range(heads):
            query_copy(h, j).wait_recv()
            pair_copy(h, j).wait_recv()
        r = lax.rem(me + j, n_mp)
        into += dot(wfull[r, :, : 3 * cols], dland[j].reshape(3 * cols, own))
    grad_in[...] = (dsum1[...] + into.T).astype(BF)

    for o in range(2, n_mp):
        add_cross(o)
    total = gbuf[me_dp].astype(F32)
    for j in range(1, n_dp):
        weight_copy(j).wait_recv()
        total += qland[j].astype(F32)
    gq[...] = total
    total = ssum[...]
    for c in send2:
        c.wait_recv()
    for j in range(1, n_dp):
        total += slot2[j]
    small[...] = total
    for t, out in ((0, gff), (1, gout)):
        total, land = kinds[t][4:]
        for o in range(n_mp - 1):
            along(o, t).wait_recv()
        for m in range(out.shape[0]):
            a = total[n_mp - 1, m].astype(F32)
            for o in range(n_mp - 1):
                a += land[o, m].astype(F32)
            out[m] = a
    for t in range(2):
        for o in range(n_mp):
            pair_up(o, t).wait_send()
            for j in range(1, n_q):
                cross(o, j, t).wait_send()
            if o < n_mp - 1:
                along(o, t).wait_send()
    for c in send2:
        c.wait_send()
    for j in range(1, n_dp):
        weight_copy(j).wait_send()
    for h in range(heads):
        for j in range(1, n_mp):
            grad_copy(h, j).wait_send()
            query_copy(h, j).wait_send()
            pair_copy(h, j).wait_send()


def norm_parts(r):
    centre = r - jnp.mean(r, axis=-1, keepdims=True)
    spread = jnp.mean(centre * centre, axis=-1, keepdims=True)
    rstd = lax.rsqrt(spread + 1e-05)
    return centre * rstd, rstd


def norm_back(dn, n, rstd):
    return rstd * (
        dn - jnp.mean(dn, axis=-1, keepdims=True) - n * jnp.mean(dn * n, axis=-1, keepdims=True)
    )


def colsum(a):
    return jnp.sum(a, axis=0, keepdims=True)


def flip(a):
    return a.astype(F32).T.astype(BF)


GELU_C = 0.7978845608
GELU_A = 0.044715


def middle(
    attn, x, cot, wlast, small, w,
    result, dsum1, dattn, gw, gwout, gsmall,
    wout, mid, midb, midt, gate, up, y, dffn, dffnt, dmid,
):
    i = pl.program_id(0)
    n = pl.num_programs(0) // 2
    parts, cols = attn.shape[0], attn.shape[1]

    @pl.when(i == 0)
    def _():
        branch = jnp.zeros((x.shape[1], x.shape[0]), F32)
        for r in range(parts):
            wout[r] = wlast[0, r, :, 3 * cols :]
            branch += dot(wout[r], attn[r])
        branch = branch.T + x[...].astype(F32) + small[2:3, :]
        nn, _ = norm_parts(branch)
        m = nn * small[3:4, :] + small[4:5, :]
        dsum1[...] = branch
        mid[...] = m
        midb[...] = m.astype(BF)
        midt[...] = m.T.astype(BF)
        y[...] = jnp.zeros_like(y)

    @pl.when(i < n)
    def _():
        mb = midb[...]
        ga = dot(mb, w[0, 0]) + small[pl.ds(8 + i, 1), :]
        u = dot(mb, w[1, 0]) + small[pl.ds(8 + n + i, 1), :]
        gate[i] = ga
        up[i] = u
        t = jnp.tanh(GELU_C * (ga + GELU_A * ga * ga * ga))
        act = (0.5 * ga * (1.0 + t) * u).astype(BF)
        y[...] += dot_nt(act, w[2, 0])

    @pl.when(i == n - 1)
    def _():
        r = mid[...] + y[...] + small[5:6, :]
        nn, rstd = norm_parts(r)
        gain = small[6:7, :]
        result[...] = (nn * gain + small[7:8, :]).astype(BF)
        c = cot[...].astype(F32)
        ds = norm_back(c * gain, nn, rstd)
        gsmall[6:7, :] = colsum(c * nn)
        gsmall[7:8, :] = colsum(c)
        dmid[...] = ds
        db = ds.astype(BF)
        dffn[...] = db
        dffnt[...] = ds.T.astype(BF)
        gsmall[5:6, :] = colsum(db.astype(F32))
        gsmall[0:2, :] = jnp.zeros_like(gsmall[0:2, :])

    @pl.when(i >= n)
    def _():
        k = 2 * n - 1 - i
        ga = gate[k]
        u = up[k]
        sq = ga * ga
        t = jnp.tanh(GELU_C * (ga + GELU_A * ga * sq))
        half = 0.5 * (1.0 + t)
        gelu = ga * half
        slope = half + (0.5 * GELU_C) * ga * (1.0 - t * t) * (1.0 + 3.0 * GELU_A * sq)
        act = (gelu * u).astype(BF)
        dact = dot(dffn[...], w[2, 0])
        gw[0, 2] = dot(dffnt[...], act).astype(BF)
        dga = (dact * u * slope).astype(BF)
        du = (dact * gelu).astype(BF)
        gsmall[pl.ds(8 + k, 1), :] = colsum(dga.astype(F32))
        gsmall[pl.ds(8 + n + k, 1), :] = colsum(du.astype(F32))
        gw[0, 0] = dot(midt[...], dga).astype(BF)
        gw[0, 1] = dot(midt[...], du).astype(BF)
        dmid[...] += dot_nt(dga, w[0, 0]) + dot_nt(du, w[1, 0])

    @pl.when(i == 2 * n - 1)
    def _():
        nn, rstd = norm_parts(dsum1[...])
        dm = dmid[...]
        gsmall[3:4, :] = colsum(dm * nn)
        gsmall[4:5, :] = colsum(dm)
        ds = norm_back(dm * small[3:4, :], nn, rstd)
        dsum1[...] = ds
        db = ds.astype(BF)
        gsmall[2:3, :] = colsum(db.astype(F32))
        dbt = ds.T.astype(BF)
        for r in range(parts):
            dattn[r] = dot(db, wout[r]).T.astype(BF)
            gwout[r] = dot_nt(dbt, attn[r]).astype(BF)


def head_slopes(first_head, head_count):
    number = first_head + jnp.arange(head_count, dtype=jnp.int32)
    exponent = jnp.where(number < 8, number.astype(F32) + 1.0, number.astype(F32) - 7.5)
    return jnp.exp2(-exponent)


def cost(flops):
    return pl.CostEstimate(flops=flops, bytes_accessed=1 << 24, transcendentals=0)


def params(**kw):
    return pltpu.CompilerParams(vmem_limit_bytes=VMEM_LIMIT, **kw)


def per_device(
    hidden_in, lengths, w_qkv, b_qv, w_out, b_out, ln1_gain, ln1_bias, w_gu, b_gu, w_down,
    b_down, ln2_gain, ln2_bias, cotangent,
):
    both = ("dp", "mp")
    n_dp, n_mp = lax.axis_size("dp"), lax.axis_size("mp")
    n = n_dp * n_mp
    mp_rank = lax.axis_index("mp")
    own, width = hidden_in.shape
    group = own * n_mp
    sds = jax.ShapeDtypeStruct

    dev = lax.axis_index("dp") * n_mp + mp_rank

    def placed(a):
        zero = jnp.zeros((a.shape[0], a.shape[1] * n), F32)
        return lax.dynamic_update_slice_in_dim(zero, a, dev * a.shape[1], 1)

    vectors = jnp.stack([b_out, ln1_gain, ln1_bias, b_down, ln2_gain, ln2_bias])
    vectors = jnp.concatenate([b_qv, vectors], axis=0)
    small_own = jnp.concatenate(
        [placed(vectors), placed(b_gu).reshape(-1, width)], axis=0
    )
    srows = small_own.shape[0]

    wq = w_qkv.astype(BF)
    wrows, cols = wq.shape[1], wq.shape[2]
    ff_part = w_gu.shape[2]
    heads = cols // HEAD
    tail = group - LONGEST

    attn_pack = jnp.concatenate([wq[0], wq[1], wq[2], w_out.T.astype(BF)], axis=1)
    pack = jnp.concatenate([w_gu.astype(BF), w_down.T.astype(BF)[None], attn_pack[None]], axis=0)
    n_q = n_dp // 2
    units = 2 * n_mp - 1

    slopes = head_slopes(mp_rank * heads, heads)
    dma = pltpu.SemaphoreType.DMA

    small, xt, qt, kp, vte, ut, attn, p, p2, weights = pl.pallas_call(
        functools.partial(front, n_dp, n_mp),
        out_shape=(
            sds((srows, width), F32),
            sds((width, group), BF),
            sds((cols, group), BF),
            sds((heads, group, 2 * HEAD), BF),
            sds((heads, 2 * HEAD, group), BF),
            sds((heads, 2 * HEAD, group), F32),
            sds((n_mp, cols, own), BF),
            sds((heads, LONGEST, LONGEST), BF),
            sds((heads, tail, tail), BF),
            sds((4, n_mp, n_q, 2, wrows, ff_part), BF),
        ),
        in_specs=[vmem(), vmem(), vmem(), smem(), smem()],
        out_specs=(
            vmem(), hbm(), hbm(), hbm(), hbm(), hbm(), vmem(), hbm(), hbm(), hbm(),
        ),
        scratch_shapes=[
            pltpu.VMEM((width, group), BF),
            pltpu.VMEM((cols, group), BF),
            pltpu.VMEM((heads, group, 2 * HEAD), BF),
            pltpu.VMEM((heads, 2 * HEAD, group), BF),
            pltpu.VMEM((heads, 2 * HEAD, group), F32),
            pltpu.VMEM((heads, tail, tail), BF),
            pltpu.VMEM((n_mp, own, width), BF),
            pltpu.VMEM((n_q, 2, wrows, ff_part), BF),
            pltpu.VMEM((3, width, cols), F32),
            pltpu.VMEM((3, width, cols), BF),
            pltpu.VMEM((n_mp, srows, width), F32),
            pltpu.VMEM((srows, width), F32),
            pltpu.VMEM((n_dp, srows, width), F32),
            pltpu.VMEM((8, cols), F32),
            pltpu.VMEM((group, cols), BF),
            pltpu.VMEM((cols, group), BF),
            pltpu.VMEM((heads, group, 2 * HEAD), BF),
            pltpu.VMEM((QB, LONGEST + LONGEST // QB * QB), F32),
            pltpu.VMEM((heads, LONGEST, LONGEST), BF),
            pltpu.VMEM((n_mp, cols, own), BF),
            pltpu.VMEM((n_mp, cols, own), BF),
            dma((2, n_mp - 1, PIECES)),
            dma((2, n_mp - 1, PIECES)),
            dma((n_mp,)),
            dma((n_mp,)),
            dma((n_dp,)),
            dma((n_dp,)),
            dma((heads, n_mp)),
            dma((heads, n_mp)),
            dma((heads, n_mp)),
            dma((2,)),
            dma((4,)),
            dma((2, heads)),
            dma((2, n_mp - 1, 4)),
            dma((2, n_mp - 1, 4)),
            dma((units, 4, n_q)),
            dma((units, 4, n_q)),
            dma((units, 2, n_q)),
            dma((units, 2, n_q)),
        ],
        compiler_params=params(collective_id=0, has_side_effects=True),
        cost_estimate=cost(11 * LONGEST * LONGEST * HEAD * heads * 12),
        name="front",
    )(hidden_in, pack, small_own, slopes, lengths)
    weights = weights.reshape(4, n_mp, width, ff_part)

    fixed = lambda *s: pl.BlockSpec(s, lambda i: (0,) * len(s))
    walk = lambda i: jnp.where(i < n_mp, i, 2 * n_mp - 1 - i)
    late = lambda i: jnp.where(i < n_mp, n_mp - 1, 2 * n_mp - 1 - i)
    result, dsum1, dattn, gw, gwout, gsmall = pl.pallas_call(
        middle,
        grid=(2 * n_mp,),
        out_shape=(
            sds((own, width), BF),
            sds((own, width), F32),
            sds((n_mp, cols, own), BF),
            sds((n_mp, 3, width, ff_part), BF),
            sds((n_mp, width, cols), BF),
            sds((srows, width), F32),
        ),
        in_specs=[
            fixed(n_mp, cols, own),
            fixed(own, width),
            fixed(own, width),
            pl.BlockSpec(
                (1, n_mp, width, ff_part),
                lambda i: (3, 0, 0, 0),
                pipeline_mode=pl.Buffered(1),
            ),
            fixed(srows, width),
            pl.BlockSpec((3, 1, width, ff_part), lambda i: (0, walk(i), 0, 0)),
        ],
        out_specs=(
            fixed(own, width),
            fixed(own, width),
            fixed(n_mp, cols, own),
            pl.BlockSpec((1, 3, width, ff_part), lambda i: (late(i), 0, 0, 0)),
            fixed(n_mp, width, cols),
            fixed(srows, width),
        ),
        scratch_shapes=[
            pltpu.VMEM((n_mp, width, cols), BF),
            pltpu.VMEM((own, width), F32),
            pltpu.VMEM((own, width), BF),
            pltpu.VMEM((width, own), BF),
            pltpu.VMEM((n_mp, own, ff_part), F32),
            pltpu.VMEM((n_mp, own, ff_part), F32),
            pltpu.VMEM((own, width), F32),
            pltpu.VMEM((own, width), BF),
            pltpu.VMEM((width, own), BF),
            pltpu.VMEM((own, width), F32),
        ],
        compiler_params=params(),
        name="middle",
    )(attn, hidden_in, cotangent, weights, small, weights)

    gw = gw.reshape(n_mp, 3, n_q, 2, wrows, ff_part)
    gwout = gwout.reshape(n_mp, 1, n_q, 2, wrows, cols)
    grad_in, gqkv, gsmall, gff, gout = pl.pallas_call(
        functools.partial(back, n_dp, n_mp),
        out_shape=(
            sds((own, width), BF),
            sds((wrows, 3 * cols), F32),
            sds((srows, width), F32),
            sds((3, wrows, ff_part), F32),
            sds((1, wrows, cols), F32),
        ),
        in_specs=[
            vmem(), vmem(), vmem(), vmem(), vmem(), vmem(), hbm(), vmem(), hbm(), vmem(), vmem(),
            hbm(), hbm(),
        ],
        out_specs=(vmem(), vmem(), vmem(), vmem(), vmem()),
        scratch_shapes=[
            pltpu.VMEM((n_mp, cols, own), BF),
            pltpu.VMEM((2, own, LONGEST), BF),
            pltpu.VMEM((HEAD, group), F32),
            pltpu.VMEM((HEAD, group), F32),
            pltpu.VMEM((n_mp, 3, cols, own), BF),
            pltpu.VMEM((n_mp, 3, cols, own), BF),
            pltpu.VMEM((n_mp, width, ff_part), BF),
            pltpu.VMEM((n_dp, wrows, 3 * cols), BF),
            pltpu.VMEM((n_dp, wrows, 3 * cols), BF),
            pltpu.VMEM((srows, width), F32),
            pltpu.VMEM((n_mp, srows, width), F32),
            pltpu.VMEM((n_dp, srows, width), F32),
            pltpu.VMEM((n_mp, 3, n_q, wrows, ff_part), BF),
            pltpu.VMEM((n_mp, 3, n_q, wrows, ff_part), BF),
            pltpu.VMEM((n_mp, n_q - 1, 3, wrows, ff_part), BF),
            pltpu.VMEM((n_mp, 3, wrows, ff_part), BF),
            pltpu.VMEM((n_mp - 1, 3, wrows, ff_part), BF),
            pltpu.VMEM((n_mp, 1, n_q, wrows, cols), BF),
            pltpu.VMEM((n_mp, 1, n_q, wrows, cols), BF),
            pltpu.VMEM((n_mp, n_q - 1, 1, wrows, cols), BF),
            pltpu.VMEM((n_mp, 1, wrows, cols), BF),
            pltpu.VMEM((n_mp - 1, 1, wrows, cols), BF),
            dma((heads, n_mp)),
            dma((heads, n_mp)),
            dma((heads, n_mp)),
            dma((heads, n_mp)),
            dma((heads, n_mp)),
            dma((heads, n_mp)),
            dma((n_dp,)),
            dma((n_dp,)),
            dma((n_mp,)),
            dma((n_mp,)),
            dma((n_dp,)),
            dma((n_dp,)),
            dma((2,)),
            dma,
            dma((n_mp, 2)),
            dma((n_mp, 2)),
            dma((n_mp, 2)),
            dma((n_mp, n_q, 2)),
            dma((n_mp, n_q, 2)),
            dma((n_mp - 1, 2)),
            dma((n_mp - 1, 2)),
        ],
        compiler_params=params(collective_id=1, has_side_effects=True),
        cost_estimate=cost(11 * LONGEST * LONGEST * HEAD * heads * 12),
        name="back",
    )(dattn, xt, qt, kp, vte, ut, p, p2, weights, dsum1, gsmall, gw, gwout)

    def own_columns(a):
        part = a.shape[1] // n
        return lax.dynamic_slice_in_dim(a, dev * part, part, 1)

    gs = own_columns(gsmall[:8])
    g_gu = own_columns(gsmall[8:].reshape(2, -1))
    gqkv = gqkv.reshape(wrows, 3, cols).transpose(1, 0, 2)

    return (
        result,
        grad_in,
        gqkv,
        gs[0:2],
        gout[0].T,
        gs[2],
        gs[3],
        gs[4],
        gff[:2],
        g_gu,
        gff[2].T,
        gs[5],
        gs[6],
        gs[7],
    )


def solution(mesh):
    rows = P(("dp", "mp"), None)
    vec = P(("dp", "mp"))
    vecs = P(None, ("dp", "mp"))
    wide = P(None, "dp", "mp")
    tall = P("mp", "dp")
    return jax.shard_map(
        per_device,
        mesh=mesh,
        in_specs=(
            rows, P("dp", None), wide, vecs, tall, vec, vec, vec, wide, vecs, tall, vec, vec, vec,
            rows,
        ),
        out_specs=(
            rows, rows, wide, vecs, tall, vec, vec, vec, wide, vecs, tall, vec, vec, vec,
        ),
        check_vma=False,
    )
```

```python
import functools

import jax
import jax.numpy as jnp
from jax import lax
from jax.experimental import pallas as pl
from jax.experimental.pallas import tpu as pltpu
from jax.sharding import PartitionSpec as P

HEAD = 64
LONGEST = 1664
QB = 256
BF = jnp.bfloat16
F32 = jnp.float32
VMEM_LIMIT = 60 * 1024 * 1024


def dot(a, b):
    return lax.dot_general(a, b, (((1,), (0,)), ((), ())), preferred_element_type=F32)


def dot_nt(a, b):
    return lax.dot_general(a, b, (((1,), (1,)), ((), ())), preferred_element_type=F32)


def vmem():
    return pl.BlockSpec(memory_space=pltpu.VMEM)


def smem():
    return pl.BlockSpec(memory_space=pltpu.SMEM)


def hbm():
    return pl.BlockSpec(memory_space=pl.ANY)


MESH = pl.DeviceIdType.MESH
PIECES = 4


def greet(n_dp, n_mp, me_dp, me_mp, meanwhile=lambda: None):
    barrier = pltpu.get_barrier_semaphore()
    for j in range(1, n_mp):
        pl.semaphore_signal(
            barrier, 1, device_id=(me_dp, lax.rem(me_mp + j, n_mp)), device_id_type=MESH
        )
    for j in range(1, n_dp):
        pl.semaphore_signal(
            barrier, 1, device_id=(lax.rem(me_dp + j, n_dp), me_mp), device_id_type=MESH
        )
    meanwhile()
    pl.semaphore_wait(barrier, n_mp - 1 + n_dp - 1)


def front(
    n_dp, n_mp,
    x, wqkv, wout, wgu, wdown, sin, slope, length,
    small, xt_out, qt_out, kp_out, vte_out, ut_out, attnt, p, p2_out, wall,
    pack, xt, qt, kp, vte, ut, p2, hid, wslot, wf, wb, slot1, ssum, slot2, bias, qs, kt, vext, dist, pbuf, obuf, land,
    hs_sem, hr_sem, s1s, s1r, s2s, s2r, os_sem, or_sem, psem,
    local_sem, early_sem, late_sem, wzs, wzr, wqs, wqr, wps, wpr,
):
    me_dp, me = lax.axis_index("dp"), lax.axis_index("mp")
    own = x.shape[0]
    group = own * n_mp
    wrows, cols = pack.shape[1], wb.shape[2]
    heads = cols // HEAD
    tail = group - LONGEST
    full = LONGEST // own
    rest = LONGEST - full * own
    piece = own // PIECES

    def across_mp(j, src, dst, ss, rs):
        to = lax.rem(me + j, n_mp)
        return pltpu.make_async_remote_copy(
            src_ref=src, dst_ref=dst, send_sem=ss, recv_sem=rs,
            device_id=(me_dp, to), device_id_type=MESH,
        )

    def across_dp(j, src, dst, ss, rs):
        to = lax.rem(me_dp + j, n_dp)
        return pltpu.make_async_remote_copy(
            src_ref=src, dst_ref=dst, send_sem=ss, recv_sem=rs,
            device_id=(to, me), device_id_type=MESH,
        )

    def make_pack():
        for m in range(2):
            pack[m] = wgu[m].astype(BF)
        pack[2] = wdown[...].astype(BF)
        last = [wqkv[0], wqkv[1], wqkv[2], wout[...].T]
        pack[3] = jnp.concatenate(last, axis=1).astype(BF)

    greet(n_dp, n_mp, me_dp, me, make_pack)

    send1 = [across_mp(j, sin, slot1.at[j], s1s.at[j], s1r.at[j]) for j in range(1, n_mp)]
    send2 = [across_dp(j, ssum, slot2.at[j], s2s.at[j], s2r.at[j]) for j in range(1, n_dp)]
    for c in send1:
        c.start()

    def hidden(way, step, k):
        shard = me - step if way == 0 else me + step
        to = me + 1 if way == 0 else me - 1
        shard, to = jnp.clip(shard, 0, n_mp - 1), jnp.clip(to, 0, n_mp - 1)
        rows = pl.ds(k * piece, piece)
        src = x.at[rows, :] if step == 0 else hid.at[shard, rows, :]
        return pltpu.make_async_remote_copy(
            src_ref=src, dst_ref=hid.at[shard, rows, :],
            send_sem=hs_sem.at[way, step, k], recv_sem=hr_sem.at[way, step, k],
            device_id=(me_dp, to), device_id_type=MESH,
        )

    def sends(way, step):
        if way == 0:
            return (me >= step) & (me < n_mp - 1)
        return (me + step <= n_mp - 1) & (me > 0)

    def receives(way, step):
        return me - 1 - step >= 0 if way == 0 else me + 1 + step <= n_mp - 1

    def send_hidden(step, k):
        for way in range(2):

            @pl.when(sends(way, step))
            def _():
                hidden(way, step, k).start()

    def wait_hidden(step, k):
        for way in range(2):

            @pl.when(receives(way, step))
            def _():
                hidden(way, step, k).wait_recv()

    n_q = n_dp // 2
    me_q, me_c = me_dp // 2, lax.rem(me_dp, 2)
    square = n_q == 4
    halves = ((3, 2), (0, 1))

    def unit_rank(level):
        if level == 0:
            return me
        step, way = (level - 1) // 2, (level - 1) % 2
        return jnp.clip(me - 1 - step if way == 0 else me + 1 + step, 0, n_mp - 1)

    def here(level):
        return True if level == 0 else receives((level - 1) % 2, (level - 1) // 2)

    def mate(j):
        if not square:
            return lax.rem(me_q + j, n_q)
        x1, y1 = lax.rem(me_q, 2), me_q // 2
        x2 = 1 - x1 if j % 2 else x1
        y2 = 1 - y1 if j // 2 else y1
        return 2 * y2 + x2

    def weight_z(way, step, m):
        level = 0 if step == 0 else 1 + 2 * (step - 1) + way
        r = unit_rank(level)
        to = jnp.clip(me + 1 if way == 0 else me - 1, 0, n_mp - 1)
        dst = wall.at[m, r, me_q, me_c]
        src = pack.at[m] if step == 0 else dst
        return pltpu.make_async_remote_copy(
            src_ref=src, dst_ref=dst,
            send_sem=wzs.at[way, step, m], recv_sem=wzr.at[way, step, m],
            device_id=(me_dp, to), device_id_type=MESH,
        )

    def weight_q(level, m, slot):
        r = unit_rank(level)
        j, what = (slot, 0) if slot else ((1, 2) if m % 2 else (2, 1))
        dst = wall.at[m, r, mate(what), me_c]
        src = pack.at[m] if level == 0 and slot else dst
        return pltpu.make_async_remote_copy(
            src_ref=src, dst_ref=dst,
            send_sem=wqs.at[level, m, slot], recv_sem=wqr.at[level, m, slot],
            device_id=(mate(j) * 2 + me_c, me), device_id_type=MESH,
        )

    def weight_p(level, half, j):
        part = pl.ds(min(halves[half]), 2)
        dst = wall.at[part, unit_rank(level), mate(j), me_c]
        src = pack.at[part] if level == 0 and j == 0 else dst
        return pltpu.make_async_remote_copy(
            src_ref=src, dst_ref=dst,
            send_sem=wps.at[level, half, j], recv_sem=wpr.at[level, half, j],
            device_id=(me_q * 2 + 1 - me_c, me), device_id_type=MESH,
        )

    near = (1, 2) if square else tuple(range(1, n_q))
    slots = ((0,) if square else ()) + near

    def weight_on(way, step, m):
        @pl.when(sends(way, step))
        def _():
            weight_z(way, step, m).start()

    def weight_stage(level, stage, half):
        step, way = (level - 1) // 2, (level - 1) % 2

        def run():
            for m in halves[half]:
                if stage == 0:
                    if level > 0:
                        weight_z(way, step, m).wait_recv()
                        if 0 < step < n_mp - 2:
                            weight_on(way, step + 1, m)
                    for j in near:
                        weight_q(level, m, j).start()
                elif stage == 1:
                    if square:
                        weight_q(level, m, 2 if m % 2 else 1).wait_recv()
                        weight_q(level, m, 0).start()
                        weight_q(level, m, 1 if m % 2 else 2).wait_recv()
                    else:
                        for j in near:
                            weight_q(level, m, j).wait_recv()
                elif stage == 2 and square:
                    weight_q(level, m, 0).wait_recv()
                elif stage == 4:
                    for j in slots:
                        weight_q(level, m, j).wait_send()
            if stage == 0:
                weight_p(level, half, 0).start()
            elif stage == 1:
                for j in near:
                    weight_p(level, half, j).start()
            elif stage == 2 and square:
                weight_p(level, half, 3).start()
            elif stage == 3:
                for j in range(n_q):
                    weight_p(level, half, j).wait_recv()
            elif stage == 4:
                for j in range(n_q):
                    weight_p(level, half, j).wait_send()

        if level == 0:
            run()
        else:
            pl.when(here(level))(run)

    def both_ways(step, stage, half):
        for way in range(2):
            weight_stage(1 + 2 * step + way, stage, half)

    for k in range(PIECES):
        send_hidden(0, k)
    for half in range(2):
        for m in halves[half]:
            for way in range(2):
                weight_on(way, 0, m)
        weight_stage(0, 0, half)
    keep = pltpu.make_async_copy(pack, wall.at[:, me, me_q, me_c], local_sem.at[0])
    keep.start()

    width = dist.shape[1]
    base = width - LONGEST
    i = lax.broadcasted_iota(jnp.int32, (QB, width), 0)
    j = lax.broadcasted_iota(jnp.int32, (QB, width), 1)
    dist[...] = jnp.abs(i + base - j).astype(F32)

    total = sin[...]
    for c in send1:
        c.wait_recv()
    for j in range(1, n_mp):
        total += slot1[j]
    ssum[...] = total
    for c in send2:
        c.start()

    for k in range(PIECES):
        wait_hidden(0, k)
        send_hidden(1, k)

    for stage in range(1, 4):
        weight_stage(0, stage, 0)
        if stage == 1:
            weight_stage(0, 1, 1)
    keep.wait()
    fetch = pltpu.make_async_copy(wall.at[3, me], wslot, local_sem.at[1])
    fetch.start()

    for c in send2:
        c.wait_recv()
    total = ssum[...]
    for j in range(1, n_dp):
        total += slot2[j]
    small[...] = total
    bias[...] = jnp.zeros_like(bias)
    for r in range(n_mp):

        @pl.when(me == r)
        def _():
            bias[0:2, :] = total[0:2, r * cols : (r + 1) * cols]

    fetch.wait()
    for j in range(n_dp):
        for s in range(3):
            part = wslot[j // 2, j % 2, :, s * cols : (s + 1) * cols]
            wf[s, j * wrows : (j + 1) * wrows, :] = part.astype(F32)
    for s in range(3):
        wb[s] = wf[s].astype(BF)

    one = jnp.where(lax.broadcasted_iota(jnp.int32, (QB, HEAD), 1) == 0, 1.0, 0.0)
    minus = jnp.where(lax.broadcasted_iota(jnp.int32, (HEAD, QB), 0) < 2, -1.0, 0.0)
    none = jnp.zeros((QB, HEAD), F32)

    def project(ref, shard):
        def part(c, _):
            rows = pl.ds(pl.multiple_of(c * QB, QB), QB)
            at = pl.ds(pl.multiple_of(shard * own + c * QB, QB), QB)
            xc = ref[rows, :]
            xt[:, at] = xc.astype(F32).T.astype(BF)
            q = (dot(xc, wb[0]) + bias[0:1, :]).astype(BF).astype(F32) * HEAD**-0.5
            qs[at, :] = q.astype(BF)
            qt[:, at] = q.T.astype(BF)
            k = dot(xc, wb[1])
            kt[:, at] = k.T.astype(BF)
            v = dot(xc, wb[2]) + bias[1:2, :]
            vt = v.T
            for h in range(heads):
                hs = slice(h * HEAD, (h + 1) * HEAD)
                kp[h, at, :] = jnp.concatenate([k[:, hs], none], axis=1).astype(BF)
                vext[h, at, :] = jnp.concatenate([v[:, hs], one], axis=1).astype(BF)
                vte[h, :, at] = jnp.concatenate([vt[hs], minus], axis=0).astype(BF)
            return 0

        lax.fori_loop(0, own // QB, part, 0)

    project(x, me)
    for half in range(2):
        both_ways(0, 0, half)
    for step in range(n_mp - 1):
        if step > 0:
            for k in range(PIECES):
                wait_hidden(step, k)
                if step < n_mp - 2:
                    send_hidden(step + 1, k)
        if step == n_mp - 2:
            for way in range(2):

                @pl.when(sends(way, step))
                def _():
                    for k in range(PIECES):
                        hidden(way, step, k).wait_send()

                for half in range(2):
                    for m in halves[half]:
                        weight_on(way, 1, m)

        for way in range(2):

            @pl.when(receives(way, step))
            def _():
                shard = me - 1 - step if way == 0 else me + 1 + step
                shard = jnp.clip(shard, 0, n_mp - 1)
                project(hid.at[shard], shard)

        if step == 1:
            weight_stage(0, 2, 1)
            for half in range(2):
                both_ways(0, 1, half)

    early = [
        pltpu.make_async_copy(a, b, early_sem.at[i])
        for i, (a, b) in enumerate(((xt, xt_out), (qt, qt_out), (kp, kp_out), (vte, vte_out)))
    ]
    for c in early:
        c.start()

    def score_block(h, c, place, rows, sl):
        hs = slice(h * HEAD, (h + 1) * HEAD)
        row = c * own + place
        at = pl.ds(pl.multiple_of(row, 128), rows)
        s = dot(qs[at, hs], kt[hs, :LONGEST])
        off = pl.multiple_of(base - row, 128)
        s = s - sl * dist[:rows, pl.ds(off, LONGEST)]
        m = jnp.max(s, axis=1, keepdims=True)
        pb = jnp.exp(s - m).astype(BF)
        pbuf[h, at, :] = pb
        finish(h, c, place, at, rows, dot(pb, vext[h, :LONGEST, :]))

    def finish(h, c, place, at, rows, uu):
        uut = uu.T
        ut[h, :, at] = uut
        oh = uut[:HEAD] * (1.0 / uut[HEAD : HEAD + 1])
        obuf[c, h * HEAD : (h + 1) * HEAD, pl.ds(place, rows)] = oh.astype(BF)

    def short_block(h, c, sl):
        hs = slice(h * HEAD, (h + 1) * HEAD)
        s = dot(qs[LONGEST:, hs], kt[hs, LONGEST:])
        ii = lax.broadcasted_iota(jnp.int32, (tail, tail), 0)
        jj = lax.broadcasted_iota(jnp.int32, (tail, tail), 1)
        s = s - sl * jnp.abs(ii - jj).astype(F32)
        cut = length[0, 1]
        s = jnp.where((ii < cut) == (jj < cut), s, -1e30)
        m = jnp.max(s, axis=1, keepdims=True)
        pb = jnp.exp(s - m).astype(BF)
        p2[h] = pb
        finish(h, c, rest, pl.ds(LONGEST, tail), tail, dot(pb, vext[h, LONGEST:, :]))

    def out_copy(h, j):
        to = lax.rem(me + j, n_mp)
        hs = pl.ds(h * HEAD, HEAD)
        return pltpu.make_async_remote_copy(
            src_ref=obuf.at[to, hs, :], dst_ref=land.at[j, hs, :],
            send_sem=os_sem.at[h, j], recv_sem=or_sem.at[h, j],
            device_id=(me_dp, to), device_id_type=MESH,
        )

    def late(what, h):
        a, b = ((ut, ut_out), (p2, p2_out))[what]
        return pltpu.make_async_copy(a.at[h], b.at[h], late_sem.at[what, h])

    def keep_p(h, c, act):
        @pl.when(c < full)
        def _():
            rows = pl.ds(pl.multiple_of(c * own, own), own)
            act(pltpu.make_async_copy(pbuf.at[h, rows], p.at[h, rows], psem.at[h, c]))

        @pl.when(c == full)
        def _():
            rows = pl.ds(full * own, rest)
            act(pltpu.make_async_copy(pbuf.at[h, rows], p.at[h, rows], psem.at[h, c]))

    pump = [
        (1, 0, 2, 0), (1, 0, 2, 1), (3, 1, 0, 0), (5, 1, 0, 1), (8, 1, 1, 0), (9, 2, 0, 0),
        (10, 1, 1, 1), (11, 1, 2, 0),
    ]
    for h in range(heads):
        sl = slope[h]

        def chunk(j, _):
            c = lax.rem(me + 1 + j, n_mp)

            @pl.when(c < full)
            def _():
                for half in range(own // QB):
                    score_block(h, c, half * QB, QB, sl)

            @pl.when(c == full)
            def _():
                score_block(h, c, 0, rest, sl)
                short_block(h, c, sl)

            keep_p(h, c, lambda copy: copy.start())

            @pl.when(j < n_mp - 1)
            def _():
                out_copy(h, j + 1).start()

            for when, step, stage, half in pump:
                if when // n_mp == h:

                    @pl.when(j == when % n_mp)
                    def _():
                        both_ways(step, stage, half)

            return 0

        lax.fori_loop(0, n_mp, chunk, 0)
        late(0, h).start()
        late(1, h).start()

    for step, stage, half in ((1, 2, 1), (2, 0, 1), (2, 1, 0), (2, 2, 0), (2, 1, 1), (2, 2, 1)):
        both_ways(step, stage, half)
    attnt[me] = obuf[me]
    for h in range(heads):
        hs = slice(h * HEAD, (h + 1) * HEAD)
        for j in range(1, n_mp):
            out_copy(h, j).wait_recv()
            attnt[lax.rem(me - j + n_mp, n_mp), hs, :] = land[j, hs, :]
    for h in range(heads):
        for j in range(1, n_mp):
            out_copy(h, j).wait_send()
        for c in range(n_mp):
            keep_p(h, c, lambda copy: copy.wait())
        late(0, h).wait()
        late(1, h).wait()
    for c in early:
        c.wait()
    for c in send1 + send2:
        c.wait_send()
    for step in range(n_mp - 1):
        for way in range(2):

            @pl.when(sends(way, step))
            def _():
                if step < n_mp - 2:
                    for k in range(PIECES):
                        hidden(way, step, k).wait_send()
                for m in range(4):
                    weight_z(way, step, m).wait_send()

    weight_stage(0, 3, 1)
    for half in range(2):
        weight_stage(0, 4, half)
        for step in range(n_mp - 1):
            both_ways(step, 3, half)
            both_ways(step, 4, half)


def back(
    n_dp, n_mp,
    gt, xt, qt, kp, vte, ut, p, p2, weights, dsum1, sin, gw, gwo,
    grad_in, gq, small, ggu, gdown, gout,
    gl, pbuf, dkt, dvt, dbuf, dland, wfull, gbuf, qland, ssum, slot1, slot2,
    pair, cland, xland, zsum, zland, opair, ocland, oxland, ozsum, ozland,
    gs_sem, gr_sem, qs_sem, qr_sem, ds_sem, dr_sem, ws_sem, wr_sem, s1s, s1r, s2s, s2r,
    psem, wsem, ls_sem, cs_sem, cr_sem, xs_sem, xr_sem, zs_sem, zr_sem,
):
    me_dp, me = lax.axis_index("dp"), lax.axis_index("mp")
    own = gt.shape[2]
    cols = gt.shape[1]
    heads = cols // HEAD
    group = own * n_mp
    tail = group - LONGEST
    full = LONGEST // own
    rest = LONGEST - full * own
    wrows = gq.shape[1]

    def across_mp(j, src, dst, ss, rs):
        to = lax.rem(me + j, n_mp)
        return pltpu.make_async_remote_copy(
            src_ref=src, dst_ref=dst, send_sem=ss, recv_sem=rs,
            device_id=(me_dp, to), device_id_type=MESH,
        )

    def across_dp(j, src, dst, ss, rs):
        to = lax.rem(me_dp + j, n_dp)
        return pltpu.make_async_remote_copy(
            src_ref=src, dst_ref=dst, send_sem=ss, recv_sem=rs,
            device_id=(to, me), device_id_type=MESH,
        )

    def fetch_p(h, j, act):
        c = lax.rem(me - j + n_mp, n_mp)
        slot = lax.rem(h * n_mp + j, 2)

        @pl.when(c < full)
        def _():
            rows = pl.ds(pl.multiple_of(c * own, own), own)
            act(pltpu.make_async_copy(p.at[h, rows, :], pbuf.at[slot], psem.at[slot]))

        @pl.when(c == full)
        def _():
            src = p.at[h, pl.ds(full * own, rest), :]
            act(pltpu.make_async_copy(src, pbuf.at[slot, pl.ds(0, rest), :], psem.at[slot]))

    start, wait = lambda copy: copy.start(), lambda copy: copy.wait()
    fetch_p(0, 0, start)
    fetch_w = pltpu.make_async_copy(weights.at[3], wfull, wsem)

    n_q = n_dp // 2
    me_q, me_c = me_dp // 2, lax.rem(me_dp, 2)
    other = me_dp + 1 - 2 * me_c
    kinds = ((gw, pair, cland, xland, zsum, zland), (gwo, opair, ocland, oxland, ozsum, ozland))

    def rank_of(o):
        return lax.rem(me + 1 + o, n_mp)

    def load_copy(o, t):
        src, own_part = kinds[t][:2]
        return pltpu.make_async_copy(
            src.at[rank_of(o), :, :, me_c], own_part.at[o], ls_sem.at[o, t]
        )

    def pair_up(o, t):
        src, land = kinds[t][0], kinds[t][2]
        return pltpu.make_async_remote_copy(
            src_ref=src.at[rank_of(o), :, :, 1 - me_c], dst_ref=land.at[o],
            send_sem=cs_sem.at[o, t], recv_sem=cr_sem.at[o, t],
            device_id=(other, me), device_id_type=MESH,
        )

    def cross(o, j, t):
        src, land = kinds[t][1], kinds[t][3]
        to = lax.rem(me_q + j, n_q)
        return pltpu.make_async_remote_copy(
            src_ref=src.at[o, :, to], dst_ref=land.at[o, j - 1],
            send_sem=xs_sem.at[o, j, t], recv_sem=xr_sem.at[o, j, t],
            device_id=(to * 2 + me_c, me), device_id_type=MESH,
        )

    def along(o, t):
        src, land = kinds[t][4:]
        return pltpu.make_async_remote_copy(
            src_ref=src.at[o], dst_ref=land.at[o],
            send_sem=zs_sem.at[o, t], recv_sem=zr_sem.at[o, t],
            device_id=(me_dp, rank_of(o)), device_id_type=MESH,
        )

    def add_pair(o):
        for t in range(2):
            own_part, land = kinds[t][1], kinds[t][2]
            load_copy(o, t).wait()
            pair_up(o, t).wait_recv()
            mats = own_part.shape[1]

            def add(i, _):
                a = own_part[o, i // n_q, lax.rem(i, n_q)].astype(F32)
                b = land[o, i // n_q, lax.rem(i, n_q)].astype(F32)
                own_part[o, i // n_q, lax.rem(i, n_q)] = (a + b).astype(BF)
                return 0

            lax.fori_loop(0, mats * n_q, add, 0)
            for j in range(1, n_q):
                cross(o, j, t).start()

    def add_cross(o):
        for t in range(2):
            own_part, land, total = kinds[t][1], kinds[t][3], kinds[t][4]
            for j in range(1, n_q):
                cross(o, j, t).wait_recv()
            for m in range(own_part.shape[1]):
                a = own_part[o, m, me_q].astype(F32)
                for j in range(1, n_q):
                    a += land[o, j - 1, m].astype(F32)
                total[o, m] = a.astype(BF)
            if o < n_mp - 1:
                along(o, t).start()

    for o in range(n_mp):
        for t in range(2):
            load_copy(o, t).start()

    greet(n_dp, n_mp, me_dp, me)

    def grad_copy(h, j):
        hs = pl.ds(h * HEAD, HEAD)
        to = lax.rem(me + j, n_mp)
        return across_mp(
            j, gt.at[to, hs, :], gl.at[j, hs, :], gs_sem.at[h, j], gr_sem.at[h, j]
        )

    for h in range(heads):
        for j in range(1, n_mp):
            grad_copy(h, j).start()
    for o in range(n_mp):
        for t in range(2):
            pair_up(o, t).start()
    fetch_w.start()
    gl[0] = gt[me]

    def query_copy(h, j):
        to = lax.rem(me - j + n_mp, n_mp)
        hs = pl.ds(h * HEAD, HEAD)
        return pltpu.make_async_remote_copy(
            src_ref=dbuf.at[to, 0, hs, :], dst_ref=dland.at[j, 0, hs, :],
            send_sem=qs_sem.at[h, j], recv_sem=qr_sem.at[h, j],
            device_id=(me_dp, to), device_id_type=MESH,
        )

    def pair_copy(h, j):
        to = lax.rem(me - j + n_mp, n_mp)
        hs = pl.ds(h * HEAD, HEAD)
        return pltpu.make_async_remote_copy(
            src_ref=dbuf.at[to, pl.ds(1, 2), hs, :], dst_ref=dland.at[j, pl.ds(1, 2), hs, :],
            send_sem=ds_sem.at[h, j], recv_sem=dr_sem.at[h, j],
            device_id=(me_dp, to), device_id_type=MESH,
        )

    def block(h, j, c, place, rows, pb, keys, add):
        row = c * own + place
        at = pl.ds(pl.multiple_of(row, 128), rows)
        hs = slice(h * HEAD, (h + 1) * HEAD)
        uu = ut[h, :, at]
        inv = 1.0 / uu[HEAD : HEAD + 1]
        gg = gl[j, hs, pl.ds(place, rows)].astype(F32) * inv
        total = jnp.sum(gg * uu[:HEAD], axis=0, keepdims=True) * inv
        high = total.astype(BF).astype(F32)
        low = total - high
        index = lax.broadcasted_iota(jnp.int32, (HEAD, rows), 0)
        extra = jnp.where(index == 0, high, jnp.where(index == 1, low, 0.0))
        gext = jnp.concatenate([gg, extra], axis=0).T.astype(BF)
        dp = dot(gext, vte[h, :, keys])
        ds = (pb.astype(F32) * dp).astype(BF)
        dq = dot(ds, kp[h, keys, :]).T[:HEAD] * (HEAD**-0.5)
        dbuf[c, 0, hs, pl.ds(place, rows)] = dq.astype(BF)
        dk = dot(qt[hs, at], ds)
        dv = dot(gg.astype(BF), pb)
        if add:
            dkt[:, keys] = dkt[:, keys] + dk
            dvt[:, keys] = dvt[:, keys] + dv
        else:
            dkt[:, keys] = dk
            dvt[:, keys] = dv

    pump = [1 + o for o in range(n_mp)]
    for h in range(heads):
        hs = slice(h * HEAD, (h + 1) * HEAD)
        dkt[:, :LONGEST] = jnp.zeros((HEAD, LONGEST), F32)
        dvt[:, :LONGEST] = jnp.zeros((HEAD, LONGEST), F32)

        def chunk(j, _):
            c = lax.rem(me - j + n_mp, n_mp)
            slot = lax.rem(h * n_mp + j, 2)

            @pl.when(j < n_mp - 1)
            def _():
                fetch_p(h, j + 1, start)

            if h < heads - 1:

                @pl.when(j == n_mp - 1)
                def _():
                    fetch_p(h + 1, 0, start)

            @pl.when(j > 0)
            def _():
                grad_copy(h, j).wait_recv()

            fetch_p(h, j, wait)

            keys = slice(0, LONGEST)

            @pl.when(c < full)
            def _():
                for half in range(own // QB):
                    at = pl.ds(half * QB, QB)
                    block(h, j, c, half * QB, QB, pbuf[slot, at, :], keys, True)

            @pl.when(c == full)
            def _():
                block(h, j, c, 0, rest, pbuf[slot, :rest, :], keys, True)
                block(h, j, c, rest, tail, p2[h], slice(LONGEST, group), False)

            @pl.when(j > 0)
            def _():
                query_copy(h, j).start()

            for o in range(n_mp):
                if pump[o] // n_mp == h:

                    @pl.when(j == pump[o] % n_mp)
                    def _():
                        add_pair(o)

            return 0

        lax.fori_loop(0, n_mp, chunk, 0)
        if h == heads - 1:
            add_cross(0)
        for c in range(n_mp):
            dbuf[c, 1, hs, :] = dkt[:, c * own : (c + 1) * own].astype(BF)
            dbuf[c, 2, hs, :] = dvt[:, c * own : (c + 1) * own].astype(BF)
        for j in range(1, n_mp):
            pair_copy(h, j).start()

    ones = jnp.ones((8, own), BF)
    sq = jnp.zeros((8, cols), F32)
    sv = jnp.zeros((8, cols), F32)
    for c in range(n_mp):
        sq += dot_nt(ones, dbuf[c, 0])
        sv += dot_nt(ones, dbuf[c, 2])
    ssum[...] = sin[...]
    for r in range(n_mp):

        @pl.when(me == r)
        def _():
            ssum[0:1, r * cols : (r + 1) * cols] = sq[0:1]
            ssum[1:2, r * cols : (r + 1) * cols] = sv[0:1]

    send1 = [across_mp(j, ssum, slot1.at[j], s1s.at[j], s1r.at[j]) for j in range(1, n_mp)]
    for c in send1:
        c.start()

    total = jnp.zeros((xt.shape[0], 3 * cols), F32)
    for c in range(n_mp):
        total += dot_nt(xt[:, c * own : (c + 1) * own], dbuf[c].reshape(3 * cols, own))
    for d in range(n_dp):
        gbuf[d] = total[d * wrows : (d + 1) * wrows].astype(BF)

    def weight_copy(j):
        to = lax.rem(me_dp + j, n_dp)
        return across_dp(j, gbuf.at[to], qland.at[j], ws_sem.at[j], wr_sem.at[j])

    for j in range(1, n_dp):
        weight_copy(j).start()

    add_cross(1)
    for c in send1:
        c.wait_send()
        c.wait_recv()
    total = ssum[...]
    for j in range(1, n_mp):
        total += slot1[j]
    ssum[...] = total
    send2 = [across_dp(j, ssum, slot2.at[j], s2s.at[j], s2r.at[j]) for j in range(1, n_dp)]
    for c in send2:
        c.start()

    fetch_w.wait()
    into = dot(wfull[me, :, : 3 * cols], dbuf[me].reshape(3 * cols, own))
    for j in range(1, n_mp):
        for h in range(heads):
            query_copy(h, j).wait_recv()
            pair_copy(h, j).wait_recv()
        r = lax.rem(me + j, n_mp)
        into += dot(wfull[r, :, : 3 * cols], dland[j].reshape(3 * cols, own))
    grad_in[...] = (dsum1[...] + into.T).astype(BF)

    for o in range(2, n_mp):
        add_cross(o)
    total = gbuf[me_dp].astype(F32)
    for j in range(1, n_dp):
        weight_copy(j).wait_recv()
        total += qland[j].astype(F32)
    for s in range(3):
        gq[s] = total[:, s * cols : (s + 1) * cols]
    total = ssum[...]
    for c in send2:
        c.wait_recv()
    for j in range(1, n_dp):
        total += slot2[j]
    small[...] = total
    for t in range(2):
        total, land = kinds[t][4:]
        for o in range(n_mp - 1):
            along(o, t).wait_recv()
        for m in range(total.shape[1]):
            a = total[n_mp - 1, m].astype(F32)
            for o in range(n_mp - 1):
                a += land[o, m].astype(F32)
            if t == 1:
                gout[...] = a.T
            elif m == 2:
                gdown[...] = a
            else:
                ggu[m] = a
    for t in range(2):
        for o in range(n_mp):
            pair_up(o, t).wait_send()
            for j in range(1, n_q):
                cross(o, j, t).wait_send()
            if o < n_mp - 1:
                along(o, t).wait_send()
    for c in send2:
        c.wait_send()
    for j in range(1, n_dp):
        weight_copy(j).wait_send()
    for h in range(heads):
        for j in range(1, n_mp):
            grad_copy(h, j).wait_send()
            query_copy(h, j).wait_send()
            pair_copy(h, j).wait_send()


def norm_parts(r):
    centre = r - jnp.mean(r, axis=-1, keepdims=True)
    spread = jnp.mean(centre * centre, axis=-1, keepdims=True)
    rstd = lax.rsqrt(spread + 1e-05)
    return centre * rstd, rstd


def norm_back(dn, n, rstd):
    return rstd * (
        dn - jnp.mean(dn, axis=-1, keepdims=True) - n * jnp.mean(dn * n, axis=-1, keepdims=True)
    )


def colsum(a):
    return jnp.sum(a, axis=0, keepdims=True)


def flip(a):
    return a.astype(F32).T.astype(BF)


GELU_C = 0.7978845608
GELU_A = 0.044715


def middle(
    attn, x, cot, wlast, small, w,
    result, dsum1, dattn, gw, gwout, gsmall,
    wout, mid, midb, midt, gate, up, y, dffn, dffnt, dmid,
):
    i = pl.program_id(0)
    n = pl.num_programs(0) // 2
    parts, cols = attn.shape[0], attn.shape[1]

    @pl.when(i == 0)
    def _():
        branch = jnp.zeros((x.shape[1], x.shape[0]), F32)
        for r in range(parts):
            wout[r] = wlast[0, r, :, 3 * cols :]
            branch += dot(wout[r], attn[r])
        branch = branch.T + x[...].astype(F32) + small[2:3, :]
        nn, _ = norm_parts(branch)
        m = nn * small[3:4, :] + small[4:5, :]
        dsum1[...] = branch
        mid[...] = m
        midb[...] = m.astype(BF)
        midt[...] = m.T.astype(BF)
        y[...] = jnp.zeros_like(y)

    @pl.when(i < n)
    def _():
        mb = midb[...]
        ga = dot(mb, w[0, 0]) + small[pl.ds(8 + i, 1), :]
        u = dot(mb, w[1, 0]) + small[pl.ds(8 + n + i, 1), :]
        gate[i] = ga
        up[i] = u
        t = jnp.tanh(GELU_C * (ga + GELU_A * ga * ga * ga))
        act = (0.5 * ga * (1.0 + t) * u).astype(BF)
        y[...] += dot_nt(act, w[2, 0])

    @pl.when(i == n - 1)
    def _():
        r = mid[...] + y[...] + small[5:6, :]
        nn, rstd = norm_parts(r)
        gain = small[6:7, :]
        result[...] = (nn * gain + small[7:8, :]).astype(BF)
        c = cot[...].astype(F32)
        ds = norm_back(c * gain, nn, rstd)
        gsmall[6:7, :] = colsum(c * nn)
        gsmall[7:8, :] = colsum(c)
        dmid[...] = ds
        db = ds.astype(BF)
        dffn[...] = db
        dffnt[...] = ds.T.astype(BF)
        gsmall[5:6, :] = colsum(db.astype(F32))
        gsmall[0:2, :] = jnp.zeros_like(gsmall[0:2, :])

    @pl.when(i >= n)
    def _():
        k = 2 * n - 1 - i
        ga = gate[k]
        u = up[k]
        sq = ga * ga
        t = jnp.tanh(GELU_C * (ga + GELU_A * ga * sq))
        half = 0.5 * (1.0 + t)
        gelu = ga * half
        slope = half + (0.5 * GELU_C) * ga * (1.0 - t * t) * (1.0 + 3.0 * GELU_A * sq)
        act = (gelu * u).astype(BF)
        dact = dot(dffn[...], w[2, 0])
        gw[0, 2] = dot(dffnt[...], act).astype(BF)
        dga = (dact * u * slope).astype(BF)
        du = (dact * gelu).astype(BF)
        gsmall[pl.ds(8 + k, 1), :] = colsum(dga.astype(F32))
        gsmall[pl.ds(8 + n + k, 1), :] = colsum(du.astype(F32))
        gw[0, 0] = dot(midt[...], dga).astype(BF)
        gw[0, 1] = dot(midt[...], du).astype(BF)
        dmid[...] += dot_nt(dga, w[0, 0]) + dot_nt(du, w[1, 0])

    @pl.when(i == 2 * n - 1)
    def _():
        nn, rstd = norm_parts(dsum1[...])
        dm = dmid[...]
        gsmall[3:4, :] = colsum(dm * nn)
        gsmall[4:5, :] = colsum(dm)
        ds = norm_back(dm * small[3:4, :], nn, rstd)
        dsum1[...] = ds
        db = ds.astype(BF)
        gsmall[2:3, :] = colsum(db.astype(F32))
        dbt = ds.T.astype(BF)
        for r in range(parts):
            dattn[r] = dot(db, wout[r]).T.astype(BF)
            gwout[r] = dot_nt(dbt, attn[r]).astype(BF)


def hand_on(*refs):
    n = len(refs) // 2
    for a, b in zip(refs[:n], refs[n:]):
        b[...] = a[...]


def head_slopes(first_head, head_count):
    number = first_head + jnp.arange(head_count, dtype=jnp.int32)
    exponent = jnp.where(number < 8, number.astype(F32) + 1.0, number.astype(F32) - 7.5)
    return jnp.exp2(-exponent)


def cost(flops):
    return pl.CostEstimate(flops=flops, bytes_accessed=1 << 24, transcendentals=0)


def params(**kw):
    return pltpu.CompilerParams(vmem_limit_bytes=VMEM_LIMIT, **kw)


def per_device(
    hidden_in, lengths, w_qkv, b_qv, w_out, b_out, ln1_gain, ln1_bias, w_gu, b_gu, w_down,
    b_down, ln2_gain, ln2_bias, cotangent,
):
    both = ("dp", "mp")
    n_dp, n_mp = lax.axis_size("dp"), lax.axis_size("mp")
    n = n_dp * n_mp
    mp_rank = lax.axis_index("mp")
    own, width = hidden_in.shape
    group = own * n_mp
    sds = jax.ShapeDtypeStruct

    dev = lax.axis_index("dp") * n_mp + mp_rank

    def placed(a):
        zero = jnp.zeros((a.shape[0], a.shape[1] * n), F32)
        return lax.dynamic_update_slice_in_dim(zero, a, dev * a.shape[1], 1)

    vectors = jnp.stack([b_out, ln1_gain, ln1_bias, b_down, ln2_gain, ln2_bias])
    vectors = jnp.concatenate([b_qv, vectors], axis=0)
    small_own = jnp.concatenate(
        [placed(vectors), placed(b_gu).reshape(-1, width)], axis=0
    )
    srows = small_own.shape[0]

    wrows, cols = w_qkv.shape[1], w_qkv.shape[2]
    ff_part = w_gu.shape[2]
    heads = cols // HEAD
    tail = group - LONGEST

    n_q = n_dp // 2
    units = 2 * n_mp - 1

    slopes = head_slopes(mp_rank * heads, heads)
    dma = pltpu.SemaphoreType.DMA

    small, xt, qt, kp, vte, ut, attn, p, p2, weights = pl.pallas_call(
        functools.partial(front, n_dp, n_mp),
        out_shape=(
            sds((srows, width), F32),
            sds((width, group), BF),
            sds((cols, group), BF),
            sds((heads, group, 2 * HEAD), BF),
            sds((heads, 2 * HEAD, group), BF),
            sds((heads, 2 * HEAD, group), F32),
            sds((n_mp, cols, own), BF),
            sds((heads, LONGEST, LONGEST), BF),
            sds((heads, tail, tail), BF),
            sds((4, n_mp, n_q, 2, wrows, ff_part), BF),
        ),
        in_specs=[vmem(), vmem(), vmem(), vmem(), vmem(), vmem(), smem(), smem()],
        out_specs=(
            vmem(), hbm(), hbm(), hbm(), hbm(), hbm(), vmem(), hbm(), hbm(), hbm(),
        ),
        scratch_shapes=[
            pltpu.VMEM((4, wrows, ff_part), BF),
            pltpu.VMEM((width, group), BF),
            pltpu.VMEM((cols, group), BF),
            pltpu.VMEM((heads, group, 2 * HEAD), BF),
            pltpu.VMEM((heads, 2 * HEAD, group), BF),
            pltpu.VMEM((heads, 2 * HEAD, group), F32),
            pltpu.VMEM((heads, tail, tail), BF),
            pltpu.VMEM((n_mp, own, width), BF),
            pltpu.VMEM((n_q, 2, wrows, ff_part), BF),
            pltpu.VMEM((3, width, cols), F32),
            pltpu.VMEM((3, width, cols), BF),
            pltpu.VMEM((n_mp, srows, width), F32),
            pltpu.VMEM((srows, width), F32),
            pltpu.VMEM((n_dp, srows, width), F32),
            pltpu.VMEM((8, cols), F32),
            pltpu.VMEM((group, cols), BF),
            pltpu.VMEM((cols, group), BF),
            pltpu.VMEM((heads, group, 2 * HEAD), BF),
            pltpu.VMEM((QB, LONGEST + LONGEST // QB * QB), F32),
            pltpu.VMEM((heads, LONGEST, LONGEST), BF),
            pltpu.VMEM((n_mp, cols, own), BF),
            pltpu.VMEM((n_mp, cols, own), BF),
            dma((2, n_mp - 1, PIECES)),
            dma((2, n_mp - 1, PIECES)),
            dma((n_mp,)),
            dma((n_mp,)),
            dma((n_dp,)),
            dma((n_dp,)),
            dma((heads, n_mp)),
            dma((heads, n_mp)),
            dma((heads, n_mp)),
            dma((2,)),
            dma((4,)),
            dma((2, heads)),
            dma((2, n_mp - 1, 4)),
            dma((2, n_mp - 1, 4)),
            dma((units, 4, n_q)),
            dma((units, 4, n_q)),
            dma((units, 2, n_q)),
            dma((units, 2, n_q)),
        ],
        compiler_params=params(collective_id=0, has_side_effects=True),
        cost_estimate=cost(11 * LONGEST * LONGEST * HEAD * heads * 12),
        name="front",
    )(hidden_in, w_qkv, w_out, w_gu, w_down.T, small_own, slopes, lengths)
    weights = weights.reshape(4, n_mp, width, ff_part)

    fixed = lambda *s: pl.BlockSpec(s, lambda i: (0,) * len(s))
    walk = lambda i: jnp.where(i < n_mp, i, 2 * n_mp - 1 - i)
    late = lambda i: jnp.where(i < n_mp, n_mp - 1, 2 * n_mp - 1 - i)
    result, dsum1, dattn, gw, gwout, gsmall = pl.pallas_call(
        middle,
        grid=(2 * n_mp,),
        out_shape=(
            sds((own, width), BF),
            sds((own, width), F32),
            sds((n_mp, cols, own), BF),
            sds((n_mp, 3, width, ff_part), BF),
            sds((n_mp, width, cols), BF),
            sds((srows, width), F32),
        ),
        in_specs=[
            fixed(n_mp, cols, own),
            fixed(own, width),
            fixed(own, width),
            pl.BlockSpec(
                (1, n_mp, width, ff_part),
                lambda i: (3, 0, 0, 0),
                pipeline_mode=pl.Buffered(1),
            ),
            fixed(srows, width),
            pl.BlockSpec((3, 1, width, ff_part), lambda i: (0, walk(i), 0, 0)),
        ],
        out_specs=(
            fixed(own, width),
            fixed(own, width),
            fixed(n_mp, cols, own),
            pl.BlockSpec((1, 3, width, ff_part), lambda i: (late(i), 0, 0, 0)),
            fixed(n_mp, width, cols),
            fixed(srows, width),
        ),
        scratch_shapes=[
            pltpu.VMEM((n_mp, width, cols), BF),
            pltpu.VMEM((own, width), F32),
            pltpu.VMEM((own, width), BF),
            pltpu.VMEM((width, own), BF),
            pltpu.VMEM((n_mp, own, ff_part), F32),
            pltpu.VMEM((n_mp, own, ff_part), F32),
            pltpu.VMEM((own, width), F32),
            pltpu.VMEM((own, width), BF),
            pltpu.VMEM((width, own), BF),
            pltpu.VMEM((own, width), F32),
        ],
        compiler_params=params(),
        name="middle",
    )(attn, hidden_in, cotangent, weights, small, weights)

    gw = gw.reshape(n_mp, 3, n_q, 2, wrows, ff_part)
    gwout = gwout.reshape(n_mp, 1, n_q, 2, wrows, cols)
    grad_in, gqkv, gsmall, ggu, gdown, gout = pl.pallas_call(
        functools.partial(back, n_dp, n_mp),
        out_shape=(
            sds((own, width), BF),
            sds((3, wrows, cols), F32),
            sds((srows, width), F32),
            sds((2, wrows, ff_part), F32),
            sds((wrows, ff_part), F32),
            sds((cols, wrows), F32),
        ),
        in_specs=[
            vmem(), vmem(), vmem(), vmem(), vmem(), vmem(), hbm(), vmem(), hbm(), vmem(), vmem(),
            hbm(), hbm(),
        ],
        out_specs=(vmem(), vmem(), vmem(), vmem(), vmem(), vmem()),
        scratch_shapes=[
            pltpu.VMEM((n_mp, cols, own), BF),
            pltpu.VMEM((2, own, LONGEST), BF),
            pltpu.VMEM((HEAD, group), F32),
            pltpu.VMEM((HEAD, group), F32),
            pltpu.VMEM((n_mp, 3, cols, own), BF),
            pltpu.VMEM((n_mp, 3, cols, own), BF),
            pltpu.VMEM((n_mp, width, ff_part), BF),
            pltpu.VMEM((n_dp, wrows, 3 * cols), BF),
            pltpu.VMEM((n_dp, wrows, 3 * cols), BF),
            pltpu.VMEM((srows, width), F32),
            pltpu.VMEM((n_mp, srows, width), F32),
            pltpu.VMEM((n_dp, srows, width), F32),
            pltpu.VMEM((n_mp, 3, n_q, wrows, ff_part), BF),
            pltpu.VMEM((n_mp, 3, n_q, wrows, ff_part), BF),
            pltpu.VMEM((n_mp, n_q - 1, 3, wrows, ff_part), BF),
            pltpu.VMEM((n_mp, 3, wrows, ff_part), BF),
            pltpu.VMEM((n_mp - 1, 3, wrows, ff_part), BF),
            pltpu.VMEM((n_mp, 1, n_q, wrows, cols), BF),
            pltpu.VMEM((n_mp, 1, n_q, wrows, cols), BF),
            pltpu.VMEM((n_mp, n_q - 1, 1, wrows, cols), BF),
            pltpu.VMEM((n_mp, 1, wrows, cols), BF),
            pltpu.VMEM((n_mp - 1, 1, wrows, cols), BF),
            dma((heads, n_mp)),
            dma((heads, n_mp)),
            dma((heads, n_mp)),
            dma((heads, n_mp)),
            dma((heads, n_mp)),
            dma((heads, n_mp)),
            dma((n_dp,)),
            dma((n_dp,)),
            dma((n_mp,)),
            dma((n_mp,)),
            dma((n_dp,)),
            dma((n_dp,)),
            dma((2,)),
            dma,
            dma((n_mp, 2)),
            dma((n_mp, 2)),
            dma((n_mp, 2)),
            dma((n_mp, n_q, 2)),
            dma((n_mp, n_q, 2)),
            dma((n_mp - 1, 2)),
            dma((n_mp - 1, 2)),
        ],
        compiler_params=params(collective_id=1, has_side_effects=True),
        cost_estimate=cost(11 * LONGEST * LONGEST * HEAD * heads * 12),
        name="back",
    )(dattn, xt, qt, kp, vte, ut, p, p2, weights, dsum1, gsmall, gw, gwout)

    finished = (grad_in, gqkv, ggu, gdown, gout)
    grad_in, gqkv, ggu, gdown, gout = pl.pallas_call(
        hand_on,
        out_shape=tuple(sds(a.shape, a.dtype) for a in finished),
        in_specs=[vmem()] * len(finished),
        out_specs=(vmem(),) * len(finished),
        compiler_params=params(),
        name="hand_on",
    )(*finished)

    def own_columns(a):
        part = a.shape[1] // n
        return lax.dynamic_slice_in_dim(a, dev * part, part, 1)

    gs = own_columns(gsmall[:8])
    g_gu = own_columns(gsmall[8:].reshape(2, -1))

    return (
        result,
        grad_in,
        gqkv,
        gs[0:2],
        gout,
        gs[2],
        gs[3],
        gs[4],
        ggu,
        g_gu,
        gdown.T,
        gs[5],
        gs[6],
        gs[7],
    )


def solution(mesh):
    rows = P(("dp", "mp"), None)
    vec = P(("dp", "mp"))
    vecs = P(None, ("dp", "mp"))
    wide = P(None, "dp", "mp")
    tall = P("mp", "dp")
    return jax.shard_map(
        per_device,
        mesh=mesh,
        in_specs=(
            rows, P("dp", None), wide, vecs, tall, vec, vec, vec, wide, vecs, tall, vec, vec, vec,
            rows,
        ),
        out_specs=(
            rows, rows, wide, vecs, tall, vec, vec, vec, wide, vecs, tall, vec, vec, vec,
        ),
        check_vma=False,
    )
```

```python
import functools

import jax
import jax.numpy as jnp
from jax import lax
from jax.experimental import pallas as pl
from jax.experimental.pallas import tpu as pltpu
from jax.sharding import PartitionSpec as P

HEAD = 64
LONGEST = 1664
QB = 256
BF = jnp.bfloat16
F32 = jnp.float32
VMEM_LIMIT = 60 * 1024 * 1024


def dot(a, b):
    return lax.dot_general(a, b, (((1,), (0,)), ((), ())), preferred_element_type=F32)


def dot_nt(a, b):
    return lax.dot_general(a, b, (((1,), (1,)), ((), ())), preferred_element_type=F32)


def vmem():
    return pl.BlockSpec(memory_space=pltpu.VMEM)


def smem():
    return pl.BlockSpec(memory_space=pltpu.SMEM)


def hbm():
    return pl.BlockSpec(memory_space=pl.ANY)


MESH = pl.DeviceIdType.MESH
PIECES = 4


def greet(n_dp, n_mp, me_dp, me_mp, meanwhile=lambda: None):
    barrier = pltpu.get_barrier_semaphore()
    for j in range(1, n_mp):
        pl.semaphore_signal(
            barrier, 1, device_id=(me_dp, lax.rem(me_mp + j, n_mp)), device_id_type=MESH
        )
    for j in range(1, n_dp):
        pl.semaphore_signal(
            barrier, 1, device_id=(lax.rem(me_dp + j, n_dp), me_mp), device_id_type=MESH
        )
    meanwhile()
    pl.semaphore_wait(barrier, n_mp - 1 + n_dp - 1)


def front(
    n_dp, n_mp,
    x, wqkv, wout, wgu, wdown, sin, slope, length,
    small, xt_out, qt_out, kp_out, vte_out, ut_out, attnt, p, p2_out, wall,
    pack, xt, qt, kp, vte, ut, p2, hid, wslot, wf, wb, slot1, ssum, slot2, bias, qs, kt, vext, dist, pbuf, obuf, land,
    hs_sem, hr_sem, s1s, s1r, s2s, s2r, os_sem, or_sem, psem,
    local_sem, early_sem, late_sem, wzs, wzr, wqs, wqr, wps, wpr,
):
    me_dp, me = lax.axis_index("dp"), lax.axis_index("mp")
    own = x.shape[0]
    group = own * n_mp
    wrows, cols = pack.shape[1], wb.shape[2]
    heads = cols // HEAD
    tail = group - LONGEST
    full = LONGEST // own
    rest = LONGEST - full * own
    piece = own // PIECES

    def across_mp(j, src, dst, ss, rs):
        to = lax.rem(me + j, n_mp)
        return pltpu.make_async_remote_copy(
            src_ref=src, dst_ref=dst, send_sem=ss, recv_sem=rs,
            device_id=(me_dp, to), device_id_type=MESH,
        )

    def across_dp(j, src, dst, ss, rs):
        to = lax.rem(me_dp + j, n_dp)
        return pltpu.make_async_remote_copy(
            src_ref=src, dst_ref=dst, send_sem=ss, recv_sem=rs,
            device_id=(to, me), device_id_type=MESH,
        )

    def make_pack():
        for m in range(2):
            pack[m] = wgu[m].astype(BF)
        pack[2] = wdown[...].astype(BF)
        last = [wqkv[0], wqkv[1], wqkv[2], wout[...].T]
        pack[3] = jnp.concatenate(last, axis=1).astype(BF)

    greet(n_dp, n_mp, me_dp, me, make_pack)

    send1 = [across_mp(j, sin, slot1.at[j], s1s.at[j], s1r.at[j]) for j in range(1, n_mp)]
    send2 = [across_dp(j, ssum, slot2.at[j], s2s.at[j], s2r.at[j]) for j in range(1, n_dp)]
    for c in send1:
        c.start()

    def hidden(way, step, k):
        shard = me - step if way == 0 else me + step
        to = me + 1 if way == 0 else me - 1
        shard, to = jnp.clip(shard, 0, n_mp - 1), jnp.clip(to, 0, n_mp - 1)
        rows = pl.ds(k * piece, piece)
        src = x.at[rows, :] if step == 0 else hid.at[shard, rows, :]
        return pltpu.make_async_remote_copy(
            src_ref=src, dst_ref=hid.at[shard, rows, :],
            send_sem=hs_sem.at[way, step, k], recv_sem=hr_sem.at[way, step, k],
            device_id=(me_dp, to), device_id_type=MESH,
        )

    def sends(way, step):
        if way == 0:
            return (me >= step) & (me < n_mp - 1)
        return (me + step <= n_mp - 1) & (me > 0)

    def receives(way, step):
        return me - 1 - step >= 0 if way == 0 else me + 1 + step <= n_mp - 1

    def send_hidden(step, k):
        for way in range(2):

            @pl.when(sends(way, step))
            def _():
                hidden(way, step, k).start()

    def wait_hidden(step, k):
        for way in range(2):

            @pl.when(receives(way, step))
            def _():
                hidden(way, step, k).wait_recv()

    n_q = n_dp // 2
    me_q, me_c = me_dp // 2, lax.rem(me_dp, 2)
    square = n_q == 4
    halves = ((3, 2), (0, 1))

    def unit_rank(level):
        if level == 0:
            return me
        step, way = (level - 1) // 2, (level - 1) % 2
        return jnp.clip(me - 1 - step if way == 0 else me + 1 + step, 0, n_mp - 1)

    def here(level):
        return True if level == 0 else receives((level - 1) % 2, (level - 1) // 2)

    def mate(j):
        if not square:
            return lax.rem(me_q + j, n_q)
        x1, y1 = lax.rem(me_q, 2), me_q // 2
        x2 = 1 - x1 if j % 2 else x1
        y2 = 1 - y1 if j // 2 else y1
        return 2 * y2 + x2

    def weight_z(way, step, m):
        level = 0 if step == 0 else 1 + 2 * (step - 1) + way
        r = unit_rank(level)
        to = jnp.clip(me + 1 if way == 0 else me - 1, 0, n_mp - 1)
        dst = wall.at[m, r, me_q, me_c]
        src = pack.at[m] if step == 0 else dst
        return pltpu.make_async_remote_copy(
            src_ref=src, dst_ref=dst,
            send_sem=wzs.at[way, step, m], recv_sem=wzr.at[way, step, m],
            device_id=(me_dp, to), device_id_type=MESH,
        )

    def weight_q(level, m, slot):
        r = unit_rank(level)
        j, what = (slot, 0) if slot else ((1, 2) if m % 2 else (2, 1))
        dst = wall.at[m, r, mate(what), me_c]
        src = pack.at[m] if level == 0 and slot else dst
        return pltpu.make_async_remote_copy(
            src_ref=src, dst_ref=dst,
            send_sem=wqs.at[level, m, slot], recv_sem=wqr.at[level, m, slot],
            device_id=(mate(j) * 2 + me_c, me), device_id_type=MESH,
        )

    def weight_p(level, half, j):
        part = pl.ds(min(halves[half]), 2)
        dst = wall.at[part, unit_rank(level), mate(j), me_c]
        src = pack.at[part] if level == 0 and j == 0 else dst
        return pltpu.make_async_remote_copy(
            src_ref=src, dst_ref=dst,
            send_sem=wps.at[level, half, j], recv_sem=wpr.at[level, half, j],
            device_id=(me_q * 2 + 1 - me_c, me), device_id_type=MESH,
        )

    near = (1, 2) if square else tuple(range(1, n_q))
    slots = ((0,) if square else ()) + near

    def weight_on(way, step, m):
        @pl.when(sends(way, step))
        def _():
            weight_z(way, step, m).start()

    def weight_stage(level, stage, half):
        step, way = (level - 1) // 2, (level - 1) % 2

        def run():
            for m in halves[half]:
                if stage == 0:
                    if level > 0:
                        weight_z(way, step, m).wait_recv()
                        if 0 < step < n_mp - 2:
                            weight_on(way, step + 1, m)
                    for j in near:
                        weight_q(level, m, j).start()
                elif stage == 1:
                    if square:
                        weight_q(level, m, 2 if m % 2 else 1).wait_recv()
                        weight_q(level, m, 0).start()
                        weight_q(level, m, 1 if m % 2 else 2).wait_recv()
                    else:
                        for j in near:
                            weight_q(level, m, j).wait_recv()
                elif stage == 2 and square:
                    weight_q(level, m, 0).wait_recv()
                elif stage == 4:
                    for j in slots:
                        weight_q(level, m, j).wait_send()
            if stage == 0:
                weight_p(level, half, 0).start()
            elif stage == 1:
                for j in near:
                    weight_p(level, half, j).start()
            elif stage == 2 and square:
                weight_p(level, half, 3).start()
            elif stage == 3:
                for j in range(n_q):
                    weight_p(level, half, j).wait_recv()
            elif stage == 4:
                for j in range(n_q):
                    weight_p(level, half, j).wait_send()

        if level == 0:
            run()
        else:
            pl.when(here(level))(run)

    def both_ways(step, stage, half):
        for way in range(2):
            weight_stage(1 + 2 * step + way, stage, half)

    for k in range(PIECES):
        send_hidden(0, k)
    for half in range(2):
        for m in halves[half]:
            for way in range(2):
                weight_on(way, 0, m)
        weight_stage(0, 0, half)
    keep = pltpu.make_async_copy(pack, wall.at[:, me, me_q, me_c], local_sem.at[0])
    keep.start()

    width = dist.shape[1]
    base = width - LONGEST
    i = lax.broadcasted_iota(jnp.int32, (QB, width), 0)
    j = lax.broadcasted_iota(jnp.int32, (QB, width), 1)
    dist[...] = jnp.abs(i + base - j).astype(F32)

    total = sin[...]
    for c in send1:
        c.wait_recv()
    for j in range(1, n_mp):
        total += slot1[j]
    ssum[...] = total
    for c in send2:
        c.start()

    for k in range(PIECES):
        wait_hidden(0, k)
        send_hidden(1, k)

    for stage in range(1, 4):
        weight_stage(0, stage, 0)
        if stage == 1:
            weight_stage(0, 1, 1)
    keep.wait()
    fetch = pltpu.make_async_copy(wall.at[3, me], wslot, local_sem.at[1])
    fetch.start()

    for c in send2:
        c.wait_recv()
    total = ssum[...]
    for j in range(1, n_dp):
        total += slot2[j]
    small[...] = total
    bias[...] = jnp.zeros_like(bias)
    for r in range(n_mp):

        @pl.when(me == r)
        def _():
            bias[0:2, :] = total[0:2, r * cols : (r + 1) * cols]

    fetch.wait()
    for j in range(n_dp):
        for s in range(3):
            part = wslot[j // 2, j % 2, :, s * cols : (s + 1) * cols]
            wf[s, j * wrows : (j + 1) * wrows, :] = part.astype(F32)
    for s in range(3):
        wb[s] = wf[s].astype(BF)

    one = jnp.where(lax.broadcasted_iota(jnp.int32, (QB, HEAD), 1) == 0, 1.0, 0.0)
    minus = jnp.where(lax.broadcasted_iota(jnp.int32, (HEAD, QB), 0) < 2, -1.0, 0.0)
    none = jnp.zeros((QB, HEAD), F32)

    def project(ref, shard):
        def part(c, _):
            rows = pl.ds(pl.multiple_of(c * QB, QB), QB)
            at = pl.ds(pl.multiple_of(shard * own + c * QB, QB), QB)
            xc = ref[rows, :]
            xt[:, at] = xc.astype(F32).T.astype(BF)
            q = (dot(xc, wb[0]) + bias[0:1, :]).astype(BF).astype(F32) * HEAD**-0.5
            qs[at, :] = q.astype(BF)
            qt[:, at] = q.T.astype(BF)
            k = dot(xc, wb[1])
            kt[:, at] = k.T.astype(BF)
            v = dot(xc, wb[2]) + bias[1:2, :]
            vt = v.T
            for h in range(heads):
                hs = slice(h * HEAD, (h + 1) * HEAD)
                kp[h, at, :] = jnp.concatenate([k[:, hs], none], axis=1).astype(BF)
                vext[h, at, :] = jnp.concatenate([v[:, hs], one], axis=1).astype(BF)
                vte[h, :, at] = jnp.concatenate([vt[hs], minus], axis=0).astype(BF)
            return 0

        lax.fori_loop(0, own // QB, part, 0)

    project(x, me)
    for half in range(2):
        both_ways(0, 0, half)
    for step in range(n_mp - 1):
        if step > 0:
            for k in range(PIECES):
                wait_hidden(step, k)
                if step < n_mp - 2:
                    send_hidden(step + 1, k)
        if step == n_mp - 2:
            for way in range(2):

                @pl.when(sends(way, step))
                def _():
                    for k in range(PIECES):
                        hidden(way, step, k).wait_send()

                for half in range(2):
                    for m in halves[half]:
                        weight_on(way, 1, m)

        for way in range(2):

            @pl.when(receives(way, step))
            def _():
                shard = me - 1 - step if way == 0 else me + 1 + step
                shard = jnp.clip(shard, 0, n_mp - 1)
                project(hid.at[shard], shard)

        if step == 1:
            weight_stage(0, 2, 1)
            for half in range(2):
                both_ways(0, 1, half)

    early = [
        pltpu.make_async_copy(a, b, early_sem.at[i])
        for i, (a, b) in enumerate(((xt, xt_out), (qt, qt_out), (kp, kp_out), (vte, vte_out)))
    ]
    for c in early:
        c.start()

    def score_block(h, c, place, rows, sl):
        hs = slice(h * HEAD, (h + 1) * HEAD)
        row = c * own + place
        at = pl.ds(pl.multiple_of(row, 128), rows)
        s = dot(qs[at, hs], kt[hs, :LONGEST])
        off = pl.multiple_of(base - row, 128)
        s = s - sl * dist[:rows, pl.ds(off, LONGEST)]
        m = jnp.max(s, axis=1, keepdims=True)
        pb = jnp.exp(s - m).astype(BF)
        pbuf[h, at, :] = pb
        finish(h, c, place, at, rows, dot(pb, vext[h, :LONGEST, :]))

    def finish(h, c, place, at, rows, uu):
        uut = uu.T
        ut[h, :, at] = uut
        oh = uut[:HEAD] * (1.0 / uut[HEAD : HEAD + 1])
        obuf[c, h * HEAD : (h + 1) * HEAD, pl.ds(place, rows)] = oh.astype(BF)

    def short_block(h, c, sl):
        hs = slice(h * HEAD, (h + 1) * HEAD)
        s = dot(qs[LONGEST:, hs], kt[hs, LONGEST:])
        ii = lax.broadcasted_iota(jnp.int32, (tail, tail), 0)
        jj = lax.broadcasted_iota(jnp.int32, (tail, tail), 1)
        s = s - sl * jnp.abs(ii - jj).astype(F32)
        cut = length[0, 1]
        s = jnp.where((ii < cut) == (jj < cut), s, -1e30)
        m = jnp.max(s, axis=1, keepdims=True)
        pb = jnp.exp(s - m).astype(BF)
        p2[h] = pb
        finish(h, c, rest, pl.ds(LONGEST, tail), tail, dot(pb, vext[h, LONGEST:, :]))

    def out_copy(h, j):
        to = lax.rem(me + j, n_mp)
        hs = pl.ds(h * HEAD, HEAD)
        return pltpu.make_async_remote_copy(
            src_ref=obuf.at[to, hs, :], dst_ref=land.at[j, hs, :],
            send_sem=os_sem.at[h, j], recv_sem=or_sem.at[h, j],
            device_id=(me_dp, to), device_id_type=MESH,
        )

    def late(what, h):
        a, b = ((ut, ut_out), (p2, p2_out))[what]
        return pltpu.make_async_copy(a.at[h], b.at[h], late_sem.at[what, h])

    def keep_p(h, c, act):
        @pl.when(c < full)
        def _():
            rows = pl.ds(pl.multiple_of(c * own, own), own)
            act(pltpu.make_async_copy(pbuf.at[h, rows], p.at[h, rows], psem.at[h, c]))

        @pl.when(c == full)
        def _():
            rows = pl.ds(full * own, rest)
            act(pltpu.make_async_copy(pbuf.at[h, rows], p.at[h, rows], psem.at[h, c]))

    pump = [
        (0, 0, 2, 0), (0, 1, 0, 0), (1, 0, 2, 1), (1, 1, 0, 1), (3, 1, 1, 0), (4, 2, 0, 0),
        (5, 1, 1, 1), (6, 2, 0, 1), (7, 1, 2, 0), (8, 1, 2, 1), (9, 2, 1, 0), (10, 2, 1, 1),
        (11, 2, 2, 0),
    ]
    for h in range(heads):
        sl = slope[h]

        def chunk(j, _):
            c = lax.rem(me + 1 + j, n_mp)

            @pl.when(c < full)
            def _():
                for half in range(own // QB):
                    score_block(h, c, half * QB, QB, sl)

            @pl.when(c == full)
            def _():
                score_block(h, c, 0, rest, sl)
                short_block(h, c, sl)

            keep_p(h, c, lambda copy: copy.start())

            @pl.when(j < n_mp - 1)
            def _():
                out_copy(h, j + 1).start()

            for when, step, stage, half in pump:
                if when // n_mp == h:

                    @pl.when(j == when % n_mp)
                    def _():
                        both_ways(step, stage, half)

            return 0

        lax.fori_loop(0, n_mp, chunk, 0)
        late(0, h).start()
        late(1, h).start()

    both_ways(2, 2, 1)
    attnt[me] = obuf[me]
    for h in range(heads):
        hs = slice(h * HEAD, (h + 1) * HEAD)
        for j in range(1, n_mp):
            out_copy(h, j).wait_recv()
            attnt[lax.rem(me - j + n_mp, n_mp), hs, :] = land[j, hs, :]
    for h in range(heads):
        for j in range(1, n_mp):
            out_copy(h, j).wait_send()
        for c in range(n_mp):
            keep_p(h, c, lambda copy: copy.wait())
        late(0, h).wait()
        late(1, h).wait()
    for c in early:
        c.wait()
    for c in send1 + send2:
        c.wait_send()
    for step in range(n_mp - 1):
        for way in range(2):

            @pl.when(sends(way, step))
            def _():
                if step < n_mp - 2:
                    for k in range(PIECES):
                        hidden(way, step, k).wait_send()
                for m in range(4):
                    weight_z(way, step, m).wait_send()

    weight_stage(0, 3, 1)
    for half in range(2):
        weight_stage(0, 4, half)
        for step in range(n_mp - 1):
            both_ways(step, 3, half)
            both_ways(step, 4, half)


def back(
    n_dp, n_mp,
    gt, xt, qt, kp, vte, ut, p, p2, weights, dsum1, sin, gw, gwo,
    grad_in, gq, small, ggu, gdown, gout,
    gl, pbuf, dkt, dvt, dbuf, dland, wfull, gbuf, qland, ssum, slot1, slot2,
    pair, cland, xland, zsum, zland, opair, ocland, oxland, ozsum, ozland,
    gs_sem, gr_sem, qs_sem, qr_sem, ds_sem, dr_sem, ws_sem, wr_sem, s1s, s1r, s2s, s2r,
    psem, wsem, ls_sem, cs_sem, cr_sem, xs_sem, xr_sem, zs_sem, zr_sem,
):
    me_dp, me = lax.axis_index("dp"), lax.axis_index("mp")
    own = gt.shape[2]
    cols = gt.shape[1]
    heads = cols // HEAD
    group = own * n_mp
    tail = group - LONGEST
    full = LONGEST // own
    rest = LONGEST - full * own
    wrows = gq.shape[1]

    def across_mp(j, src, dst, ss, rs):
        to = lax.rem(me + j, n_mp)
        return pltpu.make_async_remote_copy(
            src_ref=src, dst_ref=dst, send_sem=ss, recv_sem=rs,
            device_id=(me_dp, to), device_id_type=MESH,
        )

    def across_dp(j, src, dst, ss, rs):
        to = lax.rem(me_dp + j, n_dp)
        return pltpu.make_async_remote_copy(
            src_ref=src, dst_ref=dst, send_sem=ss, recv_sem=rs,
            device_id=(to, me), device_id_type=MESH,
        )

    def fetch_p(h, j, act):
        c = lax.rem(me - j + n_mp, n_mp)
        slot = lax.rem(h * n_mp + j, 2)

        @pl.when(c < full)
        def _():
            rows = pl.ds(pl.multiple_of(c * own, own), own)
            act(pltpu.make_async_copy(p.at[h, rows, :], pbuf.at[slot], psem.at[slot]))

        @pl.when(c == full)
        def _():
            src = p.at[h, pl.ds(full * own, rest), :]
            act(pltpu.make_async_copy(src, pbuf.at[slot, pl.ds(0, rest), :], psem.at[slot]))

    start, wait = lambda copy: copy.start(), lambda copy: copy.wait()
    fetch_p(0, 0, start)
    fetch_w = pltpu.make_async_copy(weights.at[3], wfull, wsem)

    n_q = n_dp // 2
    me_q, me_c = me_dp // 2, lax.rem(me_dp, 2)
    other = me_dp + 1 - 2 * me_c
    kinds = ((gw, pair, cland, xland, zsum, zland), (gwo, opair, ocland, oxland, ozsum, ozland))

    def rank_of(o):
        return lax.rem(me + 1 + o, n_mp)

    def load_copy(o, t):
        src, own_part = kinds[t][:2]
        return pltpu.make_async_copy(
            src.at[rank_of(o), :, :, me_c], own_part.at[o], ls_sem.at[o, t]
        )

    def pair_up(o, t):
        src, land = kinds[t][0], kinds[t][2]
        return pltpu.make_async_remote_copy(
            src_ref=src.at[rank_of(o), :, :, 1 - me_c], dst_ref=land.at[o],
            send_sem=cs_sem.at[o, t], recv_sem=cr_sem.at[o, t],
            device_id=(other, me), device_id_type=MESH,
        )

    def cross(o, j, t):
        src, land = kinds[t][1], kinds[t][3]
        to = lax.rem(me_q + j, n_q)
        return pltpu.make_async_remote_copy(
            src_ref=src.at[o, :, to], dst_ref=land.at[o, j - 1],
            send_sem=xs_sem.at[o, j, t], recv_sem=xr_sem.at[o, j, t],
            device_id=(to * 2 + me_c, me), device_id_type=MESH,
        )

    def along(o, t):
        src, land = kinds[t][4:]
        return pltpu.make_async_remote_copy(
            src_ref=src.at[o], dst_ref=land.at[o],
            send_sem=zs_sem.at[o, t], recv_sem=zr_sem.at[o, t],
            device_id=(me_dp, rank_of(o)), device_id_type=MESH,
        )

    def add_pair(o):
        for t in range(2):
            own_part, land = kinds[t][1], kinds[t][2]
            load_copy(o, t).wait()
            pair_up(o, t).wait_recv()
            mats = own_part.shape[1]

            def add(i, _):
                a = own_part[o, i // n_q, lax.rem(i, n_q)].astype(F32)
                b = land[o, i // n_q, lax.rem(i, n_q)].astype(F32)
                own_part[o, i // n_q, lax.rem(i, n_q)] = (a + b).astype(BF)
                return 0

            lax.fori_loop(0, mats * n_q, add, 0)
            for j in range(1, n_q):
                cross(o, j, t).start()

    def add_cross(o):
        for t in range(2):
            own_part, land, total = kinds[t][1], kinds[t][3], kinds[t][4]
            for j in range(1, n_q):
                cross(o, j, t).wait_recv()
            for m in range(own_part.shape[1]):
                a = own_part[o, m, me_q].astype(F32)
                for j in range(1, n_q):
                    a += land[o, j - 1, m].astype(F32)
                total[o, m] = a.astype(BF)
            if o < n_mp - 1:
                along(o, t).start()

    for o in range(n_mp):
        for t in range(2):
            load_copy(o, t).start()

    greet(n_dp, n_mp, me_dp, me)

    def grad_copy(h, j):
        hs = pl.ds(h * HEAD, HEAD)
        to = lax.rem(me + j, n_mp)
        return across_mp(
            j, gt.at[to, hs, :], gl.at[j, hs, :], gs_sem.at[h, j], gr_sem.at[h, j]
        )

    for h in range(heads):
        for j in range(1, n_mp):
            grad_copy(h, j).start()
    for o in range(n_mp):
        for t in range(2):
            pair_up(o, t).start()
    fetch_w.start()
    gl[0] = gt[me]

    def query_copy(h, j):
        to = lax.rem(me - j + n_mp, n_mp)
        hs = pl.ds(h * HEAD, HEAD)
        return pltpu.make_async_remote_copy(
            src_ref=dbuf.at[to, 0, hs, :], dst_ref=dland.at[j, 0, hs, :],
            send_sem=qs_sem.at[h, j], recv_sem=qr_sem.at[h, j],
            device_id=(me_dp, to), device_id_type=MESH,
        )

    def pair_copy(h, j):
        to = lax.rem(me - j + n_mp, n_mp)
        hs = pl.ds(h * HEAD, HEAD)
        return pltpu.make_async_remote_copy(
            src_ref=dbuf.at[to, pl.ds(1, 2), hs, :], dst_ref=dland.at[j, pl.ds(1, 2), hs, :],
            send_sem=ds_sem.at[h, j], recv_sem=dr_sem.at[h, j],
            device_id=(me_dp, to), device_id_type=MESH,
        )

    def block(h, j, c, place, rows, pb, keys, add):
        row = c * own + place
        at = pl.ds(pl.multiple_of(row, 128), rows)
        hs = slice(h * HEAD, (h + 1) * HEAD)
        uu = ut[h, :, at]
        inv = 1.0 / uu[HEAD : HEAD + 1]
        gg = gl[j, hs, pl.ds(place, rows)].astype(F32) * inv
        total = jnp.sum(gg * uu[:HEAD], axis=0, keepdims=True) * inv
        high = total.astype(BF).astype(F32)
        low = total - high
        index = lax.broadcasted_iota(jnp.int32, (HEAD, rows), 0)
        extra = jnp.where(index == 0, high, jnp.where(index == 1, low, 0.0))
        gext = jnp.concatenate([gg, extra], axis=0).T.astype(BF)
        dp = dot(gext, vte[h, :, keys])
        ds = (pb.astype(F32) * dp).astype(BF)
        dq = dot(ds, kp[h, keys, :]).T[:HEAD] * (HEAD**-0.5)
        dbuf[c, 0, hs, pl.ds(place, rows)] = dq.astype(BF)
        dk = dot(qt[hs, at], ds)
        dv = dot(gg.astype(BF), pb)
        if add:
            dkt[:, keys] = dkt[:, keys] + dk
            dvt[:, keys] = dvt[:, keys] + dv
        else:
            dkt[:, keys] = dk
            dvt[:, keys] = dv

    pump = [1 + o for o in range(n_mp)]
    for h in range(heads):
        hs = slice(h * HEAD, (h + 1) * HEAD)
        dkt[:, :LONGEST] = jnp.zeros((HEAD, LONGEST), F32)
        dvt[:, :LONGEST] = jnp.zeros((HEAD, LONGEST), F32)

        def chunk(j, _):
            c = lax.rem(me - j + n_mp, n_mp)
            slot = lax.rem(h * n_mp + j, 2)

            @pl.when(j < n_mp - 1)
            def _():
                fetch_p(h, j + 1, start)

            if h < heads - 1:

                @pl.when(j == n_mp - 1)
                def _():
                    fetch_p(h + 1, 0, start)

            @pl.when(j > 0)
            def _():
                grad_copy(h, j).wait_recv()

            fetch_p(h, j, wait)

            keys = slice(0, LONGEST)

            @pl.when(c < full)
            def _():
                for half in range(own // QB):
                    at = pl.ds(half * QB, QB)
                    block(h, j, c, half * QB, QB, pbuf[slot, at, :], keys, True)

            @pl.when(c == full)
            def _():
                block(h, j, c, 0, rest, pbuf[slot, :rest, :], keys, True)
                block(h, j, c, rest, tail, p2[h], slice(LONGEST, group), False)

            @pl.when(j > 0)
            def _():
                query_copy(h, j).start()

            for o in range(n_mp):
                if pump[o] // n_mp == h:

                    @pl.when(j == pump[o] % n_mp)
                    def _():
                        add_pair(o)

            return 0

        lax.fori_loop(0, n_mp, chunk, 0)
        if h == heads - 1:
            add_cross(0)
        for c in range(n_mp):
            dbuf[c, 1, hs, :] = dkt[:, c * own : (c + 1) * own].astype(BF)
            dbuf[c, 2, hs, :] = dvt[:, c * own : (c + 1) * own].astype(BF)
        for j in range(1, n_mp):
            pair_copy(h, j).start()

    ones = jnp.ones((8, own), BF)
    sq = jnp.zeros((8, cols), F32)
    sv = jnp.zeros((8, cols), F32)
    for c in range(n_mp):
        sq += dot_nt(ones, dbuf[c, 0])
        sv += dot_nt(ones, dbuf[c, 2])
    ssum[...] = sin[...]
    for r in range(n_mp):

        @pl.when(me == r)
        def _():
            ssum[0:1, r * cols : (r + 1) * cols] = sq[0:1]
            ssum[1:2, r * cols : (r + 1) * cols] = sv[0:1]

    send1 = [across_mp(j, ssum, slot1.at[j], s1s.at[j], s1r.at[j]) for j in range(1, n_mp)]
    for c in send1:
        c.start()

    total = jnp.zeros((xt.shape[0], 3 * cols), F32)
    for c in range(n_mp):
        total += dot_nt(xt[:, c * own : (c + 1) * own], dbuf[c].reshape(3 * cols, own))
    for d in range(n_dp):
        gbuf[d] = total[d * wrows : (d + 1) * wrows].astype(BF)

    def weight_copy(j):
        to = lax.rem(me_dp + j, n_dp)
        return across_dp(j, gbuf.at[to], qland.at[j], ws_sem.at[j], wr_sem.at[j])

    for j in range(1, n_dp):
        weight_copy(j).start()

    add_cross(1)
    for c in send1:
        c.wait_send()
        c.wait_recv()
    total = ssum[...]
    for j in range(1, n_mp):
        total += slot1[j]
    ssum[...] = total
    send2 = [across_dp(j, ssum, slot2.at[j], s2s.at[j], s2r.at[j]) for j in range(1, n_dp)]
    for c in send2:
        c.start()

    fetch_w.wait()
    into = dot(wfull[me, :, : 3 * cols], dbuf[me].reshape(3 * cols, own))
    for j in range(1, n_mp):
        for h in range(heads):
            query_copy(h, j).wait_recv()
            pair_copy(h, j).wait_recv()
        r = lax.rem(me + j, n_mp)
        into += dot(wfull[r, :, : 3 * cols], dland[j].reshape(3 * cols, own))
    grad_in[...] = (dsum1[...] + into.T).astype(BF)

    for o in range(2, n_mp):
        add_cross(o)
    total = gbuf[me_dp].astype(F32)
    for j in range(1, n_dp):
        weight_copy(j).wait_recv()
        total += qland[j].astype(F32)
    for s in range(3):
        gq[s] = total[:, s * cols : (s + 1) * cols]
    total = ssum[...]
    for c in send2:
        c.wait_recv()
    for j in range(1, n_dp):
        total += slot2[j]
    small[...] = total
    for t in range(2):
        total, land = kinds[t][4:]
        for o in range(n_mp - 1):
            along(o, t).wait_recv()
        for m in range(total.shape[1]):
            a = total[n_mp - 1, m].astype(F32)
            for o in range(n_mp - 1):
                a += land[o, m].astype(F32)
            if t == 1:
                gout[...] = a.T
            elif m == 2:
                gdown[...] = a
            else:
                ggu[m] = a
    for t in range(2):
        for o in range(n_mp):
            pair_up(o, t).wait_send()
            for j in range(1, n_q):
                cross(o, j, t).wait_send()
            if o < n_mp - 1:
                along(o, t).wait_send()
    for c in send2:
        c.wait_send()
    for j in range(1, n_dp):
        weight_copy(j).wait_send()
    for h in range(heads):
        for j in range(1, n_mp):
            grad_copy(h, j).wait_send()
            query_copy(h, j).wait_send()
            pair_copy(h, j).wait_send()


def norm_parts(r):
    centre = r - jnp.mean(r, axis=-1, keepdims=True)
    spread = jnp.mean(centre * centre, axis=-1, keepdims=True)
    rstd = lax.rsqrt(spread + 1e-05)
    return centre * rstd, rstd


def norm_back(dn, n, rstd):
    return rstd * (
        dn - jnp.mean(dn, axis=-1, keepdims=True) - n * jnp.mean(dn * n, axis=-1, keepdims=True)
    )


def colsum(a):
    return jnp.sum(a, axis=0, keepdims=True)


def flip(a):
    return a.astype(F32).T.astype(BF)


GELU_C = 0.7978845608
GELU_A = 0.044715


def middle(
    attn, x, cot, wlast, small, w,
    result, dsum1, dattn, gw, gwout, gsmall,
    wout, mid, midb, midt, gate, up, y, dffn, dffnt, dmid,
):
    i = pl.program_id(0)
    n = pl.num_programs(0) // 2
    parts, cols = attn.shape[0], attn.shape[1]

    @pl.when(i == 0)
    def _():
        branch = jnp.zeros((x.shape[1], x.shape[0]), F32)
        for r in range(parts):
            wout[r] = wlast[0, r, :, 3 * cols :]
            branch += dot(wout[r], attn[r])
        branch = branch.T + x[...].astype(F32) + small[2:3, :]
        nn, _ = norm_parts(branch)
        m = nn * small[3:4, :] + small[4:5, :]
        dsum1[...] = branch
        mid[...] = m
        midb[...] = m.astype(BF)
        midt[...] = m.T.astype(BF)
        y[...] = jnp.zeros_like(y)

    @pl.when(i < n)
    def _():
        mb = midb[...]
        ga = dot(mb, w[0, 0]) + small[pl.ds(8 + i, 1), :]
        u = dot(mb, w[1, 0]) + small[pl.ds(8 + n + i, 1), :]
        gate[i] = ga
        up[i] = u
        t = jnp.tanh(GELU_C * (ga + GELU_A * ga * ga * ga))
        act = (0.5 * ga * (1.0 + t) * u).astype(BF)
        y[...] += dot_nt(act, w[2, 0])

    @pl.when(i == n - 1)
    def _():
        r = mid[...] + y[...] + small[5:6, :]
        nn, rstd = norm_parts(r)
        gain = small[6:7, :]
        result[...] = (nn * gain + small[7:8, :]).astype(BF)
        c = cot[...].astype(F32)
        ds = norm_back(c * gain, nn, rstd)
        gsmall[6:7, :] = colsum(c * nn)
        gsmall[7:8, :] = colsum(c)
        dmid[...] = ds
        db = ds.astype(BF)
        dffn[...] = db
        dffnt[...] = ds.T.astype(BF)
        gsmall[5:6, :] = colsum(db.astype(F32))
        gsmall[0:2, :] = jnp.zeros_like(gsmall[0:2, :])

    @pl.when(i >= n)
    def _():
        k = 2 * n - 1 - i
        ga = gate[k]
        u = up[k]
        sq = ga * ga
        t = jnp.tanh(GELU_C * (ga + GELU_A * ga * sq))
        half = 0.5 * (1.0 + t)
        gelu = ga * half
        slope = half + (0.5 * GELU_C) * ga * (1.0 - t * t) * (1.0 + 3.0 * GELU_A * sq)
        act = (gelu * u).astype(BF)
        dact = dot(dffn[...], w[2, 0])
        gw[0, 2] = dot(dffnt[...], act).astype(BF)
        dga = (dact * u * slope).astype(BF)
        du = (dact * gelu).astype(BF)
        gsmall[pl.ds(8 + k, 1), :] = colsum(dga.astype(F32))
        gsmall[pl.ds(8 + n + k, 1), :] = colsum(du.astype(F32))
        gw[0, 0] = dot(midt[...], dga).astype(BF)
        gw[0, 1] = dot(midt[...], du).astype(BF)
        dmid[...] += dot_nt(dga, w[0, 0]) + dot_nt(du, w[1, 0])

    @pl.when(i == 2 * n - 1)
    def _():
        nn, rstd = norm_parts(dsum1[...])
        dm = dmid[...]
        gsmall[3:4, :] = colsum(dm * nn)
        gsmall[4:5, :] = colsum(dm)
        ds = norm_back(dm * small[3:4, :], nn, rstd)
        dsum1[...] = ds
        db = ds.astype(BF)
        gsmall[2:3, :] = colsum(db.astype(F32))
        dbt = ds.T.astype(BF)
        for r in range(parts):
            dattn[r] = dot(db, wout[r]).T.astype(BF)
            gwout[r] = dot_nt(dbt, attn[r]).astype(BF)


def hand_on(*refs):
    n = len(refs) // 2
    for a, b in zip(refs[:n], refs[n:]):
        b[...] = a[...]


def head_slopes(first_head, head_count):
    number = first_head + jnp.arange(head_count, dtype=jnp.int32)
    exponent = jnp.where(number < 8, number.astype(F32) + 1.0, number.astype(F32) - 7.5)
    return jnp.exp2(-exponent)


def cost(flops):
    return pl.CostEstimate(flops=flops, bytes_accessed=1 << 24, transcendentals=0)


def params(**kw):
    return pltpu.CompilerParams(vmem_limit_bytes=VMEM_LIMIT, **kw)


def per_device(
    hidden_in, lengths, w_qkv, b_qv, w_out, b_out, ln1_gain, ln1_bias, w_gu, b_gu, w_down,
    b_down, ln2_gain, ln2_bias, cotangent,
):
    both = ("dp", "mp")
    n_dp, n_mp = lax.axis_size("dp"), lax.axis_size("mp")
    n = n_dp * n_mp
    mp_rank = lax.axis_index("mp")
    own, width = hidden_in.shape
    group = own * n_mp
    sds = jax.ShapeDtypeStruct

    dev = lax.axis_index("dp") * n_mp + mp_rank

    def placed(a):
        zero = jnp.zeros((a.shape[0], a.shape[1] * n), F32)
        return lax.dynamic_update_slice_in_dim(zero, a, dev * a.shape[1], 1)

    vectors = jnp.stack([b_out, ln1_gain, ln1_bias, b_down, ln2_gain, ln2_bias])
    vectors = jnp.concatenate([b_qv, vectors], axis=0)
    small_own = jnp.concatenate(
        [placed(vectors), placed(b_gu).reshape(-1, width)], axis=0
    )
    srows = small_own.shape[0]

    wrows, cols = w_qkv.shape[1], w_qkv.shape[2]
    ff_part = w_gu.shape[2]
    heads = cols // HEAD
    tail = group - LONGEST

    n_q = n_dp // 2
    units = 2 * n_mp - 1

    slopes = head_slopes(mp_rank * heads, heads)
    dma = pltpu.SemaphoreType.DMA

    small, xt, qt, kp, vte, ut, attn, p, p2, weights = pl.pallas_call(
        functools.partial(front, n_dp, n_mp),
        out_shape=(
            sds((srows, width), F32),
            sds((width, group), BF),
            sds((cols, group), BF),
            sds((heads, group, 2 * HEAD), BF),
            sds((heads, 2 * HEAD, group), BF),
            sds((heads, 2 * HEAD, group), F32),
            sds((n_mp, cols, own), BF),
            sds((heads, LONGEST, LONGEST), BF),
            sds((heads, tail, tail), BF),
            sds((4, n_mp, n_q, 2, wrows, ff_part), BF),
        ),
        in_specs=[vmem(), vmem(), vmem(), vmem(), vmem(), vmem(), smem(), smem()],
        out_specs=(
            vmem(), hbm(), hbm(), hbm(), hbm(), hbm(), vmem(), hbm(), hbm(), hbm(),
        ),
        scratch_shapes=[
            pltpu.VMEM((4, wrows, ff_part), BF),
            pltpu.VMEM((width, group), BF),
            pltpu.VMEM((cols, group), BF),
            pltpu.VMEM((heads, group, 2 * HEAD), BF),
            pltpu.VMEM((heads, 2 * HEAD, group), BF),
            pltpu.VMEM((heads, 2 * HEAD, group), F32),
            pltpu.VMEM((heads, tail, tail), BF),
            pltpu.VMEM((n_mp, own, width), BF),
            pltpu.VMEM((n_q, 2, wrows, ff_part), BF),
            pltpu.VMEM((3, width, cols), F32),
            pltpu.VMEM((3, width, cols), BF),
            pltpu.VMEM((n_mp, srows, width), F32),
            pltpu.VMEM((srows, width), F32),
            pltpu.VMEM((n_dp, srows, width), F32),
            pltpu.VMEM((8, cols), F32),
            pltpu.VMEM((group, cols), BF),
            pltpu.VMEM((cols, group), BF),
            pltpu.VMEM((heads, group, 2 * HEAD), BF),
            pltpu.VMEM((QB, LONGEST + LONGEST // QB * QB), F32),
            pltpu.VMEM((heads, LONGEST, LONGEST), BF),
            pltpu.VMEM((n_mp, cols, own), BF),
            pltpu.VMEM((n_mp, cols, own), BF),
            dma((2, n_mp - 1, PIECES)),
            dma((2, n_mp - 1, PIECES)),
            dma((n_mp,)),
            dma((n_mp,)),
            dma((n_dp,)),
            dma((n_dp,)),
            dma((heads, n_mp)),
            dma((heads, n_mp)),
            dma((heads, n_mp)),
            dma((2,)),
            dma((4,)),
            dma((2, heads)),
            dma((2, n_mp - 1, 4)),
            dma((2, n_mp - 1, 4)),
            dma((units, 4, n_q)),
            dma((units, 4, n_q)),
            dma((units, 2, n_q)),
            dma((units, 2, n_q)),
        ],
        compiler_params=params(collective_id=0, has_side_effects=True),
        cost_estimate=cost(11 * LONGEST * LONGEST * HEAD * heads * 12),
        name="front",
    )(hidden_in, w_qkv, w_out, w_gu, w_down.T, small_own, slopes, lengths)
    weights = weights.reshape(4, n_mp, width, ff_part)

    fixed = lambda *s: pl.BlockSpec(s, lambda i: (0,) * len(s))
    walk = lambda i: jnp.where(i < n_mp, i, 2 * n_mp - 1 - i)
    late = lambda i: jnp.where(i < n_mp, n_mp - 1, 2 * n_mp - 1 - i)
    result, dsum1, dattn, gw, gwout, gsmall = pl.pallas_call(
        middle,
        grid=(2 * n_mp,),
        out_shape=(
            sds((own, width), BF),
            sds((own, width), F32),
            sds((n_mp, cols, own), BF),
            sds((n_mp, 3, width, ff_part), BF),
            sds((n_mp, width, cols), BF),
            sds((srows, width), F32),
        ),
        in_specs=[
            fixed(n_mp, cols, own),
            fixed(own, width),
            fixed(own, width),
            pl.BlockSpec(
                (1, n_mp, width, ff_part),
                lambda i: (3, 0, 0, 0),
                pipeline_mode=pl.Buffered(1),
            ),
            fixed(srows, width),
            pl.BlockSpec((3, 1, width, ff_part), lambda i: (0, walk(i), 0, 0)),
        ],
        out_specs=(
            fixed(own, width),
            fixed(own, width),
            fixed(n_mp, cols, own),
            pl.BlockSpec((1, 3, width, ff_part), lambda i: (late(i), 0, 0, 0)),
            fixed(n_mp, width, cols),
            fixed(srows, width),
        ),
        scratch_shapes=[
            pltpu.VMEM((n_mp, width, cols), BF),
            pltpu.VMEM((own, width), F32),
            pltpu.VMEM((own, width), BF),
            pltpu.VMEM((width, own), BF),
            pltpu.VMEM((n_mp, own, ff_part), F32),
            pltpu.VMEM((n_mp, own, ff_part), F32),
            pltpu.VMEM((own, width), F32),
            pltpu.VMEM((own, width), BF),
            pltpu.VMEM((width, own), BF),
            pltpu.VMEM((own, width), F32),
        ],
        compiler_params=params(),
        name="middle",
    )(attn, hidden_in, cotangent, weights, small, weights)

    gw = gw.reshape(n_mp, 3, n_q, 2, wrows, ff_part)
    gwout = gwout.reshape(n_mp, 1, n_q, 2, wrows, cols)
    grad_in, gqkv, gsmall, ggu, gdown, gout = pl.pallas_call(
        functools.partial(back, n_dp, n_mp),
        out_shape=(
            sds((own, width), BF),
            sds((3, wrows, cols), F32),
            sds((srows, width), F32),
            sds((2, wrows, ff_part), F32),
            sds((wrows, ff_part), F32),
            sds((cols, wrows), F32),
        ),
        in_specs=[
            vmem(), vmem(), vmem(), vmem(), vmem(), vmem(), hbm(), vmem(), hbm(), vmem(), vmem(),
            hbm(), hbm(),
        ],
        out_specs=(vmem(), vmem(), vmem(), vmem(), vmem(), vmem()),
        scratch_shapes=[
            pltpu.VMEM((n_mp, cols, own), BF),
            pltpu.VMEM((2, own, LONGEST), BF),
            pltpu.VMEM((HEAD, group), F32),
            pltpu.VMEM((HEAD, group), F32),
            pltpu.VMEM((n_mp, 3, cols, own), BF),
            pltpu.VMEM((n_mp, 3, cols, own), BF),
            pltpu.VMEM((n_mp, width, ff_part), BF),
            pltpu.VMEM((n_dp, wrows, 3 * cols), BF),
            pltpu.VMEM((n_dp, wrows, 3 * cols), BF),
            pltpu.VMEM((srows, width), F32),
            pltpu.VMEM((n_mp, srows, width), F32),
            pltpu.VMEM((n_dp, srows, width), F32),
            pltpu.VMEM((n_mp, 3, n_q, wrows, ff_part), BF),
            pltpu.VMEM((n_mp, 3, n_q, wrows, ff_part), BF),
            pltpu.VMEM((n_mp, n_q - 1, 3, wrows, ff_part), BF),
            pltpu.VMEM((n_mp, 3, wrows, ff_part), BF),
            pltpu.VMEM((n_mp - 1, 3, wrows, ff_part), BF),
            pltpu.VMEM((n_mp, 1, n_q, wrows, cols), BF),
            pltpu.VMEM((n_mp, 1, n_q, wrows, cols), BF),
            pltpu.VMEM((n_mp, n_q - 1, 1, wrows, cols), BF),
            pltpu.VMEM((n_mp, 1, wrows, cols), BF),
            pltpu.VMEM((n_mp - 1, 1, wrows, cols), BF),
            dma((heads, n_mp)),
            dma((heads, n_mp)),
            dma((heads, n_mp)),
            dma((heads, n_mp)),
            dma((heads, n_mp)),
            dma((heads, n_mp)),
            dma((n_dp,)),
            dma((n_dp,)),
            dma((n_mp,)),
            dma((n_mp,)),
            dma((n_dp,)),
            dma((n_dp,)),
            dma((2,)),
            dma,
            dma((n_mp, 2)),
            dma((n_mp, 2)),
            dma((n_mp, 2)),
            dma((n_mp, n_q, 2)),
            dma((n_mp, n_q, 2)),
            dma((n_mp - 1, 2)),
            dma((n_mp - 1, 2)),
        ],
        compiler_params=params(collective_id=1, has_side_effects=True),
        cost_estimate=cost(11 * LONGEST * LONGEST * HEAD * heads * 12),
        name="back",
    )(dattn, xt, qt, kp, vte, ut, p, p2, weights, dsum1, gsmall, gw, gwout)

    finished = (grad_in, gqkv, ggu, gdown, gout)
    grad_in, gqkv, ggu, gdown, gout = pl.pallas_call(
        hand_on,
        out_shape=tuple(sds(a.shape, a.dtype) for a in finished),
        in_specs=[vmem()] * len(finished),
        out_specs=(vmem(),) * len(finished),
        compiler_params=params(),
        name="hand_on",
    )(*finished)

    def own_columns(a):
        part = a.shape[1] // n
        return lax.dynamic_slice_in_dim(a, dev * part, part, 1)

    gs = own_columns(gsmall[:8])
    g_gu = own_columns(gsmall[8:].reshape(2, -1))

    return (
        result,
        grad_in,
        gqkv,
        gs[0:2],
        gout,
        gs[2],
        gs[3],
        gs[4],
        ggu,
        g_gu,
        gdown.T,
        gs[5],
        gs[6],
        gs[7],
    )


def solution(mesh):
    rows = P(("dp", "mp"), None)
    vec = P(("dp", "mp"))
    vecs = P(None, ("dp", "mp"))
    wide = P(None, "dp", "mp")
    tall = P("mp", "dp")
    return jax.shard_map(
        per_device,
        mesh=mesh,
        in_specs=(
            rows, P("dp", None), wide, vecs, tall, vec, vec, vec, wide, vecs, tall, vec, vec, vec,
            rows,
        ),
        out_specs=(
            rows, rows, wide, vecs, tall, vec, vec, vec, wide, vecs, tall, vec, vec, vec,
        ),
        check_vma=False,
    )
```

```python
import functools

import jax
import jax.numpy as jnp
from jax import lax
from jax.experimental import pallas as pl
from jax.experimental.pallas import tpu as pltpu
from jax.sharding import PartitionSpec as P

HEAD = 64
LONGEST = 1664
QB = 256
BF = jnp.bfloat16
F32 = jnp.float32
VMEM_LIMIT = 60 * 1024 * 1024


def dot(a, b):
    return lax.dot_general(a, b, (((1,), (0,)), ((), ())), preferred_element_type=F32)


def dot_nt(a, b):
    return lax.dot_general(a, b, (((1,), (1,)), ((), ())), preferred_element_type=F32)


def vmem():
    return pl.BlockSpec(memory_space=pltpu.VMEM)


def smem():
    return pl.BlockSpec(memory_space=pltpu.SMEM)


def hbm():
    return pl.BlockSpec(memory_space=pl.ANY)


MESH = pl.DeviceIdType.MESH
PIECES = 4


def greet(n_dp, n_mp, me_dp, me_mp, meanwhile=lambda: None):
    barrier = pltpu.get_barrier_semaphore()
    for j in range(1, n_mp):
        pl.semaphore_signal(
            barrier, 1, device_id=(me_dp, lax.rem(me_mp + j, n_mp)), device_id_type=MESH
        )
    for j in range(1, n_dp):
        pl.semaphore_signal(
            barrier, 1, device_id=(lax.rem(me_dp + j, n_dp), me_mp), device_id_type=MESH
        )
    meanwhile()
    pl.semaphore_wait(barrier, n_mp - 1 + n_dp - 1)


def front(
    n_dp, n_mp,
    x, wqkv, wout, wgu, wdown, sin, slope, length,
    small, xt_out, qt_out, kp_out, vte_out, ut_out, attnt, p, p2_out, wall,
    pack, xt, qt, kp, vte, ut, p2, hid, wslot, wf, wb, slot1, ssum, slot2, bias, qs, kt, vext, dist, pbuf, obuf, land,
    hs_sem, hr_sem, s1s, s1r, s2s, s2r, os_sem, or_sem, psem,
    local_sem, early_sem, late_sem, wzs, wzr, wqs, wqr, wps, wpr,
):
    me_dp, me = lax.axis_index("dp"), lax.axis_index("mp")
    own = x.shape[0]
    group = own * n_mp
    wrows, cols = pack.shape[1], wb.shape[2]
    heads = cols // HEAD
    tail = group - LONGEST
    full = LONGEST // own
    rest = LONGEST - full * own
    piece = own // PIECES

    def across_mp(j, src, dst, ss, rs):
        to = lax.rem(me + j, n_mp)
        return pltpu.make_async_remote_copy(
            src_ref=src, dst_ref=dst, send_sem=ss, recv_sem=rs,
            device_id=(me_dp, to), device_id_type=MESH,
        )

    def across_dp(j, src, dst, ss, rs):
        to = lax.rem(me_dp + j, n_dp)
        return pltpu.make_async_remote_copy(
            src_ref=src, dst_ref=dst, send_sem=ss, recv_sem=rs,
            device_id=(to, me), device_id_type=MESH,
        )

    def make_pack():
        for m in range(2):
            pack[m] = wgu[m].astype(BF)
        pack[2] = wdown[...].astype(BF)
        last = [wqkv[0], wqkv[1], wqkv[2], wout[...].T]
        pack[3] = jnp.concatenate(last, axis=1).astype(BF)

    greet(n_dp, n_mp, me_dp, me, make_pack)

    send1 = [across_mp(j, sin, slot1.at[j], s1s.at[j], s1r.at[j]) for j in range(1, n_mp)]
    send2 = [across_dp(j, ssum, slot2.at[j], s2s.at[j], s2r.at[j]) for j in range(1, n_dp)]
    for c in send1:
        c.start()

    def hidden(way, step, k):
        shard = me - step if way == 0 else me + step
        to = me + 1 if way == 0 else me - 1
        shard, to = jnp.clip(shard, 0, n_mp - 1), jnp.clip(to, 0, n_mp - 1)
        rows = pl.ds(k * piece, piece)
        src = x.at[rows, :] if step == 0 else hid.at[shard, rows, :]
        return pltpu.make_async_remote_copy(
            src_ref=src, dst_ref=hid.at[shard, rows, :],
            send_sem=hs_sem.at[way, step, k], recv_sem=hr_sem.at[way, step, k],
            device_id=(me_dp, to), device_id_type=MESH,
        )

    def sends(way, step):
        if way == 0:
            return (me >= step) & (me < n_mp - 1)
        return (me + step <= n_mp - 1) & (me > 0)

    def receives(way, step):
        return me - 1 - step >= 0 if way == 0 else me + 1 + step <= n_mp - 1

    def send_hidden(step, k):
        for way in range(2):

            @pl.when(sends(way, step))
            def _():
                hidden(way, step, k).start()

    def wait_hidden(step, k):
        for way in range(2):

            @pl.when(receives(way, step))
            def _():
                hidden(way, step, k).wait_recv()

    n_q = n_dp // 2
    me_q, me_c = me_dp // 2, lax.rem(me_dp, 2)
    square = n_q == 4
    halves = ((3, 2), (0, 1))

    def unit_rank(level):
        if level == 0:
            return me
        step, way = (level - 1) // 2, (level - 1) % 2
        return jnp.clip(me - 1 - step if way == 0 else me + 1 + step, 0, n_mp - 1)

    def here(level):
        return True if level == 0 else receives((level - 1) % 2, (level - 1) // 2)

    def mate(j):
        if not square:
            return lax.rem(me_q + j, n_q)
        x1, y1 = lax.rem(me_q, 2), me_q // 2
        x2 = 1 - x1 if j % 2 else x1
        y2 = 1 - y1 if j // 2 else y1
        return 2 * y2 + x2

    def weight_z(way, step, m):
        level = 0 if step == 0 else 1 + 2 * (step - 1) + way
        r = unit_rank(level)
        to = jnp.clip(me + 1 if way == 0 else me - 1, 0, n_mp - 1)
        dst = wall.at[m, r, me_q, me_c]
        src = pack.at[m] if step == 0 else dst
        return pltpu.make_async_remote_copy(
            src_ref=src, dst_ref=dst,
            send_sem=wzs.at[way, step, m], recv_sem=wzr.at[way, step, m],
            device_id=(me_dp, to), device_id_type=MESH,
        )

    def weight_q(level, m, slot):
        r = unit_rank(level)
        j, what = (slot, 0) if slot else ((1, 2) if m % 2 else (2, 1))
        dst = wall.at[m, r, mate(what), me_c]
        src = pack.at[m] if level == 0 and slot else dst
        return pltpu.make_async_remote_copy(
            src_ref=src, dst_ref=dst,
            send_sem=wqs.at[level, m, slot], recv_sem=wqr.at[level, m, slot],
            device_id=(mate(j) * 2 + me_c, me), device_id_type=MESH,
        )

    def weight_p(level, half, j):
        part = pl.ds(min(halves[half]), 2)
        dst = wall.at[part, unit_rank(level), mate(j), me_c]
        src = pack.at[part] if level == 0 and j == 0 else dst
        return pltpu.make_async_remote_copy(
            src_ref=src, dst_ref=dst,
            send_sem=wps.at[level, half, j], recv_sem=wpr.at[level, half, j],
            device_id=(me_q * 2 + 1 - me_c, me), device_id_type=MESH,
        )

    near = (1, 2) if square else tuple(range(1, n_q))
    slots = ((0,) if square else ()) + near

    def weight_on(way, step, m):
        @pl.when(sends(way, step))
        def _():
            weight_z(way, step, m).start()

    def weight_stage(level, stage, half):
        step, way = (level - 1) // 2, (level - 1) % 2

        def run():
            for m in halves[half]:
                if stage == 0:
                    if level > 0:
                        weight_z(way, step, m).wait_recv()
                        if 0 < step < n_mp - 2:
                            weight_on(way, step + 1, m)
                    for j in near:
                        weight_q(level, m, j).start()
                elif stage == 1:
                    if square:
                        weight_q(level, m, 2 if m % 2 else 1).wait_recv()
                        weight_q(level, m, 0).start()
                        weight_q(level, m, 1 if m % 2 else 2).wait_recv()
                    else:
                        for j in near:
                            weight_q(level, m, j).wait_recv()
                elif stage == 2 and square:
                    weight_q(level, m, 0).wait_recv()
                elif stage == 4:
                    for j in slots:
                        weight_q(level, m, j).wait_send()
            if stage == 0:
                weight_p(level, half, 0).start()
            elif stage == 1:
                for j in near:
                    weight_p(level, half, j).start()
            elif stage == 2 and square:
                weight_p(level, half, 3).start()
            elif stage == 3:
                for j in range(n_q):
                    weight_p(level, half, j).wait_recv()
            elif stage == 4:
                for j in range(n_q):
                    weight_p(level, half, j).wait_send()

        if level == 0:
            run()
        else:
            pl.when(here(level))(run)

    def both_ways(step, stage, half):
        for way in range(2):
            weight_stage(1 + 2 * step + way, stage, half)

    for k in range(PIECES):
        send_hidden(0, k)
    for half in range(2):
        for m in halves[half]:
            for way in range(2):
                weight_on(way, 0, m)
        weight_stage(0, 0, half)
    keep = pltpu.make_async_copy(pack, wall.at[:, me, me_q, me_c], local_sem.at[0])
    keep.start()

    width = dist.shape[1]
    base = width - LONGEST
    i = lax.broadcasted_iota(jnp.int32, (QB, width), 0)
    j = lax.broadcasted_iota(jnp.int32, (QB, width), 1)
    dist[...] = jnp.abs(i + base - j).astype(F32)

    total = sin[...]
    for c in send1:
        c.wait_recv()
    for j in range(1, n_mp):
        total += slot1[j]
    ssum[...] = total
    for c in send2:
        c.start()

    for k in range(PIECES):
        wait_hidden(0, k)
        send_hidden(1, k)

    for stage in range(1, 4):
        weight_stage(0, stage, 0)
        if stage == 1:
            weight_stage(0, 1, 1)
    keep.wait()
    fetch = pltpu.make_async_copy(wall.at[3, me], wslot, local_sem.at[1])
    fetch.start()

    for c in send2:
        c.wait_recv()
    total = ssum[...]
    for j in range(1, n_dp):
        total += slot2[j]
    small[...] = total
    bias[...] = jnp.zeros_like(bias)
    for r in range(n_mp):

        @pl.when(me == r)
        def _():
            bias[0:2, :] = total[0:2, r * cols : (r + 1) * cols]

    fetch.wait()
    for j in range(n_dp):
        for s in range(3):
            part = wslot[j // 2, j % 2, :, s * cols : (s + 1) * cols]
            wf[s, j * wrows : (j + 1) * wrows, :] = part.astype(F32)
    for s in range(3):
        wb[s] = wf[s].astype(BF)

    one = jnp.where(lax.broadcasted_iota(jnp.int32, (QB, HEAD), 1) == 0, 1.0, 0.0)
    minus = jnp.where(lax.broadcasted_iota(jnp.int32, (HEAD, QB), 0) < 2, -1.0, 0.0)
    none = jnp.zeros((QB, HEAD), F32)

    def project(ref, shard):
        def part(c, _):
            rows = pl.ds(pl.multiple_of(c * QB, QB), QB)
            at = pl.ds(pl.multiple_of(shard * own + c * QB, QB), QB)
            xc = ref[rows, :]
            xt[:, at] = xc.astype(F32).T.astype(BF)
            q = (dot(xc, wb[0]) + bias[0:1, :]).astype(BF).astype(F32) * HEAD**-0.5
            qs[at, :] = q.astype(BF)
            qt[:, at] = q.T.astype(BF)
            k = dot(xc, wb[1])
            kt[:, at] = k.T.astype(BF)
            v = dot(xc, wb[2]) + bias[1:2, :]
            vt = v.T
            for h in range(heads):
                hs = slice(h * HEAD, (h + 1) * HEAD)
                kp[h, at, :] = jnp.concatenate([k[:, hs], none], axis=1).astype(BF)
                vext[h, at, :] = jnp.concatenate([v[:, hs], one], axis=1).astype(BF)
                vte[h, :, at] = jnp.concatenate([vt[hs], minus], axis=0).astype(BF)
            return 0

        lax.fori_loop(0, own // QB, part, 0)

    project(x, me)
    for half in range(2):
        both_ways(0, 0, half)
    for step in range(n_mp - 1):
        if step > 0:
            for k in range(PIECES):
                wait_hidden(step, k)
                if step < n_mp - 2:
                    send_hidden(step + 1, k)
        if step == n_mp - 2:
            for way in range(2):

                @pl.when(sends(way, step))
                def _():
                    for k in range(PIECES):
                        hidden(way, step, k).wait_send()

                for half in range(2):
                    for m in halves[half]:
                        weight_on(way, 1, m)

        for way in range(2):

            @pl.when(receives(way, step))
            def _():
                shard = me - 1 - step if way == 0 else me + 1 + step
                shard = jnp.clip(shard, 0, n_mp - 1)
                project(hid.at[shard], shard)

        if step == 1:
            weight_stage(0, 2, 1)
            for half in range(2):
                both_ways(0, 1, half)

    early = [
        pltpu.make_async_copy(a, b, early_sem.at[i])
        for i, (a, b) in enumerate(((xt, xt_out), (qt, qt_out), (kp, kp_out), (vte, vte_out)))
    ]
    for c in early:
        c.start()

    def score_block(h, c, place, rows, sl):
        hs = slice(h * HEAD, (h + 1) * HEAD)
        row = c * own + place
        at = pl.ds(pl.multiple_of(row, 128), rows)
        s = dot(qs[at, hs], kt[hs, :LONGEST])
        off = pl.multiple_of(base - row, 128)
        s = s - sl * dist[:rows, pl.ds(off, LONGEST)]
        m = jnp.max(s, axis=1, keepdims=True)
        pb = jnp.exp(s - m).astype(BF)
        pbuf[h, at, :] = pb
        finish(h, c, place, at, rows, dot(pb, vext[h, :LONGEST, :]))

    def finish(h, c, place, at, rows, uu):
        uut = uu.T
        ut[h, :, at] = uut
        oh = uut[:HEAD] * (1.0 / uut[HEAD : HEAD + 1])
        obuf[c, h * HEAD : (h + 1) * HEAD, pl.ds(place, rows)] = oh.astype(BF)

    def short_block(h, c, sl):
        hs = slice(h * HEAD, (h + 1) * HEAD)
        s = dot(qs[LONGEST:, hs], kt[hs, LONGEST:])
        ii = lax.broadcasted_iota(jnp.int32, (tail, tail), 0)
        jj = lax.broadcasted_iota(jnp.int32, (tail, tail), 1)
        s = s - sl * jnp.abs(ii - jj).astype(F32)
        cut = length[0, 1]
        s = jnp.where((ii < cut) == (jj < cut), s, -1e30)
        m = jnp.max(s, axis=1, keepdims=True)
        pb = jnp.exp(s - m).astype(BF)
        p2[h] = pb
        finish(h, c, rest, pl.ds(LONGEST, tail), tail, dot(pb, vext[h, LONGEST:, :]))

    def out_copy(h, j):
        to = lax.rem(me + j, n_mp)
        hs = pl.ds(h * HEAD, HEAD)
        return pltpu.make_async_remote_copy(
            src_ref=obuf.at[to, hs, :], dst_ref=land.at[j, hs, :],
            send_sem=os_sem.at[h, j], recv_sem=or_sem.at[h, j],
            device_id=(me_dp, to), device_id_type=MESH,
        )

    def late(what, h):
        a, b = ((ut, ut_out), (p2, p2_out))[what]
        return pltpu.make_async_copy(a.at[h], b.at[h], late_sem.at[what, h])

    def keep_p(h, c, act):
        @pl.when(c < full)
        def _():
            rows = pl.ds(pl.multiple_of(c * own, own), own)
            act(pltpu.make_async_copy(pbuf.at[h, rows], p.at[h, rows], psem.at[h, c]))

        @pl.when(c == full)
        def _():
            rows = pl.ds(full * own, rest)
            act(pltpu.make_async_copy(pbuf.at[h, rows], p.at[h, rows], psem.at[h, c]))

    pump = [
        (0, 0, 2, 0), (0, 1, 0, 0), (1, 0, 2, 1), (1, 1, 0, 1), (3, 1, 1, 0), (4, 2, 0, 0),
        (5, 1, 1, 1), (6, 2, 0, 1), (7, 1, 2, 0), (8, 1, 2, 1), (9, 2, 1, 0), (10, 2, 1, 1),
        (11, 2, 2, 0),
    ]
    for h in range(heads):
        sl = slope[h]

        def chunk(j, _):
            c = lax.rem(me + 1 + j, n_mp)

            @pl.when(c < full)
            def _():
                for half in range(own // QB):
                    score_block(h, c, half * QB, QB, sl)

            @pl.when(c == full)
            def _():
                score_block(h, c, 0, rest, sl)
                short_block(h, c, sl)

            keep_p(h, c, lambda copy: copy.start())

            @pl.when(j < n_mp - 1)
            def _():
                out_copy(h, j + 1).start()

            for when, step, stage, half in pump:
                if when // n_mp == h:

                    @pl.when(j == when % n_mp)
                    def _():
                        both_ways(step, stage, half)

            return 0

        lax.fori_loop(0, n_mp, chunk, 0)
        late(0, h).start()
        late(1, h).start()

    both_ways(2, 2, 1)
    attnt[me] = obuf[me]
    for h in range(heads):
        hs = slice(h * HEAD, (h + 1) * HEAD)
        for j in range(1, n_mp):
            out_copy(h, j).wait_recv()
            attnt[lax.rem(me - j + n_mp, n_mp), hs, :] = land[j, hs, :]
    for h in range(heads):
        for j in range(1, n_mp):
            out_copy(h, j).wait_send()
        for c in range(n_mp):
            keep_p(h, c, lambda copy: copy.wait())
        late(0, h).wait()
        late(1, h).wait()
    for c in early:
        c.wait()
    for c in send1 + send2:
        c.wait_send()
    for step in range(n_mp - 1):
        for way in range(2):

            @pl.when(sends(way, step))
            def _():
                if step < n_mp - 2:
                    for k in range(PIECES):
                        hidden(way, step, k).wait_send()
                for m in range(4):
                    weight_z(way, step, m).wait_send()

    weight_stage(0, 3, 1)
    for half in range(2):
        weight_stage(0, 4, half)
        for step in range(n_mp - 1):
            both_ways(step, 3, half)
            both_ways(step, 4, half)


def back(
    n_dp, n_mp,
    gt, xt, qt, kp, vte, ut, p, p2, weights, dsum1, sin, gw, gwo,
    grad_in, gq, small, ggu, gdown, gout,
    gl, pbuf, dkt, dvt, dbuf, dland, wfull, gbuf, qland, ssum, slot1, slot2,
    pair, cland, xland, zsum, zland, opair, ocland, oxland, ozsum, ozland,
    gs_sem, gr_sem, qs_sem, qr_sem, ds_sem, dr_sem, ws_sem, wr_sem, s1s, s1r, s2s, s2r,
    psem, wsem, ls_sem, cs_sem, cr_sem, xs_sem, xr_sem, zs_sem, zr_sem,
):
    me_dp, me = lax.axis_index("dp"), lax.axis_index("mp")
    own = gt.shape[2]
    cols = gt.shape[1]
    heads = cols // HEAD
    group = own * n_mp
    tail = group - LONGEST
    full = LONGEST // own
    rest = LONGEST - full * own
    wrows = gq.shape[1]

    def across_mp(j, src, dst, ss, rs):
        to = lax.rem(me + j, n_mp)
        return pltpu.make_async_remote_copy(
            src_ref=src, dst_ref=dst, send_sem=ss, recv_sem=rs,
            device_id=(me_dp, to), device_id_type=MESH,
        )

    def across_dp(j, src, dst, ss, rs):
        to = lax.rem(me_dp + j, n_dp)
        return pltpu.make_async_remote_copy(
            src_ref=src, dst_ref=dst, send_sem=ss, recv_sem=rs,
            device_id=(to, me), device_id_type=MESH,
        )

    def fetch_p(h, j, act):
        c = lax.rem(me - j + n_mp, n_mp)
        slot = lax.rem(h * n_mp + j, 2)

        @pl.when(c < full)
        def _():
            rows = pl.ds(pl.multiple_of(c * own, own), own)
            act(pltpu.make_async_copy(p.at[h, rows, :], pbuf.at[slot], psem.at[slot]))

        @pl.when(c == full)
        def _():
            src = p.at[h, pl.ds(full * own, rest), :]
            act(pltpu.make_async_copy(src, pbuf.at[slot, pl.ds(0, rest), :], psem.at[slot]))

    start, wait = lambda copy: copy.start(), lambda copy: copy.wait()
    fetch_p(0, 0, start)
    fetch_w = pltpu.make_async_copy(weights.at[3], wfull, wsem)

    n_q = n_dp // 2
    me_q, me_c = me_dp // 2, lax.rem(me_dp, 2)
    other = me_dp + 1 - 2 * me_c
    kinds = ((gw, pair, cland, xland, zsum, zland), (gwo, opair, ocland, oxland, ozsum, ozland))

    def rank_of(o):
        return lax.rem(me + 1 + o, n_mp)

    def load_copy(o, t):
        src, own_part = kinds[t][:2]
        return pltpu.make_async_copy(
            src.at[rank_of(o), :, :, me_c], own_part.at[o], ls_sem.at[o, t]
        )

    def pair_up(o, t):
        src, land = kinds[t][0], kinds[t][2]
        return pltpu.make_async_remote_copy(
            src_ref=src.at[rank_of(o), :, :, 1 - me_c], dst_ref=land.at[o],
            send_sem=cs_sem.at[o, t], recv_sem=cr_sem.at[o, t],
            device_id=(other, me), device_id_type=MESH,
        )

    def cross(o, j, t):
        src, land = kinds[t][1], kinds[t][3]
        to = lax.rem(me_q + j, n_q)
        return pltpu.make_async_remote_copy(
            src_ref=src.at[o, :, to], dst_ref=land.at[o, j - 1],
            send_sem=xs_sem.at[o, j, t], recv_sem=xr_sem.at[o, j, t],
            device_id=(to * 2 + me_c, me), device_id_type=MESH,
        )

    def along(o, t):
        src, land = kinds[t][4:]
        return pltpu.make_async_remote_copy(
            src_ref=src.at[o], dst_ref=land.at[o],
            send_sem=zs_sem.at[o, t], recv_sem=zr_sem.at[o, t],
            device_id=(me_dp, rank_of(o)), device_id_type=MESH,
        )

    def add_pair(o):
        for t in range(2):
            own_part, land = kinds[t][1], kinds[t][2]
            load_copy(o, t).wait()
            pair_up(o, t).wait_recv()
            mats = own_part.shape[1]

            def add(i, _):
                a = own_part[o, i // n_q, lax.rem(i, n_q)].astype(F32)
                b = land[o, i // n_q, lax.rem(i, n_q)].astype(F32)
                own_part[o, i // n_q, lax.rem(i, n_q)] = (a + b).astype(BF)
                return 0

            lax.fori_loop(0, mats * n_q, add, 0)
            for j in range(1, n_q):
                cross(o, j, t).start()

    def add_cross(o):
        for t in range(2):
            own_part, land, total = kinds[t][1], kinds[t][3], kinds[t][4]
            for j in range(1, n_q):
                cross(o, j, t).wait_recv()
            for m in range(own_part.shape[1]):
                a = own_part[o, m, me_q].astype(F32)
                for j in range(1, n_q):
                    a += land[o, j - 1, m].astype(F32)
                total[o, m] = a.astype(BF)
            if o < n_mp - 1:
                along(o, t).start()

    for o in range(n_mp):
        for t in range(2):
            load_copy(o, t).start()

    greet(n_dp, n_mp, me_dp, me)

    def grad_copy(h, j):
        hs = pl.ds(h * HEAD, HEAD)
        to = lax.rem(me + j, n_mp)
        return across_mp(
            j, gt.at[to, hs, :], gl.at[j, hs, :], gs_sem.at[h, j], gr_sem.at[h, j]
        )

    for h in range(heads):
        for j in range(1, n_mp):
            grad_copy(h, j).start()
    for o in range(n_mp):
        for t in range(2):
            pair_up(o, t).start()
    fetch_w.start()
    gl[0] = gt[me]

    def query_copy(h, j):
        to = lax.rem(me - j + n_mp, n_mp)
        hs = pl.ds(h * HEAD, HEAD)
        return pltpu.make_async_remote_copy(
            src_ref=dbuf.at[to, 0, hs, :], dst_ref=dland.at[j, 0, hs, :],
            send_sem=qs_sem.at[h, j], recv_sem=qr_sem.at[h, j],
            device_id=(me_dp, to), device_id_type=MESH,
        )

    def pair_copy(h, j):
        to = lax.rem(me - j + n_mp, n_mp)
        hs = pl.ds(h * HEAD, HEAD)
        return pltpu.make_async_remote_copy(
            src_ref=dbuf.at[to, pl.ds(1, 2), hs, :], dst_ref=dland.at[j, pl.ds(1, 2), hs, :],
            send_sem=ds_sem.at[h, j], recv_sem=dr_sem.at[h, j],
            device_id=(me_dp, to), device_id_type=MESH,
        )

    def block(h, j, c, place, rows, pb, keys, add):
        row = c * own + place
        at = pl.ds(pl.multiple_of(row, 128), rows)
        hs = slice(h * HEAD, (h + 1) * HEAD)
        uu = ut[h, :, at]
        inv = 1.0 / uu[HEAD : HEAD + 1]
        gg = gl[j, hs, pl.ds(place, rows)].astype(F32) * inv
        total = jnp.sum(gg * uu[:HEAD], axis=0, keepdims=True) * inv
        high = total.astype(BF).astype(F32)
        low = total - high
        index = lax.broadcasted_iota(jnp.int32, (HEAD, rows), 0)
        extra = jnp.where(index == 0, high, jnp.where(index == 1, low, 0.0))
        gext = jnp.concatenate([gg, extra], axis=0).T.astype(BF)
        dp = dot(gext, vte[h, :, keys])
        ds = (pb.astype(F32) * dp).astype(BF)
        dq = dot(ds, kp[h, keys, :]).T[:HEAD] * (HEAD**-0.5)
        dbuf[c, 0, hs, pl.ds(place, rows)] = dq.astype(BF)
        dk = dot(qt[hs, at], ds)
        dv = dot(gg.astype(BF), pb)
        if add:
            dkt[:, keys] = dkt[:, keys] + dk
            dvt[:, keys] = dvt[:, keys] + dv
        else:
            dkt[:, keys] = dk
            dvt[:, keys] = dv

    pump = [o for o in range(n_mp)]
    for h in range(heads):
        hs = slice(h * HEAD, (h + 1) * HEAD)
        dkt[:, :LONGEST] = jnp.zeros((HEAD, LONGEST), F32)
        dvt[:, :LONGEST] = jnp.zeros((HEAD, LONGEST), F32)

        def chunk(j, _):
            c = lax.rem(me - j + n_mp, n_mp)
            slot = lax.rem(h * n_mp + j, 2)

            @pl.when(j < n_mp - 1)
            def _():
                fetch_p(h, j + 1, start)

            if h < heads - 1:

                @pl.when(j == n_mp - 1)
                def _():
                    fetch_p(h + 1, 0, start)

            @pl.when(j > 0)
            def _():
                grad_copy(h, j).wait_recv()

            fetch_p(h, j, wait)

            keys = slice(0, LONGEST)

            @pl.when(c < full)
            def _():
                for half in range(own // QB):
                    at = pl.ds(half * QB, QB)
                    block(h, j, c, half * QB, QB, pbuf[slot, at, :], keys, True)

            @pl.when(c == full)
            def _():
                block(h, j, c, 0, rest, pbuf[slot, :rest, :], keys, True)
                block(h, j, c, rest, tail, p2[h], slice(LONGEST, group), False)

            @pl.when(j > 0)
            def _():
                query_copy(h, j).start()

            for o in range(n_mp):
                if pump[o] // n_mp == h:

                    @pl.when(j == pump[o] % n_mp)
                    def _():
                        add_pair(o)

            return 0

        lax.fori_loop(0, n_mp, chunk, 0)
        if h == heads - 1:
            add_cross(0)
        for c in range(n_mp):
            dbuf[c, 1, hs, :] = dkt[:, c * own : (c + 1) * own].astype(BF)
            dbuf[c, 2, hs, :] = dvt[:, c * own : (c + 1) * own].astype(BF)
        for j in range(1, n_mp):
            pair_copy(h, j).start()

    ones = jnp.ones((8, own), BF)
    sq = jnp.zeros((8, cols), F32)
    sv = jnp.zeros((8, cols), F32)
    for c in range(n_mp):
        sq += dot_nt(ones, dbuf[c, 0])
        sv += dot_nt(ones, dbuf[c, 2])
    ssum[...] = sin[...]
    for r in range(n_mp):

        @pl.when(me == r)
        def _():
            ssum[0:1, r * cols : (r + 1) * cols] = sq[0:1]
            ssum[1:2, r * cols : (r + 1) * cols] = sv[0:1]

    send1 = [across_mp(j, ssum, slot1.at[j], s1s.at[j], s1r.at[j]) for j in range(1, n_mp)]
    for c in send1:
        c.start()

    total = jnp.zeros((xt.shape[0], 3 * cols), F32)
    for c in range(n_mp):
        total += dot_nt(xt[:, c * own : (c + 1) * own], dbuf[c].reshape(3 * cols, own))
    for d in range(n_dp):
        gbuf[d] = total[d * wrows : (d + 1) * wrows].astype(BF)

    def weight_copy(j):
        to = lax.rem(me_dp + j, n_dp)
        return across_dp(j, gbuf.at[to], qland.at[j], ws_sem.at[j], wr_sem.at[j])

    for j in range(1, n_dp):
        weight_copy(j).start()

    add_cross(1)
    for c in send1:
        c.wait_send()
        c.wait_recv()
    total = ssum[...]
    for j in range(1, n_mp):
        total += slot1[j]
    ssum[...] = total
    send2 = [across_dp(j, ssum, slot2.at[j], s2s.at[j], s2r.at[j]) for j in range(1, n_dp)]
    for c in send2:
        c.start()

    fetch_w.wait()
    into = dot(wfull[me, :, : 3 * cols], dbuf[me].reshape(3 * cols, own))
    for j in range(1, n_mp):
        for h in range(heads):
            query_copy(h, j).wait_recv()
            pair_copy(h, j).wait_recv()
        r = lax.rem(me + j, n_mp)
        into += dot(wfull[r, :, : 3 * cols], dland[j].reshape(3 * cols, own))
    grad_in[...] = (dsum1[...] + into.T).astype(BF)

    for o in range(2, n_mp):
        add_cross(o)
    total = gbuf[me_dp].astype(F32)
    for j in range(1, n_dp):
        weight_copy(j).wait_recv()
        total += qland[j].astype(F32)
    for s in range(3):
        gq[s] = total[:, s * cols : (s + 1) * cols]
    total = ssum[...]
    for c in send2:
        c.wait_recv()
    for j in range(1, n_dp):
        total += slot2[j]
    small[...] = total
    for t in range(2):
        total, land = kinds[t][4:]
        for o in range(n_mp - 1):
            along(o, t).wait_recv()
        for m in range(total.shape[1]):
            a = total[n_mp - 1, m].astype(F32)
            for o in range(n_mp - 1):
                a += land[o, m].astype(F32)
            if t == 1:
                gout[...] = a.T
            elif m == 2:
                gdown[...] = a
            else:
                ggu[m] = a
    for t in range(2):
        for o in range(n_mp):
            pair_up(o, t).wait_send()
            for j in range(1, n_q):
                cross(o, j, t).wait_send()
            if o < n_mp - 1:
                along(o, t).wait_send()
    for c in send2:
        c.wait_send()
    for j in range(1, n_dp):
        weight_copy(j).wait_send()
    for h in range(heads):
        for j in range(1, n_mp):
            grad_copy(h, j).wait_send()
            query_copy(h, j).wait_send()
            pair_copy(h, j).wait_send()


def norm_parts(r):
    centre = r - jnp.mean(r, axis=-1, keepdims=True)
    spread = jnp.mean(centre * centre, axis=-1, keepdims=True)
    rstd = lax.rsqrt(spread + 1e-05)
    return centre * rstd, rstd


def norm_back(dn, n, rstd):
    return rstd * (
        dn - jnp.mean(dn, axis=-1, keepdims=True) - n * jnp.mean(dn * n, axis=-1, keepdims=True)
    )


def colsum(a):
    return jnp.sum(a, axis=0, keepdims=True)


def flip(a):
    return a.astype(F32).T.astype(BF)


GELU_C = 0.7978845608
GELU_A = 0.044715


def middle(
    attn, x, cot, wlast, small, w,
    result, dsum1, dattn, gw, gwout, gsmall,
    wout, mid, midb, midt, gate, up, y, dffn, dffnt, dmid,
):
    i = pl.program_id(0)
    n = pl.num_programs(0) // 2
    parts, cols = attn.shape[0], attn.shape[1]

    @pl.when(i == 0)
    def _():
        branch = jnp.zeros((x.shape[1], x.shape[0]), F32)
        for r in range(parts):
            wout[r] = wlast[0, r, :, 3 * cols :]
            branch += dot(wout[r], attn[r])
        branch = branch.T + x[...].astype(F32) + small[2:3, :]
        nn, _ = norm_parts(branch)
        m = nn * small[3:4, :] + small[4:5, :]
        dsum1[...] = branch
        mid[...] = m
        midb[...] = m.astype(BF)
        midt[...] = m.T.astype(BF)
        y[...] = jnp.zeros_like(y)

    @pl.when(i < n)
    def _():
        mb = midb[...]
        ga = dot(mb, w[0, 0]) + small[pl.ds(8 + i, 1), :]
        u = dot(mb, w[1, 0]) + small[pl.ds(8 + n + i, 1), :]
        gate[i] = ga
        up[i] = u
        t = jnp.tanh(GELU_C * (ga + GELU_A * ga * ga * ga))
        act = (0.5 * ga * (1.0 + t) * u).astype(BF)
        y[...] += dot_nt(act, w[2, 0])

    @pl.when(i == n - 1)
    def _():
        r = mid[...] + y[...] + small[5:6, :]
        nn, rstd = norm_parts(r)
        gain = small[6:7, :]
        result[...] = (nn * gain + small[7:8, :]).astype(BF)
        c = cot[...].astype(F32)
        ds = norm_back(c * gain, nn, rstd)
        gsmall[6:7, :] = colsum(c * nn)
        gsmall[7:8, :] = colsum(c)
        dmid[...] = ds
        db = ds.astype(BF)
        dffn[...] = db
        dffnt[...] = ds.T.astype(BF)
        gsmall[5:6, :] = colsum(db.astype(F32))
        gsmall[0:2, :] = jnp.zeros_like(gsmall[0:2, :])

    @pl.when(i >= n)
    def _():
        k = 2 * n - 1 - i
        ga = gate[k]
        u = up[k]
        sq = ga * ga
        t = jnp.tanh(GELU_C * (ga + GELU_A * ga * sq))
        half = 0.5 * (1.0 + t)
        gelu = ga * half
        slope = half + (0.5 * GELU_C) * ga * (1.0 - t * t) * (1.0 + 3.0 * GELU_A * sq)
        act = (gelu * u).astype(BF)
        dact = dot(dffn[...], w[2, 0])
        gw[0, 2] = dot(dffnt[...], act).astype(BF)
        dga = (dact * u * slope).astype(BF)
        du = (dact * gelu).astype(BF)
        gsmall[pl.ds(8 + k, 1), :] = colsum(dga.astype(F32))
        gsmall[pl.ds(8 + n + k, 1), :] = colsum(du.astype(F32))
        gw[0, 0] = dot(midt[...], dga).astype(BF)
        gw[0, 1] = dot(midt[...], du).astype(BF)
        dmid[...] += dot_nt(dga, w[0, 0]) + dot_nt(du, w[1, 0])

    @pl.when(i == 2 * n - 1)
    def _():
        nn, rstd = norm_parts(dsum1[...])
        dm = dmid[...]
        gsmall[3:4, :] = colsum(dm * nn)
        gsmall[4:5, :] = colsum(dm)
        ds = norm_back(dm * small[3:4, :], nn, rstd)
        dsum1[...] = ds
        db = ds.astype(BF)
        gsmall[2:3, :] = colsum(db.astype(F32))
        dbt = ds.T.astype(BF)
        for r in range(parts):
            dattn[r] = dot(db, wout[r]).T.astype(BF)
            gwout[r] = dot_nt(dbt, attn[r]).astype(BF)


def hand_on(*refs):
    n = len(refs) // 2
    for a, b in zip(refs[:n], refs[n:]):
        b[...] = a[...]


def head_slopes(first_head, head_count):
    number = first_head + jnp.arange(head_count, dtype=jnp.int32)
    exponent = jnp.where(number < 8, number.astype(F32) + 1.0, number.astype(F32) - 7.5)
    return jnp.exp2(-exponent)


def cost(flops):
    return pl.CostEstimate(flops=flops, bytes_accessed=1 << 24, transcendentals=0)


def params(**kw):
    return pltpu.CompilerParams(vmem_limit_bytes=VMEM_LIMIT, **kw)


def per_device(
    hidden_in, lengths, w_qkv, b_qv, w_out, b_out, ln1_gain, ln1_bias, w_gu, b_gu, w_down,
    b_down, ln2_gain, ln2_bias, cotangent,
):
    both = ("dp", "mp")
    n_dp, n_mp = lax.axis_size("dp"), lax.axis_size("mp")
    n = n_dp * n_mp
    mp_rank = lax.axis_index("mp")
    own, width = hidden_in.shape
    group = own * n_mp
    sds = jax.ShapeDtypeStruct

    dev = lax.axis_index("dp") * n_mp + mp_rank

    def placed(a):
        zero = jnp.zeros((a.shape[0], a.shape[1] * n), F32)
        return lax.dynamic_update_slice_in_dim(zero, a, dev * a.shape[1], 1)

    vectors = jnp.stack([b_out, ln1_gain, ln1_bias, b_down, ln2_gain, ln2_bias])
    vectors = jnp.concatenate([b_qv, vectors], axis=0)
    small_own = jnp.concatenate(
        [placed(vectors), placed(b_gu).reshape(-1, width)], axis=0
    )
    srows = small_own.shape[0]

    wrows, cols = w_qkv.shape[1], w_qkv.shape[2]
    ff_part = w_gu.shape[2]
    heads = cols // HEAD
    tail = group - LONGEST

    n_q = n_dp // 2
    units = 2 * n_mp - 1

    slopes = head_slopes(mp_rank * heads, heads)
    dma = pltpu.SemaphoreType.DMA

    small, xt, qt, kp, vte, ut, attn, p, p2, weights = pl.pallas_call(
        functools.partial(front, n_dp, n_mp),
        out_shape=(
            sds((srows, width), F32),
            sds((width, group), BF),
            sds((cols, group), BF),
            sds((heads, group, 2 * HEAD), BF),
            sds((heads, 2 * HEAD, group), BF),
            sds((heads, 2 * HEAD, group), F32),
            sds((n_mp, cols, own), BF),
            sds((heads, LONGEST, LONGEST), BF),
            sds((heads, tail, tail), BF),
            sds((4, n_mp, n_q, 2, wrows, ff_part), BF),
        ),
        in_specs=[vmem(), vmem(), vmem(), vmem(), vmem(), vmem(), smem(), smem()],
        out_specs=(
            vmem(), hbm(), hbm(), hbm(), hbm(), hbm(), vmem(), hbm(), hbm(), hbm(),
        ),
        scratch_shapes=[
            pltpu.VMEM((4, wrows, ff_part), BF),
            pltpu.VMEM((width, group), BF),
            pltpu.VMEM((cols, group), BF),
            pltpu.VMEM((heads, group, 2 * HEAD), BF),
            pltpu.VMEM((heads, 2 * HEAD, group), BF),
            pltpu.VMEM((heads, 2 * HEAD, group), F32),
            pltpu.VMEM((heads, tail, tail), BF),
            pltpu.VMEM((n_mp, own, width), BF),
            pltpu.VMEM((n_q, 2, wrows, ff_part), BF),
            pltpu.VMEM((3, width, cols), F32),
            pltpu.VMEM((3, width, cols), BF),
            pltpu.VMEM((n_mp, srows, width), F32),
            pltpu.VMEM((srows, width), F32),
            pltpu.VMEM((n_dp, srows, width), F32),
            pltpu.VMEM((8, cols), F32),
            pltpu.VMEM((group, cols), BF),
            pltpu.VMEM((cols, group), BF),
            pltpu.VMEM((heads, group, 2 * HEAD), BF),
            pltpu.VMEM((QB, LONGEST + LONGEST // QB * QB), F32),
            pltpu.VMEM((heads, LONGEST, LONGEST), BF),
            pltpu.VMEM((n_mp, cols, own), BF),
            pltpu.VMEM((n_mp, cols, own), BF),
            dma((2, n_mp - 1, PIECES)),
            dma((2, n_mp - 1, PIECES)),
            dma((n_mp,)),
            dma((n_mp,)),
            dma((n_dp,)),
            dma((n_dp,)),
            dma((heads, n_mp)),
            dma((heads, n_mp)),
            dma((heads, n_mp)),
            dma((2,)),
            dma((4,)),
            dma((2, heads)),
            dma((2, n_mp - 1, 4)),
            dma((2, n_mp - 1, 4)),
            dma((units, 4, n_q)),
            dma((units, 4, n_q)),
            dma((units, 2, n_q)),
            dma((units, 2, n_q)),
        ],
        compiler_params=params(collective_id=0, has_side_effects=True),
        cost_estimate=cost(11 * LONGEST * LONGEST * HEAD * heads * 12),
        name="front",
    )(hidden_in, w_qkv, w_out, w_gu, w_down.T, small_own, slopes, lengths)
    weights = weights.reshape(4, n_mp, width, ff_part)

    fixed = lambda *s: pl.BlockSpec(s, lambda i: (0,) * len(s))
    walk = lambda i: jnp.where(i < n_mp, i, 2 * n_mp - 1 - i)
    late = lambda i: jnp.where(i < n_mp, n_mp - 1, 2 * n_mp - 1 - i)
    result, dsum1, dattn, gw, gwout, gsmall = pl.pallas_call(
        middle,
        grid=(2 * n_mp,),
        out_shape=(
            sds((own, width), BF),
            sds((own, width), F32),
            sds((n_mp, cols, own), BF),
            sds((n_mp, 3, width, ff_part), BF),
            sds((n_mp, width, cols), BF),
            sds((srows, width), F32),
        ),
        in_specs=[
            fixed(n_mp, cols, own),
            fixed(own, width),
            fixed(own, width),
            pl.BlockSpec(
                (1, n_mp, width, ff_part),
                lambda i: (3, 0, 0, 0),
                pipeline_mode=pl.Buffered(1),
            ),
            fixed(srows, width),
            pl.BlockSpec((3, 1, width, ff_part), lambda i: (0, walk(i), 0, 0)),
        ],
        out_specs=(
            fixed(own, width),
            fixed(own, width),
            fixed(n_mp, cols, own),
            pl.BlockSpec((1, 3, width, ff_part), lambda i: (late(i), 0, 0, 0)),
            fixed(n_mp, width, cols),
            fixed(srows, width),
        ),
        scratch_shapes=[
            pltpu.VMEM((n_mp, width, cols), BF),
            pltpu.VMEM((own, width), F32),
            pltpu.VMEM((own, width), BF),
            pltpu.VMEM((width, own), BF),
            pltpu.VMEM((n_mp, own, ff_part), F32),
            pltpu.VMEM((n_mp, own, ff_part), F32),
            pltpu.VMEM((own, width), F32),
            pltpu.VMEM((own, width), BF),
            pltpu.VMEM((width, own), BF),
            pltpu.VMEM((own, width), F32),
        ],
        compiler_params=params(),
        name="middle",
    )(attn, hidden_in, cotangent, weights, small, weights)

    gw = gw.reshape(n_mp, 3, n_q, 2, wrows, ff_part)
    gwout = gwout.reshape(n_mp, 1, n_q, 2, wrows, cols)
    grad_in, gqkv, gsmall, ggu, gdown, gout = pl.pallas_call(
        functools.partial(back, n_dp, n_mp),
        out_shape=(
            sds((own, width), BF),
            sds((3, wrows, cols), F32),
            sds((srows, width), F32),
            sds((2, wrows, ff_part), F32),
            sds((wrows, ff_part), F32),
            sds((cols, wrows), F32),
        ),
        in_specs=[
            vmem(), vmem(), vmem(), vmem(), vmem(), vmem(), hbm(), vmem(), hbm(), vmem(), vmem(),
            hbm(), hbm(),
        ],
        out_specs=(vmem(), vmem(), vmem(), vmem(), vmem(), vmem()),
        scratch_shapes=[
            pltpu.VMEM((n_mp, cols, own), BF),
            pltpu.VMEM((2, own, LONGEST), BF),
            pltpu.VMEM((HEAD, group), F32),
            pltpu.VMEM((HEAD, group), F32),
            pltpu.VMEM((n_mp, 3, cols, own), BF),
            pltpu.VMEM((n_mp, 3, cols, own), BF),
            pltpu.VMEM((n_mp, width, ff_part), BF),
            pltpu.VMEM((n_dp, wrows, 3 * cols), BF),
            pltpu.VMEM((n_dp, wrows, 3 * cols), BF),
            pltpu.VMEM((srows, width), F32),
            pltpu.VMEM((n_mp, srows, width), F32),
            pltpu.VMEM((n_dp, srows, width), F32),
            pltpu.VMEM((n_mp, 3, n_q, wrows, ff_part), BF),
            pltpu.VMEM((n_mp, 3, n_q, wrows, ff_part), BF),
            pltpu.VMEM((n_mp, n_q - 1, 3, wrows, ff_part), BF),
            pltpu.VMEM((n_mp, 3, wrows, ff_part), BF),
            pltpu.VMEM((n_mp - 1, 3, wrows, ff_part), BF),
            pltpu.VMEM((n_mp, 1, n_q, wrows, cols), BF),
            pltpu.VMEM((n_mp, 1, n_q, wrows, cols), BF),
            pltpu.VMEM((n_mp, n_q - 1, 1, wrows, cols), BF),
            pltpu.VMEM((n_mp, 1, wrows, cols), BF),
            pltpu.VMEM((n_mp - 1, 1, wrows, cols), BF),
            dma((heads, n_mp)),
            dma((heads, n_mp)),
            dma((heads, n_mp)),
            dma((heads, n_mp)),
            dma((heads, n_mp)),
            dma((heads, n_mp)),
            dma((n_dp,)),
            dma((n_dp,)),
            dma((n_mp,)),
            dma((n_mp,)),
            dma((n_dp,)),
            dma((n_dp,)),
            dma((2,)),
            dma,
            dma((n_mp, 2)),
            dma((n_mp, 2)),
            dma((n_mp, 2)),
            dma((n_mp, n_q, 2)),
            dma((n_mp, n_q, 2)),
            dma((n_mp - 1, 2)),
            dma((n_mp - 1, 2)),
        ],
        compiler_params=params(collective_id=1, has_side_effects=True),
        cost_estimate=cost(11 * LONGEST * LONGEST * HEAD * heads * 12),
        name="back",
    )(dattn, xt, qt, kp, vte, ut, p, p2, weights, dsum1, gsmall, gw, gwout)

    finished = (grad_in, gqkv, ggu, gdown, gout)
    grad_in, gqkv, ggu, gdown, gout = pl.pallas_call(
        hand_on,
        out_shape=tuple(sds(a.shape, a.dtype) for a in finished),
        in_specs=[vmem()] * len(finished),
        out_specs=(vmem(),) * len(finished),
        compiler_params=params(),
        name="hand_on",
    )(*finished)

    def own_columns(a):
        part = a.shape[1] // n
        return lax.dynamic_slice_in_dim(a, dev * part, part, 1)

    gs = own_columns(gsmall[:8])
    g_gu = own_columns(gsmall[8:].reshape(2, -1))

    return (
        result,
        grad_in,
        gqkv,
        gs[0:2],
        gout,
        gs[2],
        gs[3],
        gs[4],
        ggu,
        g_gu,
        gdown.T,
        gs[5],
        gs[6],
        gs[7],
    )


def solution(mesh):
    rows = P(("dp", "mp"), None)
    vec = P(("dp", "mp"))
    vecs = P(None, ("dp", "mp"))
    wide = P(None, "dp", "mp")
    tall = P("mp", "dp")
    return jax.shard_map(
        per_device,
        mesh=mesh,
        in_specs=(
            rows, P("dp", None), wide, vecs, tall, vec, vec, vec, wide, vecs, tall, vec, vec, vec,
            rows,
        ),
        out_specs=(
            rows, rows, wide, vecs, tall, vec, vec, vec, wide, vecs, tall, vec, vec, vec,
        ),
        check_vma=False,
    )
```
